768 devices in a mesh: lon: 96 (over z_lo, y, core), lat: 8 (over z_hi, x).
Axes of the slice: x: 4, y: 8, z: 12 (z_hi: 2, z_lo: 6; z = z_hi * 6 + z_lo), core: 2. Of those that a mesh axis runs over, the one named last changes fastest.
Arguments:
- state: float32 [16, 512, 12288], P(None, 'lat', 'lon'), may hold values from -6 to 6
- land_mask: int32 [512, 12288], P('lat', 'lon'), may hold values from 0 to 1, as said below
- kernel_one: bfloat16 [3, 3, 16, 16], replicated, may hold values from -0.5 to 0.5
- bias_one: float32 [16], replicated, may hold values from -3 to 3
- kernel_two: bfloat16 [3, 3, 16, 16], replicated, may hold values from -0.5 to 0.5
- bias_two: float32 [16], replicated, may hold values from -3 to 3
- kernel_three: bfloat16 [3, 3, 8, 16], replicated, may hold values from -0.5 to 0.5
- bias_three: float32 [8], replicated, may hold values from -3 to 3
Outputs:
- updated: float32 [16, 512, 12288], P(None, 'lat', 'lon')
The draws below stay inside these ranges and needn't reach their ends.
Inputs may be any that keep to these rules, and one draw needn't show every extreme that they name: `land_mask`: 1 marks an ocean cell and 0 land; whole tiles of 64 x 128 cells may be land.
All inputs are finite; a program needn't handle non-finite values.
Results may differ from the reference program's by a relative error of at most 0.0003.
Values sent between devices are 32-bit elements; how exact they have to be, the bound alone decides.
A program may use at most 128 MiB of HBM per device.

```python
import jax
import jax.numpy as jnp

CLAT = 64
CLON = 128
LEV = 4
HID = 16
STATE = 16
FORCE = 8
NLAT = 512
NLON = 12288


def draw_land_mask(key, part):
    key = jax.random.fold_in(key, 7)
    first, second = jax.random.split(key)
    tiles = jax.random.randint(first, (NLAT // CLAT, NLON // CLON), 0, 4)
    cells = jax.random.randint(second, (NLAT, NLON), 0, 5)
    tile_ocean = (tiles > 0).astype(jnp.int32)
    spread = jnp.repeat(jnp.repeat(tile_ocean, CLAT, axis=0), CLON, axis=1)
    return (cells > 0).astype(jnp.int32) * spread


def level_of(rng, dims, shards, low, largest):
    level = 1.0
    for axis_at, blocks in shards:
        draws = jax.random.uniform(jax.random.fold_in(jax.random.fold_in(rng, 6), axis_at), (blocks,), jnp.float32, low / len(shards), largest / len(shards))
        level = level * jnp.repeat(jnp.exp(draws), dims[axis_at] // blocks).reshape((-1,) + (1,) * (len(dims) - 1 - axis_at))
    return level


def noise(rng, dims, scale, reach, cuts=(), held_as=jnp.bfloat16):
    result = jax.random.normal(rng, dims, jnp.float32) * scale
    if len(cuts) > 0:
        result = level_of(rng, dims, cuts, -0.22, 0.18) * result
    return jnp.clip(result, min=-reach, max=reach).astype(held_as)


def setup_inputs(seed: int = 0) -> dict:
    streams_of = jax.random.split(jax.random.key(seed), 9)
    return {
        "state": noise(streams_of[0], (STATE, NLAT, NLON), 1.0, 6.0, ((1, 8), (2, 96)), jnp.float32),
        "land_mask": draw_land_mask(jax.random.fold_in(streams_of[8], 71), 0),
        "kernel_one": noise(streams_of[2], (3, 3, HID, STATE), (9 * STATE) ** -0.5, 0.5),
        "bias_one": noise(streams_of[3], (HID,), 0.5, 3.0, (), jnp.float32),
        "kernel_two": noise(streams_of[4], (3, 3, HID, HID), (9 * HID) ** -0.5, 0.5),
        "bias_two": noise(streams_of[5], (HID,), 0.5, 3.0, (), jnp.float32),
        "kernel_three": noise(streams_of[6], (3, 3, FORCE, HID), (9 * HID) ** -0.5, 0.5),
        "bias_three": noise(streams_of[7], (FORCE,), 0.5, 3.0, (), jnp.float32),
    }


def conv(x, kernel, bias):
    rows = x.shape[1] - 2
    cols = x.shape[2] - 2
    xf = x.astype(jnp.float32)
    kf = kernel.astype(jnp.float32)
    total = jnp.zeros((kernel.shape[2], rows, cols), jnp.float32) + bias[:, None, None]
    for a in range(3):
        for c in range(3):
            total = total + jnp.einsum("ok,khw->ohw", kf[a, c], xf[:, a:a + rows, c:c + cols])
    return total


def reference(state, land_mask, kernel_one, bias_one, kernel_two, bias_two, kernel_three, bias_three):
    channels = state.shape[0]
    lon_padded = jnp.concatenate([state[:, :, -3:], state, state[:, :, :3]], axis=2)
    sign = jnp.where(jnp.arange(channels) < 2 * LEV, -1.0, 1.0).astype(jnp.float32)
    fold = lon_padded[:, NLAT - 3:, :][:, ::-1, ::-1] * sign[:, None, None]
    south = jnp.zeros((channels, 3, NLON + 6), jnp.float32)
    padded = jnp.concatenate([south, lon_padded, fold], axis=1)
    layer_in = padded.astype(jnp.bfloat16)
    hidden_one = jax.nn.silu(conv(layer_in, kernel_one, bias_one)).astype(jnp.bfloat16)
    hidden_two = jax.nn.silu(conv(hidden_one, kernel_two, bias_two)).astype(jnp.bfloat16)
    forcing = conv(hidden_two, kernel_three, bias_three)
    centre = padded[:, 3:-3, 3:-3]
    east = padded[:, 3:-3, 4:-2]
    west = padded[:, 3:-3, 2:-4]
    north = padded[:, 4:-2, 3:-3]
    south_cells = padded[:, 2:-4, 3:-3]
    speed_u = jnp.tile(centre[0:LEV], (4, 1, 1))
    speed_v = jnp.tile(centre[LEV:2 * LEV], (4, 1, 1))
    tendency = -0.5 * (speed_u * (east - west) + speed_v * (north - south_cells))
    tendency = tendency + 0.2 * (east + west + north + south_cells - 4.0 * centre)
    extra = jnp.concatenate([forcing, jnp.zeros((channels - forcing.shape[0], NLAT, NLON), jnp.float32)], axis=0)
    tendency = tendency + extra
    ocean = land_mask.astype(jnp.float32)
    return state + 0.1 * ocean[None, :, :] * tendency
```

```python
import functools

import jax
import jax.numpy as jnp
from jax import lax
from jax.experimental import pallas as pl
from jax.experimental.pallas import tpu as pltpu
from jax.sharding import PartitionSpec as P

MESH = pl.DeviceIdType.MESH
F32, BF16 = jnp.float32, jnp.bfloat16
HW, HE, HS, HN, BS, BN, SW, SE, NW, NE = range(10)


def iota(shape, dim):
    return lax.broadcasted_iota(jnp.int32, shape, dim)


def silu(v):
    half = 0.5 * v
    return half + half * jnp.tanh(half)


def roll(x, shift, axis):
    return pltpu.roll(x, shift % x.shape[axis], axis)


def bands(taps, spread, band):
    outs = taps.shape[2]
    spreading = (iota((16, 128), 0) == iota((16, 128), 1) // 8).astype(BF16)
    flat = taps[...].reshape(9 * outs, 16)
    spread[0 : 9 * outs, :] = jnp.dot(flat, spreading, preferred_element_type=F32)
    ahead = iota((8, 128), 1) % 8 - iota((8, 128), 0)
    for c in range(3):
        for pair in range(8):
            parts = []
            for o in (2 * pair, 2 * pair + 1):
                if o >= outs:
                    parts.append(jnp.zeros((8, 384), F32))
                    continue
                tap = []
                for a in range(3):
                    at = (a * 3 + c) * outs + o
                    tap.append(jnp.broadcast_to(spread[at : at + 1, :], (8, 128)))
                before = jnp.where(ahead == 7, tap[0], 0.0)
                centre = jnp.where(
                    ahead == -1,
                    tap[0],
                    jnp.where(ahead == 0, tap[1], jnp.where(ahead == 1, tap[2], 0.0)),
                )
                after = jnp.where(ahead == -7, tap[2], 0.0)
                parts.append(jnp.concatenate([before, centre, after], axis=1))
            at = c * 128 + pair * 16
            band[at : at + 16, :] = jnp.concatenate(parts, axis=0).astype(BF16)


def across(y, outs):
    parts = []
    for at in range(0, y.shape[1], 128):
        z = y[:, at : at + 128]
        parts.append(
            roll(z[0:outs], 1, 1) + z[outs : 2 * outs] + roll(z[2 * outs : 3 * outs], -1, 1)
        )
    return parts


def down(y, groups):
    z = [y[:, 128 * c : 128 * c + 128].reshape(groups, 32, 128) for c in range(3)]
    return roll(z[0], 1, 1) + z[1] + roll(z[2], -1, 1)


def kernel(
    lon_count,
    lat_count,
    state,
    land_mask,
    kernel_one,
    bias_one,
    kernel_two,
    bias_two,
    kernel_three,
    bias_three,
    out,
    own,
    mask,
    taps_one,
    taps_two,
    taps_three,
    b_one,
    b_two,
    b_three,
    south,
    north,
    edges,
    west_cols,
    east_cols,
    south_edges,
    north_edges,
    corner_sw,
    corner_se,
    corner_nw,
    corner_ne,
    fold_rows,
    fold_edges,
    spread,
    band_one,
    band_two,
    band_three,
    bias_full,
    hidden_a,
    hidden_b,
    in_sems,
    send_sems,
    recv_sems,
):
    t, j = lax.axis_index("lon"), lax.axis_index("lat")
    top = lat_count - 1
    east, west = lax.rem(t + 1, lon_count), lax.rem(t + lon_count - 1, lon_count)
    mirror = lon_count - 1 - t
    mirror_up = lax.rem(mirror + 1, lon_count)
    mirror_down = lax.rem(mirror + lon_count - 1, lon_count)

    loads = [
        pltpu.make_async_copy(src, dst, in_sems.at[i])
        for i, (src, dst) in enumerate(
            [
                (state, own.at[:, 8:72, :]),
                (land_mask, mask),
                (kernel_one, taps_one),
                (kernel_two, taps_two),
                (kernel_three, taps_three),
                (bias_one, b_one),
                (bias_two, b_two),
                (bias_three, b_three),
            ]
        )
    ]
    for load in loads:
        load.start()

    south[...] = jnp.zeros_like(south)
    north[...] = jnp.zeros_like(north)
    south_edges[...] = jnp.zeros_like(south_edges)
    corner_sw[...] = jnp.zeros_like(corner_sw)
    corner_se[...] = jnp.zeros_like(corner_se)

    barrier = pltpu.get_barrier_semaphore()

    def greet(lon, lat):
        pl.semaphore_signal(barrier, inc=1, device_id={"lon": lon, "lat": lat}, device_id_type=MESH)

    greet(east, j)
    greet(west, j)

    @pl.when(j > 0)
    def _():
        greet(t, j - 1)
        greet(east, j - 1)
        greet(west, j - 1)

    @pl.when(j < top)
    def _():
        greet(t, j + 1)
        greet(east, j + 1)
        greet(west, j + 1)

    @pl.when(j == top)
    def _():
        greet(mirror, j)

        @pl.when(mirror_up != t)
        def _():
            greet(mirror_up, j)

        @pl.when(mirror_down != t)
        def _():
            greet(mirror_down, j)

    own[:, 0:8, :] = jnp.zeros((16, 8, 128), F32)
    own[:, 72:80, :] = jnp.zeros((16, 8, 128), F32)
    zeros = jnp.zeros((128, 128), BF16)
    for ref in (hidden_a, hidden_b):
        ref[0:128, :] = zeros
        ref[1152:1280, :] = zeros

    loads[0].wait()

    for g in range(8):
        turned = own[:, 8 * g + 8 : 8 * g + 16, :].reshape(128, 128).T
        edges[0:8, 128 * g : 128 * g + 128] = turned[120:128]
        edges[8:16, 128 * g : 128 * g + 128] = turned[0:8]

    @pl.when(j == top)
    def _():
        back = 127 - iota((8, 128), 1)
        up = 7 - iota((8, 128), 0)
        for ch in range(16):
            x = own[ch, 64:72, :]
            x = jnp.take_along_axis(x, back, axis=1)
            x = jnp.take_along_axis(x, up, axis=0)
            fold_rows[ch] = -x if ch < 8 else x
        lane = iota((8, 128), 1)
        rows_back = lane + 7 - 2 * (lane % 8)
        for at in (0, 8):
            x = edges[at : at + 8, 896:1024]
            x = jnp.take_along_axis(x, rows_back, axis=1)
            x = jnp.take_along_axis(x, up, axis=0)
            fold_edges[8 - at : 16 - at, :] = jnp.where(lane < 64, -x, x)

    partners = 2 + 3 * (j > 0).astype(jnp.int32)
    partners += jnp.where(
        j < top,
        3,
        1 + (mirror_up != t).astype(jnp.int32) + (mirror_down != t).astype(jnp.int32),
    )
    pl.semaphore_wait(barrier, partners)

    def copy(src, dst, slot, sender, lon, lat):
        return pltpu.make_async_remote_copy(
            src_ref=src,
            dst_ref=dst,
            send_sem=send_sems.at[sender],
            recv_sem=recv_sems.at[slot],
            device_id={"lon": lon, "lat": lat},
            device_id_type=MESH,
        )

    first, last = pl.ds(0, 128), pl.ds(896, 128)
    lon_copies = [
        copy(edges.at[0:8, :], west_cols, HW, 0, east, j),
        copy(edges.at[8:16, :], east_cols, HE, 1, west, j),
    ]
    south_copies = [
        copy(own.at[:, 8:11, :], north.at[:, 0:3, :], HN, 2, t, j - 1),
        copy(edges.at[:, first], north_edges, BN, 3, t, j - 1),
        copy(edges.at[0:8, first], corner_nw, NW, 4, east, j - 1),
        copy(edges.at[8:16, first], corner_ne, NE, 5, west, j - 1),
    ]
    north_copies = [
        copy(own.at[:, 69:72, :], south.at[:, 5:8, :], HS, 6, t, j + 1),
        copy(edges.at[:, last], south_edges, BS, 7, t, j + 1),
        copy(edges.at[0:8, last], corner_sw, SW, 8, east, j + 1),
        copy(edges.at[8:16, last], corner_se, SE, 9, west, j + 1),
    ]
    fold_copies = [
        copy(fold_rows.at[:, 0:3, :], north.at[:, 0:3, :], HN, 6, mirror, j),
        copy(fold_edges, north_edges, BN, 7, mirror, j),
    ]
    fold_up = copy(fold_edges.at[0:8, :], corner_nw, NW, 8, mirror_up, j)
    fold_down = copy(fold_edges.at[8:16, :], corner_ne, NE, 9, mirror_down, j)

    @pl.when(j == top)
    def _():
        for c in fold_copies:
            c.start()

        @pl.when(mirror_up != t)
        def _():
            fold_up.start()

        @pl.when(mirror_up == t)
        def _():
            corner_nw[...] = fold_edges[0:8, :]

        @pl.when(mirror_down != t)
        def _():
            fold_down.start()

        @pl.when(mirror_down == t)
        def _():
            corner_ne[...] = fold_edges[8:16, :]

    @pl.when(j < top)
    def _():
        for c in north_copies:
            c.start()

    @pl.when(j > 0)
    def _():
        for c in south_copies:
            c.start()

    for c in lon_copies:
        c.start()

    for load in loads[1:]:
        load.wait()
    bands(taps_one, spread, band_one)
    bands(taps_two, spread, band_two)
    bands(taps_three, spread, band_three)
    lane_out = iota((1, 128), 1) // 8
    bias_rows = []
    for i, (ref, outs) in enumerate(((b_one, 16), (b_two, 16), (b_three, 8))):
        row = jnp.zeros((1, 128), F32)
        for o in range(outs):
            bias_full[i, 8 * o : 8 * o + 8, :] = jnp.full((8, 128), ref[o], F32)
            row = jnp.where(lane_out == o, ref[o], row)
        bias_rows.append(row)

    for g in range(8):
        x = own[:, 8 * g + 8 : 8 * g + 16, :].reshape(128, 128)
        hidden_a[128 * g + 128 : 128 * g + 256, :] = x.astype(BF16)

    band_last = jnp.concatenate(
        [band_three[128 * c : 128 * c + 64, :] for c in range(3)], axis=0
    )

    def windows(ref, g):
        return jnp.concatenate(
            [ref[128 * g : 128 * g + 384, :], ref[128 * g + 128 : 128 * g + 512, :]], axis=1
        )

    for src, band, i, dst in (
        (hidden_a, band_one, 0, hidden_b),
        (hidden_b, band_two, 1, hidden_a),
    ):
        for g in range(0, 8, 2):
            y = jnp.dot(band[...], windows(src, g), preferred_element_type=F32)
            for h, v in enumerate(across(y, 128)):
                at = 128 * (g + h) + 128
                dst[at : at + 128, :] = silu(v + bias_full[i]).astype(BF16)

    lane = iota((8, 128), 1)
    row = iota((8, 128), 0)
    for g in range(0, 8, 2):
        y = jnp.dot(band_last, windows(hidden_a, g), preferred_element_type=F32)
        for h, v in enumerate(across(y, 64)):
            inner = (lane >= 3) & (lane < 125)
            if g + h == 0:
                inner = inner & (row >= 3)
            if g + h == 7:
                inner = inner & (row < 5)
            forcing = jnp.where(inner[None], (v + bias_full[2, 0:64, :]).reshape(8, 8, 128), 0.0)
            at = 8 * (g + h)
            x = own[:, at + 8 : at + 16, :]
            qn = own[:, at + 9 : at + 17, :]
            qs = own[:, at + 7 : at + 15, :]
            qe = jnp.where(lane[None] < 127, roll(x, -1, 2), 0.0)
            qw = jnp.where(lane[None] > 0, roll(x, 1, 2), 0.0)
            u = jnp.concatenate([x[0:4]] * 4, axis=0)
            w = jnp.concatenate([x[4:8]] * 4, axis=0)
            tendency = -0.5 * (u * (qe - qw) + w * (qn - qs))
            tendency = tendency + 0.2 * (qe + qw + qn + qs - 4.0 * x)
            tendency = jnp.concatenate([tendency[0:8] + forcing, tendency[8:16]], axis=0)
            ocean = 0.1 * mask[at : at + 8, :].astype(F32)
            out[:, at : at + 8, :] = x + ocean[None] * tendency

    @pl.when(j > 0)
    def _():
        for c in (north_copies[0], north_copies[1], north_copies[2], north_copies[3]):
            c.wait_recv()

    fold_copies[0].wait_recv()
    fold_copies[1].wait_recv()

    @pl.when((j < top) | (mirror_up != t))
    def _():
        fold_up.wait_recv()

    @pl.when((j < top) | (mirror_down != t))
    def _():
        fold_down.wait_recv()

    for c in lon_copies:
        c.wait_recv()

    strip = jnp.concatenate(
        [
            jnp.concatenate([south[...], own[:, 64:72, :]], axis=2).reshape(128, 256),
            jnp.concatenate([own[:, 8:16, :], north[...]], axis=2).reshape(128, 256),
        ],
        axis=0,
    ).astype(BF16)
    cols = [
        jnp.concatenate(
            [corner_sw[...], south_edges[8:16, :], south_edges[0:8, :], corner_se[...]], axis=0
        )
    ]
    for g in range(8):
        at = pl.ds(128 * g, 128)
        cols.append(
            jnp.concatenate(
                [west_cols[:, at], edges[8:16, at], edges[0:8, at], east_cols[:, at]], axis=0
            )
        )
    cols.append(
        jnp.concatenate(
            [corner_nw[...], north_edges[8:16, :], north_edges[0:8, :], corner_ne[...]], axis=0
        )
    )
    cols = [x.astype(BF16) for x in cols]

    def sides(cols, band, groups):
        none = jnp.zeros((32, 128), BF16)
        padded = [none] + cols + [none]
        lhs = jnp.concatenate(
            [jnp.concatenate(padded[g : g + 3], axis=1) for g in groups], axis=0
        )
        y = lax.dot_general(
            lhs, band[...], (((1,), (1,)), ((), ())), preferred_element_type=F32
        )
        return down(y, len(groups))

    for band, i in ((band_one, 0), (band_two, 1)):
        halves = []
        for at in (128, 0):
            y = jnp.dot(band[:, at : at + 256], strip, preferred_element_type=F32)
            bias = bias_full[i]
            halves.append(
                jnp.concatenate([silu(v + bias).astype(BF16) for v in across(y, 128)], axis=1)
            )
        strip = jnp.concatenate(halves, axis=0)
        y = silu(sides(cols, band, range(10)) + bias_rows[i][None]).astype(BF16)
        cols = [y[g] for g in range(10)]

    bias = bias_full[2, 0:64, :]
    y = jnp.dot(band_last[:, 0:256], strip[:, 0:128], preferred_element_type=F32)
    forcing_south = (across(y, 64)[0] + bias).reshape(8, 8, 128)
    y = jnp.dot(band_last[:, 128:384], strip[:, 128:256], preferred_element_type=F32)
    forcing_north = (across(y, 64)[0] + bias).reshape(8, 8, 128)
    forcing_sides = sides(cols, band_three, range(1, 9)) + bias_rows[2][None]

    place = iota((8, 128), 0)
    lane = iota((8, 128), 1)
    patches = []
    for g in range(8):
        at = pl.ds(128 * g, 128)

        def speed(x):
            x = jnp.where(lane < 32, x, 0.0)
            x = x + roll(x, 32, 1)
            return x + roll(x, 64, 1)

        e = edges[0:8, at]
        w = edges[8:16, at]
        east_term = jnp.where(place == 7, (0.2 - 0.5 * speed(e)) * roll(east_cols[:, at], -1, 0), 0.0)
        west_term = jnp.where(place == 0, (0.2 + 0.5 * speed(w)) * roll(west_cols[:, at], 1, 0), 0.0)
        patches.append(forcing_sides[g, 16:24] + east_term)
        patches.append(forcing_sides[g, 8:16] + west_term)
    turned = jnp.concatenate(patches, axis=0).T
    inner = (lane >= 3) & (lane < 125)
    for g in range(8):
        patch = roll(turned, 120 - 16 * g, 1).reshape(16, 8, 128)
        patch = jnp.where(inner[None], 0.0, patch)
        if g in (0, 7):
            x = own[:, 8 * g + 8 : 8 * g + 16, :]
            v = jnp.concatenate([x[4:8]] * 4, axis=0)
            if g == 0:
                near = jnp.where(place[None] == 0, (0.2 + 0.5 * v) * roll(south[...], 1, 1), 0.0)
                forcing = jnp.where((inner & (place < 3))[None], forcing_south, 0.0)
            else:
                near = jnp.where(place[None] == 7, (0.2 - 0.5 * v) * roll(north[...], -1, 1), 0.0)
                forcing = jnp.where((inner & (place >= 5))[None], forcing_north, 0.0)
            patch = patch + near
            patch = jnp.concatenate([patch[0:8] + forcing, patch[8:16]], axis=0)
        at = 8 * g
        ocean = 0.1 * mask[at : at + 8, :].astype(F32)
        out[:, at : at + 8, :] = out[:, at : at + 8, :] + ocean[None] * patch

    @pl.when(j == top)
    def _():
        for c in fold_copies:
            c.wait_send()

        @pl.when(mirror_up != t)
        def _():
            fold_up.wait_send()

        @pl.when(mirror_down != t)
        def _():
            fold_down.wait_send()

    @pl.when(j < top)
    def _():
        for c in north_copies:
            c.wait_send()

    @pl.when(j > 0)
    def _():
        for c in south_copies:
            c.wait_send()

    for c in lon_copies:
        c.wait_send()


def solution(mesh):
    lon_count, lat_count = mesh.shape["lon"], mesh.shape["lat"]

    def step(*args):
        state, *rest = [pltpu.with_memory_space_constraint(x, pltpu.HBM) for x in args]
        return pl.pallas_call(
            functools.partial(kernel, lon_count, lat_count),
            out_shape=jax.ShapeDtypeStruct(state.shape, F32),
            in_specs=[pl.BlockSpec(memory_space=pltpu.HBM)] * 8,
            out_specs=pl.BlockSpec(memory_space=pltpu.VMEM),
            scratch_shapes=[
                pltpu.VMEM((16, 80, 128), F32),
                pltpu.VMEM((64, 128), jnp.int32),
                pltpu.VMEM((3, 3, 16, 16), BF16),
                pltpu.VMEM((3, 3, 16, 16), BF16),
                pltpu.VMEM((3, 3, 8, 16), BF16),
                pltpu.SMEM((16,), F32),
                pltpu.SMEM((16,), F32),
                pltpu.SMEM((8,), F32),
                pltpu.VMEM((16, 8, 128), F32),
                pltpu.VMEM((16, 8, 128), F32),
                pltpu.VMEM((16, 1024), F32),
                pltpu.VMEM((8, 1024), F32),
                pltpu.VMEM((8, 1024), F32),
                pltpu.VMEM((16, 128), F32),
                pltpu.VMEM((16, 128), F32),
                pltpu.VMEM((8, 128), F32),
                pltpu.VMEM((8, 128), F32),
                pltpu.VMEM((8, 128), F32),
                pltpu.VMEM((8, 128), F32),
                pltpu.VMEM((16, 8, 128), F32),
                pltpu.VMEM((16, 128), F32),
                pltpu.VMEM((144, 128), F32),
                pltpu.VMEM((384, 384), BF16),
                pltpu.VMEM((384, 384), BF16),
                pltpu.VMEM((384, 384), BF16),
                pltpu.VMEM((3, 128, 128), F32),
                pltpu.VMEM((1280, 128), BF16),
                pltpu.VMEM((1280, 128), BF16),
                pltpu.SemaphoreType.DMA((8,)),
                pltpu.SemaphoreType.DMA((10,)),
                pltpu.SemaphoreType.DMA((10,)),
            ],
            compiler_params=pltpu.CompilerParams(
                collective_id=0, has_side_effects=True, vmem_limit_bytes=32 * 1024 * 1024
            ),
        )(state, *rest)

    return jax.shard_map(
        step,
        mesh=mesh,
        in_specs=(P(None, "lat", "lon"), P("lat", "lon"), P(), P(), P(), P(), P(), P()),
        out_specs=P(None, "lat", "lon"),
        check_vma=False,
    )
```

```python
import functools

import jax
import jax.numpy as jnp
from jax import lax
from jax.experimental import pallas as pl
from jax.experimental.pallas import tpu as pltpu
from jax.sharding import PartitionSpec as P

MESH = pl.DeviceIdType.MESH
F32, BF16 = jnp.float32, jnp.bfloat16
HW, HE, HS, HN, BS, BN, SW, SE, NW, NE = range(10)


def iota(shape, dim):
    return lax.broadcasted_iota(jnp.int32, shape, dim)


def silu(v):
    half = 0.5 * v
    return half + half * jnp.tanh(half)


def roll(x, shift, axis):
    return pltpu.roll(x, shift % x.shape[axis], axis)


def bands(taps, spread, band):
    outs = taps.shape[2]
    spreading = (iota((16, 128), 0) == iota((16, 128), 1) // 8).astype(BF16)
    flat = taps[...].reshape(9 * outs, 16)
    spread[0 : 9 * outs, :] = jnp.dot(flat, spreading, preferred_element_type=F32)
    ahead = iota((8, 128), 1) % 8 - iota((8, 128), 0)
    for c in range(3):
        for pair in range(8):
            parts = []
            for o in (2 * pair, 2 * pair + 1):
                if o >= outs:
                    parts.append(jnp.zeros((8, 384), F32))
                    continue
                tap = []
                for a in range(3):
                    at = (a * 3 + c) * outs + o
                    tap.append(jnp.broadcast_to(spread[at : at + 1, :], (8, 128)))
                before = jnp.where(ahead == 7, tap[0], 0.0)
                centre = jnp.where(
                    ahead == -1,
                    tap[0],
                    jnp.where(ahead == 0, tap[1], jnp.where(ahead == 1, tap[2], 0.0)),
                )
                after = jnp.where(ahead == -7, tap[2], 0.0)
                parts.append(jnp.concatenate([before, centre, after], axis=1))
            at = c * 128 + pair * 16
            band[at : at + 16, :] = jnp.concatenate(parts, axis=0).astype(BF16)


def across(y, outs):
    parts = []
    for at in range(0, y.shape[1], 128):
        z = y[:, at : at + 128]
        parts.append(
            roll(z[0:outs], 1, 1) + z[outs : 2 * outs] + roll(z[2 * outs : 3 * outs], -1, 1)
        )
    return parts


def down(y, groups):
    z = [y[:, 128 * c : 128 * c + 128].reshape(groups, 32, 128) for c in range(3)]
    return roll(z[0], 1, 1) + z[1] + roll(z[2], -1, 1)


def kernel(
    lon_count,
    lat_count,
    state,
    land_mask,
    kernel_one,
    bias_one,
    kernel_two,
    bias_two,
    kernel_three,
    bias_three,
    out,
    own,
    mask,
    taps_one,
    taps_two,
    taps_three,
    b_one,
    b_two,
    b_three,
    south,
    north,
    edges,
    west_cols,
    east_cols,
    south_edges,
    north_edges,
    corner_sw,
    corner_se,
    corner_nw,
    corner_ne,
    fold_rows,
    fold_edges,
    spread,
    band_one,
    band_two,
    band_three,
    bias_full,
    hidden_a,
    hidden_b,
    in_sems,
    send_sems,
    recv_sems,
    answers,
):
    t, j = lax.axis_index("lon"), lax.axis_index("lat")
    top = lat_count - 1
    east, west = lax.rem(t + 1, lon_count), lax.rem(t + lon_count - 1, lon_count)
    mirror = lon_count - 1 - t
    mirror_up = lax.rem(mirror + 1, lon_count)
    mirror_down = lax.rem(mirror + lon_count - 1, lon_count)

    loads = [
        pltpu.make_async_copy(src, dst, in_sems.at[i])
        for i, (src, dst) in enumerate(
            [
                (state, own.at[:, 8:72, :]),
                (land_mask, mask),
                (kernel_one, taps_one),
                (kernel_two, taps_two),
                (kernel_three, taps_three),
                (bias_one, b_one),
                (bias_two, b_two),
                (bias_three, b_three),
            ]
        )
    ]
    for load in loads:
        load.start()

    south[...] = jnp.zeros_like(south)
    north[...] = jnp.zeros_like(north)
    south_edges[...] = jnp.zeros_like(south_edges)
    corner_sw[...] = jnp.zeros_like(corner_sw)
    corner_se[...] = jnp.zeros_like(corner_se)

    def rank(lon, lat):
        z, y, x, core = (lat // 4) * 6 + lon // 16, (lon % 16) // 2, lat % 4, lon % 2
        guess = jnp.where(z < 6, 14 * z, 60 + 5 * z) + 6 * jnp.minimum(y, 9 - y) + 4 * x + 4 * (1 - core)
        guess = guess + jnp.where(lon + lat == 0, 100, 0)
        return guess * 1024 + lat * lon_count + lon

    mine = rank(t, j)
    first, last = pl.ds(0, 128), pl.ds(896, 128)

    def copy(src, dst, slot, sender, lon, lat):
        return pltpu.make_async_remote_copy(
            src_ref=src,
            dst_ref=dst,
            send_sem=send_sems.at[sender],
            recv_sem=recv_sems.at[slot],
            device_id={"lon": lon, "lat": lat},
            device_id_type=MESH,
        )

    class Route:
        def __init__(self, there, lon, lat, here, yonder, *copies):
            self.there, self.lon, self.lat, self.here, self.yonder = there, lon, lat, here, yonder
            theirs = rank(lon, lat)
            self.greets = there & (mine < theirs)
            self.answers = there & (mine > theirs)
            self.far = theirs - mine > 25 * 1024
            self.copies = [copy(*c, lon, lat) for c in copies]

        def signal(self, sem):
            pl.semaphore_signal(
                sem, inc=1, device_id={"lon": self.lon, "lat": self.lat}, device_id_type=MESH
            )

        def send(self):
            for c in self.copies:
                c.start()

    below, above, fold = j > 0, j < top, j == top
    routes = [
        Route(
            below, t, j - 1, 2, 3,
            (own.at[:, 8:11, :], north.at[:, 0:3, :], HN, 2),
            (edges.at[:, first], north_edges, BN, 3),
        ),
        Route(below, east, j - 1, 4, 7, (edges.at[0:8, first], corner_nw, NW, 4)),
        Route(below, west, j - 1, 5, 6, (edges.at[8:16, first], corner_ne, NE, 5)),
        Route(
            above, t, j + 1, 3, 2,
            (own.at[:, 69:72, :], south.at[:, 5:8, :], HS, 6),
            (edges.at[:, last], south_edges, BS, 7),
        ),
        Route(above, east, j + 1, 6, 5, (edges.at[0:8, last], corner_sw, SW, 8)),
        Route(above, west, j + 1, 7, 4, (edges.at[8:16, last], corner_se, SE, 9)),
        Route(
            fold, mirror, j, 3, 3,
            (fold_rows.at[:, 0:3, :], north.at[:, 0:3, :], HN, 6),
            (fold_edges, north_edges, BN, 7),
        ),
        Route(
            fold & (mirror_down != t), mirror_down, j, 6, 6,
            (fold_edges.at[8:16, :], corner_ne, NE, 9),
        ),
        Route(
            fold & (mirror_up != t), mirror_up, j, 7, 7,
            (fold_edges.at[0:8, :], corner_nw, NW, 8),
        ),
        Route(j >= 0, east, j, 0, 1, (edges.at[5:8, :], west_cols.at[5:8, :], HW, 0)),
        Route(j >= 0, west, j, 1, 0, (edges.at[8:11, :], east_cols.at[0:3, :], HE, 1)),
    ]

    barrier = pltpu.get_barrier_semaphore()
    greeted = jnp.int32(0)
    for route in routes:
        greeted = greeted + route.answers.astype(jnp.int32)

        @pl.when(route.greets)
        def _():
            route.signal(barrier)

    @pl.when(greeted > 0)
    def _():
        pl.semaphore_wait(barrier, greeted)

    for route in routes:

        @pl.when(route.answers)
        def _():
            route.signal(answers.at[route.yonder])

    own[:, 0:8, :] = jnp.zeros((16, 8, 128), F32)
    own[:, 72:80, :] = jnp.zeros((16, 8, 128), F32)
    zeros = jnp.zeros((128, 128), BF16)
    for ref in (hidden_a, hidden_b):
        ref[0:128, :] = zeros
        ref[1152:1280, :] = zeros

    loads[0].wait()

    for g in range(8):
        turned = own[:, 8 * g + 8 : 8 * g + 16, :].reshape(128, 128).T
        edges[0:8, 128 * g : 128 * g + 128] = turned[120:128]
        edges[8:16, 128 * g : 128 * g + 128] = turned[0:8]

    @pl.when(fold)
    def _():
        back = 127 - iota((8, 128), 1)
        up = 7 - iota((8, 128), 0)
        for ch in range(16):
            x = own[ch, 64:72, :]
            x = jnp.take_along_axis(x, back, axis=1)
            x = jnp.take_along_axis(x, up, axis=0)
            fold_rows[ch] = -x if ch < 8 else x
        lane = iota((8, 128), 1)
        rows_back = lane + 7 - 2 * (lane % 8)
        for at in (0, 8):
            x = edges[at : at + 8, 896:1024]
            x = jnp.take_along_axis(x, rows_back, axis=1)
            x = jnp.take_along_axis(x, up, axis=0)
            fold_edges[8 - at : 16 - at, :] = jnp.where(lane < 64, -x, x)

    for route in routes:
        pl.when(route.answers)(route.send)

    @pl.when(fold & (mirror_up == t))
    def _():
        corner_nw[...] = fold_edges[0:8, :]

    @pl.when(fold & (mirror_down == t))
    def _():
        corner_ne[...] = fold_edges[8:16, :]

    for load in loads[1:]:
        load.wait()
    bands(taps_one, spread, band_one)
    bands(taps_two, spread, band_two)
    bands(taps_three, spread, band_three)
    lane_out = iota((1, 128), 1) // 8
    bias_rows = []
    for i, (ref, outs) in enumerate(((b_one, 16), (b_two, 16), (b_three, 8))):
        row = jnp.zeros((1, 128), F32)
        for o in range(outs):
            bias_full[i, 8 * o : 8 * o + 8, :] = jnp.full((8, 128), ref[o], F32)
            row = jnp.where(lane_out == o, ref[o], row)
        bias_rows.append(row)

    for route in routes:

        @pl.when(route.greets & ~route.far)
        def _():
            pl.semaphore_wait(answers.at[route.here], 1)
            route.send()

    for g in range(8):
        x = own[:, 8 * g + 8 : 8 * g + 16, :].reshape(128, 128)
        hidden_a[128 * g + 128 : 128 * g + 256, :] = x.astype(BF16)

    band_last = jnp.concatenate(
        [band_three[128 * c : 128 * c + 64, :] for c in range(3)], axis=0
    )

    def windows(ref, g):
        return jnp.concatenate(
            [ref[128 * g : 128 * g + 384, :], ref[128 * g + 128 : 128 * g + 512, :]], axis=1
        )

    for src, band, i, dst in (
        (hidden_a, band_one, 0, hidden_b),
        (hidden_b, band_two, 1, hidden_a),
    ):
        for g in range(0, 8, 2):
            y = jnp.dot(band[...], windows(src, g), preferred_element_type=F32)
            for h, v in enumerate(across(y, 128)):
                at = 128 * (g + h) + 128
                dst[at : at + 128, :] = silu(v + bias_full[i]).astype(BF16)

    lane = iota((8, 128), 1)
    row = iota((8, 128), 0)
    for g in range(0, 8, 2):
        y = jnp.dot(band_last, windows(hidden_a, g), preferred_element_type=F32)
        for h, v in enumerate(across(y, 64)):
            inner = (lane >= 3) & (lane < 125)
            if g + h == 0:
                inner = inner & (row >= 3)
            if g + h == 7:
                inner = inner & (row < 5)
            forcing = jnp.where(inner[None], (v + bias_full[2, 0:64, :]).reshape(8, 8, 128), 0.0)
            at = 8 * (g + h)
            x = own[:, at + 8 : at + 16, :]
            qn = own[:, at + 9 : at + 17, :]
            qs = own[:, at + 7 : at + 15, :]
            qe = jnp.where(lane[None] < 127, roll(x, -1, 2), 0.0)
            qw = jnp.where(lane[None] > 0, roll(x, 1, 2), 0.0)
            u = jnp.concatenate([x[0:4]] * 4, axis=0)
            w = jnp.concatenate([x[4:8]] * 4, axis=0)
            tendency = -0.5 * (u * (qe - qw) + w * (qn - qs))
            tendency = tendency + 0.2 * (qe + qw + qn + qs - 4.0 * x)
            tendency = jnp.concatenate([tendency[0:8] + forcing, tendency[8:16]], axis=0)
            ocean = 0.1 * mask[at : at + 8, :].astype(F32)
            out[:, at : at + 8, :] = x + ocean[None] * tendency

    for route in routes:

        @pl.when(route.greets & route.far)
        def _():
            pl.semaphore_wait(answers.at[route.here], 1)
            route.send()

    def arrive(dst, slot):
        copy(dst, dst, slot, 0, east, j).wait_recv()

    arrive(west_cols.at[5:8, :], HW)
    arrive(east_cols.at[0:3, :], HE)

    @pl.when(below)
    def _():
        arrive(south.at[:, 5:8, :], HS)
        arrive(south_edges, BS)
        arrive(corner_sw, SW)
        arrive(corner_se, SE)

    arrive(north.at[:, 0:3, :], HN)
    arrive(north_edges, BN)

    @pl.when(above | (mirror_up != t))
    def _():
        arrive(corner_nw, NW)

    @pl.when(above | (mirror_down != t))
    def _():
        arrive(corner_ne, NE)

    strip = jnp.concatenate(
        [
            jnp.concatenate([south[...], own[:, 64:72, :]], axis=2).reshape(128, 256),
            jnp.concatenate([own[:, 8:16, :], north[...]], axis=2).reshape(128, 256),
        ],
        axis=0,
    ).astype(BF16)
    cols = [
        jnp.concatenate(
            [corner_sw[...], south_edges[8:16, :], south_edges[0:8, :], corner_se[...]], axis=0
        )
    ]
    for g in range(8):
        at = pl.ds(128 * g, 128)
        cols.append(
            jnp.concatenate(
                [west_cols[:, at], edges[8:16, at], edges[0:8, at], east_cols[:, at]], axis=0
            )
        )
    cols.append(
        jnp.concatenate(
            [corner_nw[...], north_edges[8:16, :], north_edges[0:8, :], corner_ne[...]], axis=0
        )
    )
    cols = [x.astype(BF16) for x in cols]

    def sides(cols, band, groups):
        none = jnp.zeros((32, 128), BF16)
        padded = [none] + cols + [none]
        lhs = jnp.concatenate(
            [jnp.concatenate(padded[g : g + 3], axis=1) for g in groups], axis=0
        )
        y = lax.dot_general(
            lhs, band[...], (((1,), (1,)), ((), ())), preferred_element_type=F32
        )
        return down(y, len(groups))

    for band, i in ((band_one, 0), (band_two, 1)):
        halves = []
        for at in (128, 0):
            y = jnp.dot(band[:, at : at + 256], strip, preferred_element_type=F32)
            bias = bias_full[i]
            halves.append(
                jnp.concatenate([silu(v + bias).astype(BF16) for v in across(y, 128)], axis=1)
            )
        strip = jnp.concatenate(halves, axis=0)
        y = silu(sides(cols, band, range(10)) + bias_rows[i][None]).astype(BF16)
        cols = [y[g] for g in range(10)]

    bias = bias_full[2, 0:64, :]
    y = jnp.dot(band_last[:, 0:256], strip[:, 0:128], preferred_element_type=F32)
    forcing_south = (across(y, 64)[0] + bias).reshape(8, 8, 128)
    y = jnp.dot(band_last[:, 128:384], strip[:, 128:256], preferred_element_type=F32)
    forcing_north = (across(y, 64)[0] + bias).reshape(8, 8, 128)
    forcing_sides = sides(cols, band_three, range(1, 9)) + bias_rows[2][None]

    place = iota((8, 128), 0)
    lane = iota((8, 128), 1)
    patches = []
    for g in range(8):
        at = pl.ds(128 * g, 128)

        def speed(x):
            x = jnp.where(lane < 32, x, 0.0)
            x = x + roll(x, 32, 1)
            return x + roll(x, 64, 1)

        e = edges[0:8, at]
        w = edges[8:16, at]
        east_term = jnp.where(place == 7, (0.2 - 0.5 * speed(e)) * roll(east_cols[:, at], -1, 0), 0.0)
        west_term = jnp.where(place == 0, (0.2 + 0.5 * speed(w)) * roll(west_cols[:, at], 1, 0), 0.0)
        patches.append(forcing_sides[g, 16:24] + east_term)
        patches.append(forcing_sides[g, 8:16] + west_term)
    turned = jnp.concatenate(patches, axis=0).T
    inner = (lane >= 3) & (lane < 125)
    for g in range(8):
        patch = roll(turned, 120 - 16 * g, 1).reshape(16, 8, 128)
        patch = jnp.where(inner[None], 0.0, patch)
        if g in (0, 7):
            x = own[:, 8 * g + 8 : 8 * g + 16, :]
            v = jnp.concatenate([x[4:8]] * 4, axis=0)
            if g == 0:
                near = jnp.where(place[None] == 0, (0.2 + 0.5 * v) * roll(south[...], 1, 1), 0.0)
                forcing = jnp.where((inner & (place < 3))[None], forcing_south, 0.0)
            else:
                near = jnp.where(place[None] == 7, (0.2 - 0.5 * v) * roll(north[...], -1, 1), 0.0)
                forcing = jnp.where((inner & (place >= 5))[None], forcing_north, 0.0)
            patch = patch + near
            patch = jnp.concatenate([patch[0:8] + forcing, patch[8:16]], axis=0)
        at = 8 * g
        ocean = 0.1 * mask[at : at + 8, :].astype(F32)
        out[:, at : at + 8, :] = out[:, at : at + 8, :] + ocean[None] * patch

    for route in routes:

        @pl.when(route.there)
        def _():
            for c in route.copies:
                c.wait_send()


def solution(mesh):
    lon_count, lat_count = mesh.shape["lon"], mesh.shape["lat"]

    def step(*args):
        state, *rest = [pltpu.with_memory_space_constraint(x, pltpu.HBM) for x in args]
        return pl.pallas_call(
            functools.partial(kernel, lon_count, lat_count),
            out_shape=jax.ShapeDtypeStruct(state.shape, F32),
            in_specs=[pl.BlockSpec(memory_space=pltpu.HBM)] * 8,
            out_specs=pl.BlockSpec(memory_space=pltpu.VMEM),
            scratch_shapes=[
                pltpu.VMEM((16, 80, 128), F32),
                pltpu.VMEM((64, 128), jnp.int32),
                pltpu.VMEM((3, 3, 16, 16), BF16),
                pltpu.VMEM((3, 3, 16, 16), BF16),
                pltpu.VMEM((3, 3, 8, 16), BF16),
                pltpu.SMEM((16,), F32),
                pltpu.SMEM((16,), F32),
                pltpu.SMEM((8,), F32),
                pltpu.VMEM((16, 8, 128), F32),
                pltpu.VMEM((16, 8, 128), F32),
                pltpu.VMEM((16, 1024), F32),
                pltpu.VMEM((8, 1024), F32),
                pltpu.VMEM((8, 1024), F32),
                pltpu.VMEM((16, 128), F32),
                pltpu.VMEM((16, 128), F32),
                pltpu.VMEM((8, 128), F32),
                pltpu.VMEM((8, 128), F32),
                pltpu.VMEM((8, 128), F32),
                pltpu.VMEM((8, 128), F32),
                pltpu.VMEM((16, 8, 128), F32),
                pltpu.VMEM((16, 128), F32),
                pltpu.VMEM((144, 128), F32),
                pltpu.VMEM((384, 384), BF16),
                pltpu.VMEM((384, 384), BF16),
                pltpu.VMEM((384, 384), BF16),
                pltpu.VMEM((3, 128, 128), F32),
                pltpu.VMEM((1280, 128), BF16),
                pltpu.VMEM((1280, 128), BF16),
                pltpu.SemaphoreType.DMA((8,)),
                pltpu.SemaphoreType.DMA((10,)),
                pltpu.SemaphoreType.DMA((10,)),
                pltpu.SemaphoreType.REGULAR((8,)),
            ],
            compiler_params=pltpu.CompilerParams(
                collective_id=0, has_side_effects=True, vmem_limit_bytes=32 * 1024 * 1024
            ),
        )(state, *rest)

    return jax.shard_map(
        step,
        mesh=mesh,
        in_specs=(P(None, "lat", "lon"), P("lat", "lon"), P(), P(), P(), P(), P(), P()),
        out_specs=P(None, "lat", "lon"),
        check_vma=False,
    )
```

```python
import functools

import jax
import jax.numpy as jnp
from jax import lax
from jax.experimental import pallas as pl
from jax.experimental.pallas import tpu as pltpu
from jax.sharding import PartitionSpec as P

MESH = pl.DeviceIdType.MESH
F32, BF16 = jnp.float32, jnp.bfloat16
HW, HE, HS, HN, SW, SE, NW, NE = range(8)


def iota(shape, dim):
    return lax.broadcasted_iota(jnp.int32, shape, dim)


def silu(v):
    half = 0.5 * v
    return half + half * jnp.tanh(half)


def roll(x, shift, axis):
    return pltpu.roll(x, shift % x.shape[axis], axis)


def bands(taps, spread, band):
    outs = taps.shape[2]
    spreading = (iota((16, 128), 0) == iota((16, 128), 1) // 8).astype(BF16)
    flat = taps[...].reshape(9 * outs, 16)
    spread[0 : 9 * outs, :] = jnp.dot(flat, spreading, preferred_element_type=F32)
    ahead = iota((8, 128), 1) % 8 - iota((8, 128), 0)
    for c in range(3):
        for pair in range(8):
            parts = []
            for o in (2 * pair, 2 * pair + 1):
                if o >= outs:
                    parts.append(jnp.zeros((8, 384), F32))
                    continue
                tap = []
                for a in range(3):
                    at = (a * 3 + c) * outs + o
                    tap.append(jnp.broadcast_to(spread[at : at + 1, :], (8, 128)))
                before = jnp.where(ahead == 7, tap[0], 0.0)
                centre = jnp.where(
                    ahead == -1,
                    tap[0],
                    jnp.where(ahead == 0, tap[1], jnp.where(ahead == 1, tap[2], 0.0)),
                )
                after = jnp.where(ahead == -7, tap[2], 0.0)
                parts.append(jnp.concatenate([before, centre, after], axis=1))
            at = c * 128 + pair * 16
            band[at : at + 16, :] = jnp.concatenate(parts, axis=0).astype(BF16)


def across(y, outs):
    parts = []
    for at in range(0, y.shape[1], 128):
        z = y[:, at : at + 128]
        parts.append(
            roll(z[0:outs], 1, 1) + z[outs : 2 * outs] + roll(z[2 * outs : 3 * outs], -1, 1)
        )
    return parts


def down(y, groups):
    z = [y[:, 128 * c : 128 * c + 128].reshape(groups, 32, 128) for c in range(3)]
    return roll(z[0], 1, 1) + z[1] + roll(z[2], -1, 1)


def kernel(
    lon_count,
    lat_count,
    state,
    land_mask,
    kernel_one,
    bias_one,
    kernel_two,
    bias_two,
    kernel_three,
    bias_three,
    out,
    own,
    mask,
    taps_one,
    taps_two,
    taps_three,
    b_one,
    b_two,
    b_three,
    south,
    north,
    edges,
    west_cols,
    east_cols,
    corner_sw,
    corner_se,
    corner_nw,
    corner_ne,
    fold_rows,
    fold_edges,
    spread,
    band_one,
    band_two,
    band_three,
    bias_full,
    hidden_a,
    hidden_b,
    in_sems,
    send_sems,
    recv_sems,
    answers,
):
    t, j = lax.axis_index("lon"), lax.axis_index("lat")
    top = lat_count - 1
    east, west = lax.rem(t + 1, lon_count), lax.rem(t + lon_count - 1, lon_count)
    mirror = lon_count - 1 - t
    mirror_up = lax.rem(mirror + 1, lon_count)
    mirror_down = lax.rem(mirror + lon_count - 1, lon_count)

    loads = [
        pltpu.make_async_copy(src, dst, in_sems.at[i])
        for i, (src, dst) in enumerate(
            [
                (state.at[:, 0:8, :], own.at[:, 8:16, :]),
                (state.at[:, 56:64, :], own.at[:, 64:72, :]),
                (state.at[:, 8:56, :], own.at[:, 16:64, :]),
                (land_mask, mask),
                (kernel_one, taps_one),
                (kernel_two, taps_two),
                (kernel_three, taps_three),
                (bias_one, b_one),
                (bias_two, b_two),
                (bias_three, b_three),
            ]
        )
    ]
    for load in loads:
        load.start()

    def rank(lon, lat):
        z, y, x, core = (lat // 4) * 6 + lon // 16, (lon % 16) // 2, lat % 4, lon % 2
        guess = jnp.where(z < 6, 128 + 150 * z, 940 + 30 * z) + 45 * x - 41 * core
        guess = guess + jnp.where(y < 4, 57 * y, 430 - 35 * y)
        guess = jnp.where(lon + lat == 0, 1050, guess)
        return guess * 1024 + lat * lon_count + lon

    mine = rank(t, j)
    first, last = pl.ds(0, 128), pl.ds(896, 128)

    def copy(src, dst, slot, sender, lon, lat):
        return pltpu.make_async_remote_copy(
            src_ref=src,
            dst_ref=dst,
            send_sem=send_sems.at[sender],
            recv_sem=recv_sems.at[slot],
            device_id={"lon": lon, "lat": lat},
            device_id_type=MESH,
        )

    class Route:
        def __init__(self, there, lon, lat, here, yonder, *copies, step=0):
            self.there, self.lon, self.lat, self.here, self.yonder = there, lon, lat, here, yonder
            theirs = rank(lon, lat)
            ahead = mine < theirs
            if step == 1:
                ahead = ahead | (j == seam)
            if step == -1:
                ahead = ahead & (j != seam + 1)
            self.greets = there & ahead
            self.answers = there & ~ahead
            self.far = (theirs - mine > 250 * 1024) | (step == 2)
            self.copies = [copy(*c, lon, lat) for c in copies]

        def signal(self, sem):
            pl.semaphore_signal(
                sem, inc=1, device_id={"lon": self.lon, "lat": self.lat}, device_id_type=MESH
            )

        def send(self):
            for c in self.copies:
                c.start()

    below, above, fold = j > 0, j < top, j == top
    seam = lat_count // 2 if lat_count > 3 else lat_count
    beside = j != seam
    e_cols, w_cols = pl.ds(5, 3), pl.ds(8, 3)
    routes = [
        Route(below, t, j - 1, 2, 3, (state.at[:, 0:3, :], north.at[:, 0:3, :], HN, 2), step=-1),
        Route(
            above, t, j + 1, 3, 2, (state.at[:, 61:64, :], south.at[:, 5:8, :], HS, 6), step=1
        ),
        Route(below, east, j - 1, 4, 7, (edges.at[e_cols, first], corner_nw.at[5:8, :], NW, 4), step=-1),
        Route(below, west, j - 1, 5, 6, (edges.at[w_cols, first], corner_ne.at[0:3, :], NE, 5), step=-1),
        Route(above, east, j + 1, 6, 5, (edges.at[e_cols, last], corner_sw.at[5:8, :], SW, 8), step=1),
        Route(above, west, j + 1, 7, 4, (edges.at[w_cols, last], corner_se.at[0:3, :], SE, 9), step=1),
        Route(fold, mirror, j, 3, 3, (fold_rows.at[:, 0:3, :], north.at[:, 0:3, :], HN, 6)),
        Route(
            fold & (mirror_down != t), mirror_down, j, 6, 6,
            (fold_edges.at[8:11, :], corner_ne.at[0:3, :], NE, 9),
        ),
        Route(
            fold & (mirror_up != t), mirror_up, j, 7, 7,
            (fold_edges.at[5:8, :], corner_nw.at[5:8, :], NW, 8),
        ),
        Route(beside, east, j, 0, 1, (edges.at[e_cols, :], west_cols.at[5:8, :], HW, 0)),
        Route(beside, west, j, 1, 0, (edges.at[w_cols, :], east_cols.at[0:3, :], HE, 1)),
    ]
    rows_routes, edge_routes = routes[0:2], routes[2:]

    barrier = pltpu.get_barrier_semaphore()
    greeted = jnp.int32(0)
    for route in routes:
        greeted = greeted + route.answers.astype(jnp.int32)

        @pl.when(route.greets)
        def _():
            route.signal(barrier)

    @pl.when(greeted > 0)
    def _():
        pl.semaphore_wait(barrier, greeted)

    for route in routes:

        @pl.when(route.answers)
        def _():
            route.signal(answers.at[route.yonder])

    for route in rows_routes:
        pl.when(route.answers)(route.send)

    own[:, 0:8, :] = jnp.zeros((16, 8, 128), F32)
    own[:, 72:80, :] = jnp.zeros((16, 8, 128), F32)
    zeros = jnp.zeros((128, 128), BF16)
    for ref in (hidden_a, hidden_b):
        ref[0:128, :] = zeros
        ref[1152:1280, :] = zeros

    loads[0].wait()
    loads[1].wait()

    def turn(g):
        turned = own[:, 8 * g + 8 : 8 * g + 16, :].reshape(128, 128).T
        edges[0:8, 128 * g : 128 * g + 128] = turned[120:128]
        edges[8:16, 128 * g : 128 * g + 128] = turned[0:8]

    turn(0)
    turn(7)

    @pl.when(fold)
    def _():
        back = 127 - iota((8, 128), 1)
        up = 7 - iota((8, 128), 0)
        for ch in range(16):
            x = own[ch, 64:72, :]
            x = jnp.take_along_axis(x, back, axis=1)
            x = jnp.take_along_axis(x, up, axis=0)
            fold_rows[ch] = -x if ch < 8 else x
        lane = iota((8, 128), 1)
        rows_back = lane + 7 - 2 * (lane % 8)
        for at in (0, 8):
            x = edges[at : at + 8, 896:1024]
            x = jnp.take_along_axis(x, rows_back, axis=1)
            x = jnp.take_along_axis(x, up, axis=0)
            fold_edges[8 - at : 16 - at, :] = jnp.where(lane < 64, -x, x)

    for route in edge_routes[:-2]:
        pl.when(route.answers)(route.send)

    loads[2].wait()
    for g in range(1, 7):
        turn(g)

    for route in edge_routes[-2:]:
        pl.when(route.answers)(route.send)

    @pl.when(fold & (mirror_up == t))
    def _():
        corner_nw[5:8, :] = fold_edges[5:8, :]

    @pl.when(fold & (mirror_down == t))
    def _():
        corner_ne[0:3, :] = fold_edges[8:11, :]

    for load in loads[3:]:
        load.wait()
    bands(taps_one, spread, band_one)
    bands(taps_two, spread, band_two)
    bands(taps_three, spread, band_three)
    lane_out = iota((1, 128), 1) // 8
    bias_rows = []
    for i, (ref, outs) in enumerate(((b_one, 16), (b_two, 16), (b_three, 8))):
        row = jnp.zeros((1, 128), F32)
        for o in range(outs):
            bias_full[i, 8 * o : 8 * o + 8, :] = jnp.full((8, 128), ref[o], F32)
            row = jnp.where(lane_out == o, ref[o], row)
        bias_rows.append(row)

    for route in routes:

        @pl.when(route.greets & ~route.far)
        def _():
            pl.semaphore_wait(answers.at[route.here], 1)
            route.send()

    @pl.when(j == seam)
    def _():
        for route in routes[-2:]:
            route.send()

    for g in range(8):
        x = own[:, 8 * g + 8 : 8 * g + 16, :].reshape(128, 128)
        hidden_a[128 * g + 128 : 128 * g + 256, :] = x.astype(BF16)

    band_last = jnp.concatenate(
        [band_three[128 * c : 128 * c + 64, :] for c in range(3)], axis=0
    )

    def windows(ref, g):
        return jnp.concatenate(
            [ref[128 * g : 128 * g + 384, :], ref[128 * g + 128 : 128 * g + 512, :]], axis=1
        )

    for src, band, i, dst in (
        (hidden_a, band_one, 0, hidden_b),
        (hidden_b, band_two, 1, hidden_a),
    ):
        for g in range(0, 8, 2):
            y = jnp.dot(band[...], windows(src, g), preferred_element_type=F32)
            for h, v in enumerate(across(y, 128)):
                at = 128 * (g + h) + 128
                dst[at : at + 128, :] = silu(v + bias_full[i]).astype(BF16)

    lane = iota((8, 128), 1)
    row = iota((8, 128), 0)
    for g in range(0, 8, 2):
        y = jnp.dot(band_last, windows(hidden_a, g), preferred_element_type=F32)
        for h, v in enumerate(across(y, 64)):
            inner = (lane >= 3) & (lane < 125)
            if g + h == 0:
                inner = inner & (row >= 3)
            if g + h == 7:
                inner = inner & (row < 5)
            forcing = jnp.where(inner[None], (v + bias_full[2, 0:64, :]).reshape(8, 8, 128), 0.0)
            at = 8 * (g + h)
            x = own[:, at + 8 : at + 16, :]
            qn = own[:, at + 9 : at + 17, :]
            qs = own[:, at + 7 : at + 15, :]
            qe = jnp.where(lane[None] < 127, roll(x, -1, 2), 0.0)
            qw = jnp.where(lane[None] > 0, roll(x, 1, 2), 0.0)
            u = jnp.concatenate([x[0:4]] * 4, axis=0)
            w = jnp.concatenate([x[4:8]] * 4, axis=0)
            tendency = -0.5 * (u * (qe - qw) + w * (qn - qs))
            tendency = tendency + 0.2 * (qe + qw + qn + qs - 4.0 * x)
            tendency = jnp.concatenate([tendency[0:8] + forcing, tendency[8:16]], axis=0)
            ocean = 0.1 * mask[at : at + 8, :].astype(F32)
            out[:, at : at + 8, :] = x + ocean[None] * tendency

    for route in routes:

        @pl.when(route.greets & route.far)
        def _():
            pl.semaphore_wait(answers.at[route.here], 1)
            route.send()

    def arrive(dst, slot):
        copy(dst, dst, slot, 0, east, j).wait_recv()

    arrive(west_cols.at[5:8, :], HW)
    arrive(east_cols.at[0:3, :], HE)

    @pl.when(below)
    def _():
        arrive(south.at[:, 5:8, :], HS)
        arrive(corner_sw.at[5:8, :], SW)
        arrive(corner_se.at[0:3, :], SE)

    arrive(north.at[:, 0:3, :], HN)

    @pl.when(above | (mirror_up != t))
    def _():
        arrive(corner_nw.at[5:8, :], NW)

    @pl.when(above | (mirror_down != t))
    def _():
        arrive(corner_ne.at[0:3, :], NE)

    place = iota((8, 128), 0)
    rows_south = jnp.where(((place >= 5) & below)[None], south[...], 0.0)
    rows_north = jnp.where((place < 3)[None], north[...], 0.0)
    south_turned = rows_south.reshape(128, 128).T
    north_turned = rows_north.reshape(128, 128).T
    strip = jnp.concatenate(
        [
            jnp.concatenate([rows_south, own[:, 64:72, :]], axis=2).reshape(128, 256),
            jnp.concatenate([own[:, 8:16, :], rows_north], axis=2).reshape(128, 256),
        ],
        axis=0,
    ).astype(BF16)
    cols = [
        jnp.concatenate(
            [
                jnp.where(below, corner_sw[...], 0.0),
                south_turned[0:8],
                south_turned[120:128],
                jnp.where(below, corner_se[...], 0.0),
            ],
            axis=0,
        )
    ]
    for g in range(8):
        at = pl.ds(128 * g, 128)
        cols.append(
            jnp.concatenate(
                [west_cols[:, at], edges[8:16, at], edges[0:8, at], east_cols[:, at]], axis=0
            )
        )
    cols.append(
        jnp.concatenate(
            [corner_nw[...], north_turned[0:8], north_turned[120:128], corner_ne[...]], axis=0
        )
    )
    cols = [x.astype(BF16) for x in cols]

    def sides(cols, band, groups):
        none = jnp.zeros((32, 128), BF16)
        padded = [none] + cols + [none]
        lhs = jnp.concatenate(
            [jnp.concatenate(padded[g : g + 3], axis=1) for g in groups], axis=0
        )
        y = lax.dot_general(
            lhs, band[...], (((1,), (1,)), ((), ())), preferred_element_type=F32
        )
        return down(y, len(groups))

    for band, i in ((band_one, 0), (band_two, 1)):
        halves = []
        for at in (128, 0):
            y = jnp.dot(band[:, at : at + 256], strip, preferred_element_type=F32)
            bias = bias_full[i]
            halves.append(
                jnp.concatenate([silu(v + bias).astype(BF16) for v in across(y, 128)], axis=1)
            )
        strip = jnp.concatenate(halves, axis=0)
        y = silu(sides(cols, band, range(10)) + bias_rows[i][None]).astype(BF16)
        cols = [y[g] for g in range(10)]

    bias = bias_full[2, 0:64, :]
    y = jnp.dot(band_last[:, 0:256], strip[:, 0:128], preferred_element_type=F32)
    forcing_south = (across(y, 64)[0] + bias).reshape(8, 8, 128)
    y = jnp.dot(band_last[:, 128:384], strip[:, 128:256], preferred_element_type=F32)
    forcing_north = (across(y, 64)[0] + bias).reshape(8, 8, 128)
    forcing_sides = sides(cols, band_three, range(1, 9)) + bias_rows[2][None]

    patches = []
    for g in range(8):
        at = pl.ds(128 * g, 128)

        def speed(x):
            x = jnp.where(lane < 32, x, 0.0)
            x = x + roll(x, 32, 1)
            return x + roll(x, 64, 1)

        e = edges[0:8, at]
        w = edges[8:16, at]
        east_term = jnp.where(place == 7, (0.2 - 0.5 * speed(e)) * roll(east_cols[:, at], -1, 0), 0.0)
        west_term = jnp.where(place == 0, (0.2 + 0.5 * speed(w)) * roll(west_cols[:, at], 1, 0), 0.0)
        patches.append(forcing_sides[g, 16:24] + east_term)
        patches.append(forcing_sides[g, 8:16] + west_term)
    turned = jnp.concatenate(patches, axis=0).T
    inner = (lane >= 3) & (lane < 125)
    for g in range(8):
        patch = roll(turned, 120 - 16 * g, 1).reshape(16, 8, 128)
        patch = jnp.where(inner[None], 0.0, patch)
        if g in (0, 7):
            x = own[:, 8 * g + 8 : 8 * g + 16, :]
            v = jnp.concatenate([x[4:8]] * 4, axis=0)
            if g == 0:
                near = jnp.where(place[None] == 0, (0.2 + 0.5 * v) * roll(rows_south, 1, 1), 0.0)
                forcing = jnp.where((inner & (place < 3))[None], forcing_south, 0.0)
            else:
                near = jnp.where(place[None] == 7, (0.2 - 0.5 * v) * roll(rows_north, -1, 1), 0.0)
                forcing = jnp.where((inner & (place >= 5))[None], forcing_north, 0.0)
            patch = patch + near
            patch = jnp.concatenate([patch[0:8] + forcing, patch[8:16]], axis=0)
        at = 8 * g
        ocean = 0.1 * mask[at : at + 8, :].astype(F32)
        out[:, at : at + 8, :] = out[:, at : at + 8, :] + ocean[None] * patch

    for route in routes:

        there = route.there | (j == seam) if route in routes[-2:] else route.there

        @pl.when(there)
        def _():
            for c in route.copies:
                c.wait_send()


def solution(mesh):
    lon_count, lat_count = mesh.shape["lon"], mesh.shape["lat"]

    def step(*args):
        state, *rest = [pltpu.with_memory_space_constraint(x, pltpu.HBM) for x in args]
        return pl.pallas_call(
            functools.partial(kernel, lon_count, lat_count),
            out_shape=jax.ShapeDtypeStruct(state.shape, F32),
            in_specs=[pl.BlockSpec(memory_space=pltpu.HBM)] * 8,
            out_specs=pl.BlockSpec(memory_space=pltpu.VMEM),
            scratch_shapes=[
                pltpu.VMEM((16, 80, 128), F32),
                pltpu.VMEM((64, 128), jnp.int32),
                pltpu.VMEM((3, 3, 16, 16), BF16),
                pltpu.VMEM((3, 3, 16, 16), BF16),
                pltpu.VMEM((3, 3, 8, 16), BF16),
                pltpu.SMEM((16,), F32),
                pltpu.SMEM((16,), F32),
                pltpu.SMEM((8,), F32),
                pltpu.VMEM((16, 8, 128), F32),
                pltpu.VMEM((16, 8, 128), F32),
                pltpu.VMEM((16, 1024), F32),
                pltpu.VMEM((8, 1024), F32),
                pltpu.VMEM((8, 1024), F32),
                pltpu.VMEM((8, 128), F32),
                pltpu.VMEM((8, 128), F32),
                pltpu.VMEM((8, 128), F32),
                pltpu.VMEM((8, 128), F32),
                pltpu.VMEM((16, 8, 128), F32),
                pltpu.VMEM((16, 128), F32),
                pltpu.VMEM((144, 128), F32),
                pltpu.VMEM((384, 384), BF16),
                pltpu.VMEM((384, 384), BF16),
                pltpu.VMEM((384, 384), BF16),
                pltpu.VMEM((3, 128, 128), F32),
                pltpu.VMEM((1280, 128), BF16),
                pltpu.VMEM((1280, 128), BF16),
                pltpu.SemaphoreType.DMA((10,)),
                pltpu.SemaphoreType.DMA((10,)),
                pltpu.SemaphoreType.DMA((10,)),
                pltpu.SemaphoreType.REGULAR((8,)),
            ],
            compiler_params=pltpu.CompilerParams(
                collective_id=0, has_side_effects=True, vmem_limit_bytes=32 * 1024 * 1024
            ),
        )(state, *rest)

    return jax.shard_map(
        step,
        mesh=mesh,
        in_specs=(P(None, "lat", "lon"), P("lat", "lon"), P(), P(), P(), P(), P(), P()),
        out_specs=P(None, "lat", "lon"),
        check_vma=False,
    )
```

```python
import functools

import jax
import jax.numpy as jnp
from jax import lax
from jax.experimental import pallas as pl
from jax.experimental.pallas import tpu as pltpu
from jax.sharding import PartitionSpec as P

MESH = pl.DeviceIdType.MESH
F32, BF16 = jnp.float32, jnp.bfloat16
HW, HE, HS, HN, SW, SE, NW, NE = range(8)


def iota(shape, dim):
    return lax.broadcasted_iota(jnp.int32, shape, dim)


def silu(v):
    half = 0.5 * v
    return half + half * jnp.tanh(half)


def roll(x, shift, axis):
    return pltpu.roll(x, shift % x.shape[axis], axis)


def bands(taps, spread, band):
    outs = taps.shape[2]
    spreading = (iota((16, 128), 0) == iota((16, 128), 1) // 8).astype(BF16)
    flat = taps[...].reshape(9 * outs, 16)
    spread[0 : 9 * outs, :] = jnp.dot(flat, spreading, preferred_element_type=F32)
    ahead = iota((8, 128), 1) % 8 - iota((8, 128), 0)
    for c in range(3):
        for pair in range(8):
            parts = []
            for o in (2 * pair, 2 * pair + 1):
                if o >= outs:
                    parts.append(jnp.zeros((8, 384), F32))
                    continue
                tap = []
                for a in range(3):
                    at = (a * 3 + c) * outs + o
                    tap.append(jnp.broadcast_to(spread[at : at + 1, :], (8, 128)))
                before = jnp.where(ahead == 7, tap[0], 0.0)
                centre = jnp.where(
                    ahead == -1,
                    tap[0],
                    jnp.where(ahead == 0, tap[1], jnp.where(ahead == 1, tap[2], 0.0)),
                )
                after = jnp.where(ahead == -7, tap[2], 0.0)
                parts.append(jnp.concatenate([before, centre, after], axis=1))
            at = c * 128 + pair * 16
            band[at : at + 16, :] = jnp.concatenate(parts, axis=0).astype(BF16)


def across(y, outs):
    parts = []
    for at in range(0, y.shape[1], 128):
        z = y[:, at : at + 128]
        parts.append(
            roll(z[0:outs], 1, 1) + z[outs : 2 * outs] + roll(z[2 * outs : 3 * outs], -1, 1)
        )
    return parts


def down(y, groups):
    z = [y[:, 128 * c : 128 * c + 128].reshape(groups, 32, 128) for c in range(3)]
    return roll(z[0], 1, 1) + z[1] + roll(z[2], -1, 1)


def kernel(
    lon_count,
    lat_count,
    state,
    land_mask,
    kernel_one,
    bias_one,
    kernel_two,
    bias_two,
    kernel_three,
    bias_three,
    out,
    own,
    mask,
    taps_one,
    taps_two,
    taps_three,
    b_one,
    b_two,
    b_three,
    south,
    north,
    edges,
    west_cols,
    east_cols,
    corner_sw,
    corner_se,
    corner_nw,
    corner_ne,
    fold_rows,
    fold_edges,
    spread,
    band_one,
    band_two,
    band_three,
    bias_full,
    hidden_a,
    hidden_b,
    in_sems,
    send_sems,
    recv_sems,
    answers,
):
    t, j = lax.axis_index("lon"), lax.axis_index("lat")
    top = lat_count - 1
    east, west = lax.rem(t + 1, lon_count), lax.rem(t + lon_count - 1, lon_count)
    mirror = lon_count - 1 - t
    mirror_up = lax.rem(mirror + 1, lon_count)
    mirror_down = lax.rem(mirror + lon_count - 1, lon_count)

    loads = [
        pltpu.make_async_copy(src, dst, in_sems.at[i])
        for i, (src, dst) in enumerate(
            [
                (state.at[:, 0:8, :], own.at[:, 8:16, :]),
                (state.at[:, 56:64, :], own.at[:, 64:72, :]),
                (state.at[:, 8:56, :], own.at[:, 16:64, :]),
                (land_mask, mask),
                (kernel_one, taps_one),
                (kernel_two, taps_two),
                (kernel_three, taps_three),
                (bias_one, b_one),
                (bias_two, b_two),
                (bias_three, b_three),
            ]
        )
    ]
    for load in loads:
        load.start()

    def rank(lon, lat):
        z, y, x, core = (lat // 4) * 6 + lon // 16, (lon % 16) // 2, lat % 4, lon % 2
        guess = jnp.where(z < 6, 128 + 150 * z, 940 + 30 * z) + 45 * x - 41 * core
        guess = guess + jnp.where(y < 4, 57 * y, 430 - 35 * y)
        guess = jnp.where(lon + lat == 0, 1050, guess)
        return guess * 1024 + lat * lon_count + lon

    mine = rank(t, j)
    first, last = pl.ds(0, 128), pl.ds(896, 128)

    def copy(src, dst, slot, sender, lon, lat):
        return pltpu.make_async_remote_copy(
            src_ref=src,
            dst_ref=dst,
            send_sem=send_sems.at[sender],
            recv_sem=recv_sems.at[slot],
            device_id={"lon": lon, "lat": lat},
            device_id_type=MESH,
        )

    class Route:
        def __init__(self, there, lon, lat, here, yonder, *copies, step=0, quiet=False):
            self.there, self.lon, self.lat, self.here, self.yonder = there, lon, lat, here, yonder
            theirs = rank(lon, lat)
            ahead = mine < theirs
            level = jnp.abs(theirs - mine) < 300 * 1024
            if here == yonder:
                both = level
            else:
                inside = (lon > 0) & (t > 0) & (lon < lon_count - 1) & (t < lon_count - 1)
                crossing = (j == seam) if step == -1 else (j == seam - 1) if step == 1 else False
                both = level & inside & crossing
            if step == 1:
                ahead = ahead | (j == seam)
            if step == -1:
                ahead = ahead & (j != seam + 1)
            if (here, yonder) == (5, 6):
                ahead = ahead | ((t == lon_count - 1) & (j == seam))
            if (here, yonder) == (6, 5):
                ahead = ahead & ~((t == lon_count - 2) & (j == seam - 1))
            loud = there & ~jnp.bool_(quiet)
            self.greets = loud & (both | ahead)
            self.counts = loud & (both | ~ahead)
            self.answers = loud & ~both & ~ahead
            self.awaits = loud & ~both & ahead
            wraps = (lon - t > 1) | (t - lon > 1)
            self.far = (theirs - mine > 250 * 1024) | (wraps & (here != yonder))
            if (here, yonder) == (5, 6):
                self.awaits = self.awaits & ~((t == lon_count - 1) & (j == seam))
            if (here, yonder) == (6, 5):
                self.answers = self.answers & ~((t == lon_count - 2) & (j == seam - 1))
            self.copies = [copy(*c, lon, lat) for c in copies]

        def signal(self, sem):
            pl.semaphore_signal(
                sem, inc=1, device_id={"lon": self.lon, "lat": self.lat}, device_id_type=MESH
            )

        def send(self):
            for c in self.copies:
                c.start()

    below, above, fold = j > 0, j < top, j == top
    seam = lat_count // 2 if lat_count > 3 and lon_count > 3 else 2 * lat_count
    end = lon_count - 1
    corner = seam < lat_count
    at_first = (t == 0) & (j == 0) & corner
    at_end, at_start = (t == end) & corner, (t == 0) & corner
    e_cols, w_cols = pl.ds(5, 3), pl.ds(8, 3)
    route_s = Route(
        below, t, j - 1, 2, 3, (state.at[:, 0:3, :], north.at[:, 0:3, :], HN, 2),
        step=-1, quiet=at_end & (j == seam),
    )
    route_n = Route(
        above, t, j + 1, 3, 2, (state.at[:, 61:64, :], south.at[:, 5:8, :], HS, 6),
        step=1, quiet=at_end & (j == seam - 1),
    )
    route_se = Route(
        below, east, j - 1, 4, 7, (edges.at[e_cols, first], corner_nw.at[5:8, :], NW, 4),
        step=-1, quiet=at_end & (j == 1),
    )
    route_sw = Route(
        below, west, j - 1, 5, 6, (edges.at[w_cols, first], corner_ne.at[0:3, :], NE, 5),
        step=-1, quiet=at_start & ((j == seam) | (j == seam + 1)),
    )
    route_ne = Route(
        above, east, j + 1, 6, 5, (edges.at[e_cols, last], corner_sw.at[5:8, :], SW, 8),
        step=1, quiet=at_end & ((j == seam - 1) | (j == seam)),
    )
    route_nw = Route(
        above, west, j + 1, 7, 4, (edges.at[w_cols, last], corner_se.at[0:3, :], SE, 9),
        step=1, quiet=at_first,
    )
    fold_routes = [
        Route(fold, mirror, j, 3, 3, (fold_rows.at[:, 0:3, :], north.at[:, 0:3, :], HN, 6)),
        Route(
            fold & (mirror_down != t), mirror_down, j, 6, 6,
            (fold_edges.at[8:11, :], corner_ne.at[0:3, :], NE, 9),
        ),
        Route(
            fold & (mirror_up != t), mirror_up, j, 7, 7,
            (fold_edges.at[5:8, :], corner_nw.at[5:8, :], NW, 8),
        ),
    ]
    route_e = Route(
        j >= 0, east, j, 0, 1, (edges.at[e_cols, :], west_cols.at[5:8, :], HW, 0),
        quiet=(j == seam) | (at_end & (j == 0)),
    )
    route_w = Route(
        j >= 0, west, j, 1, 0, (edges.at[w_cols, :], east_cols.at[0:3, :], HE, 1),
        quiet=(j == seam) | at_first,
    )
    rows_routes = [route_s, route_n]
    corner_routes = [route_se, route_sw, route_ne, route_nw] + fold_routes
    side_routes = [route_e, route_w]
    routes = rows_routes + corner_routes + side_routes

    barrier = pltpu.get_barrier_semaphore()
    greeted = jnp.int32(0)
    for route in routes:
        greeted = greeted + route.counts.astype(jnp.int32)

        @pl.when(route.greets)
        def _():
            route.signal(barrier)

    for host, guest in (((end - 1, 0), (0, 0)), ((end - 1, seam - 1), (0, seam))):
        greeted = greeted + ((t == host[0]) & (j == host[1]) & corner).astype(jnp.int32)

        @pl.when((t == guest[0]) & (j == guest[1]) & corner)
        def _():
            pl.semaphore_signal(
                barrier, inc=1, device_id={"lon": host[0], "lat": host[1]}, device_id_type=MESH
            )

    @pl.when(greeted > 0)
    def _():
        pl.semaphore_wait(barrier, greeted)

    for route in routes:

        @pl.when(route.answers)
        def _():
            route.signal(answers.at[route.yonder])

    for route in rows_routes:
        pl.when(route.counts)(route.send)

    own[:, 0:8, :] = jnp.zeros((16, 8, 128), F32)
    own[:, 72:80, :] = jnp.zeros((16, 8, 128), F32)
    zeros = jnp.zeros((128, 128), BF16)
    for ref in (hidden_a, hidden_b):
        ref[0:128, :] = zeros
        ref[1152:1280, :] = zeros

    loads[0].wait()
    loads[1].wait()

    def turn(g):
        turned = own[:, 8 * g + 8 : 8 * g + 16, :].reshape(128, 128).T
        edges[0:8, 128 * g : 128 * g + 128] = turned[120:128]
        edges[8:16, 128 * g : 128 * g + 128] = turned[0:8]

    turn(0)
    turn(7)

    @pl.when(fold)
    def _():
        back = 127 - iota((8, 128), 1)
        up = 7 - iota((8, 128), 0)
        for ch in range(16):
            x = own[ch, 64:72, :]
            x = jnp.take_along_axis(x, back, axis=1)
            x = jnp.take_along_axis(x, up, axis=0)
            fold_rows[ch] = -x if ch < 8 else x
        lane = iota((8, 128), 1)
        rows_back = lane + 7 - 2 * (lane % 8)
        for at in (0, 8):
            x = edges[at : at + 8, 896:1024]
            x = jnp.take_along_axis(x, rows_back, axis=1)
            x = jnp.take_along_axis(x, up, axis=0)
            fold_edges[8 - at : 16 - at, :] = jnp.where(lane < 64, -x, x)

    for route in corner_routes:
        pl.when(route.counts)(route.send)

    loads[2].wait()
    for g in range(1, 7):
        turn(g)

    for route in side_routes:
        pl.when(route.counts)(route.send)

    @pl.when(fold & (mirror_up == t))
    def _():
        corner_nw[5:8, :] = fold_edges[5:8, :]

    @pl.when(fold & (mirror_down == t))
    def _():
        corner_ne[0:3, :] = fold_edges[8:11, :]

    for load in loads[3:]:
        load.wait()
    bands(taps_one, spread, band_one)
    bands(taps_two, spread, band_two)
    bands(taps_three, spread, band_three)
    lane_out = iota((1, 128), 1) // 8
    bias_rows = []
    for i, (ref, outs) in enumerate(((b_one, 16), (b_two, 16), (b_three, 8))):
        row = jnp.zeros((1, 128), F32)
        for o in range(outs):
            bias_full[i, 8 * o : 8 * o + 8, :] = jnp.full((8, 128), ref[o], F32)
            row = jnp.where(lane_out == o, ref[o], row)
        bias_rows.append(row)

    for route in routes:

        @pl.when(route.awaits & ~route.far)
        def _():
            pl.semaphore_wait(answers.at[route.here], 1)
            route.send()

    @pl.when(j == seam)
    def _():
        route_e.send()

        @pl.when(t > 0)
        def _():
            route_w.send()

        @pl.when(t == end)
        def _():
            route_ne.send()

    for g in range(8):
        x = own[:, 8 * g + 8 : 8 * g + 16, :].reshape(128, 128)
        hidden_a[128 * g + 128 : 128 * g + 256, :] = x.astype(BF16)

    band_last = jnp.concatenate(
        [band_three[128 * c : 128 * c + 64, :] for c in range(3)], axis=0
    )

    def windows(ref, g):
        return jnp.concatenate(
            [ref[128 * g : 128 * g + 384, :], ref[128 * g + 128 : 128 * g + 512, :]], axis=1
        )

    for src, band, i, dst in (
        (hidden_a, band_one, 0, hidden_b),
        (hidden_b, band_two, 1, hidden_a),
    ):
        for g in range(0, 8, 2):
            y = jnp.dot(band[...], windows(src, g), preferred_element_type=F32)
            for h, v in enumerate(across(y, 128)):
                at = 128 * (g + h) + 128
                dst[at : at + 128, :] = silu(v + bias_full[i]).astype(BF16)

    lane = iota((8, 128), 1)
    row = iota((8, 128), 0)
    for g in range(0, 8, 2):
        y = jnp.dot(band_last, windows(hidden_a, g), preferred_element_type=F32)
        for h, v in enumerate(across(y, 64)):
            inner = (lane >= 3) & (lane < 125)
            if g + h == 0:
                inner = inner & (row >= 3)
            if g + h == 7:
                inner = inner & (row < 5)
            forcing = jnp.where(inner[None], (v + bias_full[2, 0:64, :]).reshape(8, 8, 128), 0.0)
            at = 8 * (g + h)
            x = own[:, at + 8 : at + 16, :]
            qn = own[:, at + 9 : at + 17, :]
            qs = own[:, at + 7 : at + 15, :]
            qe = jnp.where(lane[None] < 127, roll(x, -1, 2), 0.0)
            qw = jnp.where(lane[None] > 0, roll(x, 1, 2), 0.0)
            u = jnp.concatenate([x[0:4]] * 4, axis=0)
            w = jnp.concatenate([x[4:8]] * 4, axis=0)
            tendency = -0.5 * (u * (qe - qw) + w * (qn - qs))
            tendency = tendency + 0.2 * (qe + qw + qn + qs - 4.0 * x)
            tendency = jnp.concatenate([tendency[0:8] + forcing, tendency[8:16]], axis=0)
            ocean = 0.1 * mask[at : at + 8, :].astype(F32)
            out[:, at : at + 8, :] = x + ocean[None] * tendency

    for route in [route_e, route_w, route_sw, route_se, route_nw, route_ne] + fold_routes + rows_routes:

        @pl.when(route.awaits & route.far)
        def _():
            pl.semaphore_wait(answers.at[route.here], 1)
            route.send()

        if route is route_w:

            @pl.when(at_start & (j == seam + 1))
            def _():
                route_sw.send()

    def arrive(dst, slot):
        copy(dst, dst, slot, 0, east, j).wait_recv()

    def arrive_west():
        arrive(west_cols.at[5:8, :], HW)

    def arrive_south():
        arrive(south.at[:, 5:8, :], HS)

    def arrive_north():
        arrive(north.at[:, 0:3, :], HN)

    def arrive_sw():
        arrive(corner_sw.at[5:8, :], SW)

    via_west = at_end & ((j == 0) | (j == seam - 1) | (j == seam))
    via_sw = at_end & (j == 1)
    via_south = at_start & (j == seam)
    via_north = at_first

    @pl.when(via_west)
    def _():
        arrive_west()

        @pl.when(j == 0)
        def _():
            route_e.send()

        @pl.when(j == seam - 1)
        def _():
            route_n.send()
            route_ne.send()

        @pl.when(j == seam)
        def _():
            route_s.send()
            route_sw.send()

    @pl.when(via_sw)
    def _():
        arrive_sw()
        route_se.send()

    @pl.when(via_south)
    def _():
        arrive_south()
        route_w.send()
        route_sw.send()

    @pl.when(via_north)
    def _():
        arrive_north()
        route_w.send()
        route_nw.send()

    pl.when(~via_west)(arrive_west)
    arrive(east_cols.at[0:3, :], HE)

    @pl.when(below)
    def _():
        pl.when(~via_south)(arrive_south)
        pl.when(~via_sw)(arrive_sw)
        arrive(corner_se.at[0:3, :], SE)

    pl.when(~via_north)(arrive_north)

    @pl.when(above | (mirror_up != t))
    def _():
        arrive(corner_nw.at[5:8, :], NW)

    @pl.when(above | (mirror_down != t))
    def _():
        arrive(corner_ne.at[0:3, :], NE)

    place = iota((8, 128), 0)
    rows_south = jnp.where(((place >= 5) & below)[None], south[...], 0.0)
    rows_north = jnp.where((place < 3)[None], north[...], 0.0)
    south_turned = rows_south.reshape(128, 128).T
    north_turned = rows_north.reshape(128, 128).T
    strip = jnp.concatenate(
        [
            jnp.concatenate([rows_south, own[:, 64:72, :]], axis=2).reshape(128, 256),
            jnp.concatenate([own[:, 8:16, :], rows_north], axis=2).reshape(128, 256),
        ],
        axis=0,
    ).astype(BF16)
    cols = [
        jnp.concatenate(
            [
                jnp.where(below, corner_sw[...], 0.0),
                south_turned[0:8],
                south_turned[120:128],
                jnp.where(below, corner_se[...], 0.0),
            ],
            axis=0,
        )
    ]
    for g in range(8):
        at = pl.ds(128 * g, 128)
        cols.append(
            jnp.concatenate(
                [west_cols[:, at], edges[8:16, at], edges[0:8, at], east_cols[:, at]], axis=0
            )
        )
    cols.append(
        jnp.concatenate(
            [corner_nw[...], north_turned[0:8], north_turned[120:128], corner_ne[...]], axis=0
        )
    )
    cols = [x.astype(BF16) for x in cols]

    def sides(cols, band, groups):
        none = jnp.zeros((32, 128), BF16)
        padded = [none] + cols + [none]
        lhs = jnp.concatenate(
            [jnp.concatenate(padded[g : g + 3], axis=1) for g in groups], axis=0
        )
        y = lax.dot_general(
            lhs, band[...], (((1,), (1,)), ((), ())), preferred_element_type=F32
        )
        return down(y, len(groups))

    for band, i in ((band_one, 0), (band_two, 1)):
        halves = []
        for at in (128, 0):
            y = jnp.dot(band[:, at : at + 256], strip, preferred_element_type=F32)
            bias = bias_full[i]
            halves.append(
                jnp.concatenate([silu(v + bias).astype(BF16) for v in across(y, 128)], axis=1)
            )
        strip = jnp.concatenate(halves, axis=0)
        y = silu(sides(cols, band, range(10)) + bias_rows[i][None]).astype(BF16)
        cols = [y[g] for g in range(10)]

    bias = bias_full[2, 0:64, :]
    y = jnp.dot(band_last[:, 0:256], strip[:, 0:128], preferred_element_type=F32)
    forcing_south = (across(y, 64)[0] + bias).reshape(8, 8, 128)
    y = jnp.dot(band_last[:, 128:384], strip[:, 128:256], preferred_element_type=F32)
    forcing_north = (across(y, 64)[0] + bias).reshape(8, 8, 128)
    forcing_sides = sides(cols, band_three, range(1, 9)) + bias_rows[2][None]

    patches = []
    for g in range(8):
        at = pl.ds(128 * g, 128)

        def speed(x):
            x = jnp.where(lane < 32, x, 0.0)
            x = x + roll(x, 32, 1)
            return x + roll(x, 64, 1)

        e = edges[0:8, at]
        w = edges[8:16, at]
        east_term = jnp.where(place == 7, (0.2 - 0.5 * speed(e)) * roll(east_cols[:, at], -1, 0), 0.0)
        west_term = jnp.where(place == 0, (0.2 + 0.5 * speed(w)) * roll(west_cols[:, at], 1, 0), 0.0)
        patches.append(forcing_sides[g, 16:24] + east_term)
        patches.append(forcing_sides[g, 8:16] + west_term)
    turned = jnp.concatenate(patches, axis=0).T
    inner = (lane >= 3) & (lane < 125)
    for g in range(8):
        patch = roll(turned, 120 - 16 * g, 1).reshape(16, 8, 128)
        patch = jnp.where(inner[None], 0.0, patch)
        if g in (0, 7):
            x = own[:, 8 * g + 8 : 8 * g + 16, :]
            v = jnp.concatenate([x[4:8]] * 4, axis=0)
            if g == 0:
                near = jnp.where(place[None] == 0, (0.2 + 0.5 * v) * roll(rows_south, 1, 1), 0.0)
                forcing = jnp.where((inner & (place < 3))[None], forcing_south, 0.0)
            else:
                near = jnp.where(place[None] == 7, (0.2 - 0.5 * v) * roll(rows_north, -1, 1), 0.0)
                forcing = jnp.where((inner & (place >= 5))[None], forcing_north, 0.0)
            patch = patch + near
            patch = jnp.concatenate([patch[0:8] + forcing, patch[8:16]], axis=0)
        at = 8 * g
        ocean = 0.1 * mask[at : at + 8, :].astype(F32)
        out[:, at : at + 8, :] = out[:, at : at + 8, :] + ocean[None] * patch

    for route in routes:

        @pl.when(route.there)
        def _():
            for c in route.copies:
                c.wait_send()


def solution(mesh):
    lon_count, lat_count = mesh.shape["lon"], mesh.shape["lat"]

    def step(*args):
        state, *rest = [pltpu.with_memory_space_constraint(x, pltpu.HBM) for x in args]
        return pl.pallas_call(
            functools.partial(kernel, lon_count, lat_count),
            out_shape=jax.ShapeDtypeStruct(state.shape, F32),
            in_specs=[pl.BlockSpec(memory_space=pltpu.HBM)] * 8,
            out_specs=pl.BlockSpec(memory_space=pltpu.VMEM),
            scratch_shapes=[
                pltpu.VMEM((16, 80, 128), F32),
                pltpu.VMEM((64, 128), jnp.int32),
                pltpu.VMEM((3, 3, 16, 16), BF16),
                pltpu.VMEM((3, 3, 16, 16), BF16),
                pltpu.VMEM((3, 3, 8, 16), BF16),
                pltpu.SMEM((16,), F32),
                pltpu.SMEM((16,), F32),
                pltpu.SMEM((8,), F32),
                pltpu.VMEM((16, 8, 128), F32),
                pltpu.VMEM((16, 8, 128), F32),
                pltpu.VMEM((16, 1024), F32),
                pltpu.VMEM((8, 1024), F32),
                pltpu.VMEM((8, 1024), F32),
                pltpu.VMEM((8, 128), F32),
                pltpu.VMEM((8, 128), F32),
                pltpu.VMEM((8, 128), F32),
                pltpu.VMEM((8, 128), F32),
                pltpu.VMEM((16, 8, 128), F32),
                pltpu.VMEM((16, 128), F32),
                pltpu.VMEM((144, 128), F32),
                pltpu.VMEM((384, 384), BF16),
                pltpu.VMEM((384, 384), BF16),
                pltpu.VMEM((384, 384), BF16),
                pltpu.VMEM((3, 128, 128), F32),
                pltpu.VMEM((1280, 128), BF16),
                pltpu.VMEM((1280, 128), BF16),
                pltpu.SemaphoreType.DMA((10,)),
                pltpu.SemaphoreType.DMA((10,)),
                pltpu.SemaphoreType.DMA((10,)),
                pltpu.SemaphoreType.REGULAR((8,)),
            ],
            compiler_params=pltpu.CompilerParams(
                collective_id=0, has_side_effects=True, vmem_limit_bytes=32 * 1024 * 1024
            ),
        )(state, *rest)

    return jax.shard_map(
        step,
        mesh=mesh,
        in_specs=(P(None, "lat", "lon"), P("lat", "lon"), P(), P(), P(), P(), P(), P()),
        out_specs=P(None, "lat", "lon"),
        check_vma=False,
    )
```

```python
import functools

import jax
import jax.numpy as jnp
from jax import lax
from jax.experimental import pallas as pl
from jax.experimental.pallas import tpu as pltpu
from jax.sharding import PartitionSpec as P

MESH = pl.DeviceIdType.MESH
F32, BF16 = jnp.float32, jnp.bfloat16
HW, HE, HS, HN, SW, SE, NW, NE = range(8)


def iota(shape, dim):
    return lax.broadcasted_iota(jnp.int32, shape, dim)


def silu(v):
    half = 0.5 * v
    return half + half * jnp.tanh(half)


def roll(x, shift, axis):
    return pltpu.roll(x, shift % x.shape[axis], axis)


def spread_taps(taps, spread):
    outs = taps.shape[2]
    spreading = (iota((16, 128), 0) == iota((16, 128), 1) // 8).astype(BF16)
    flat = taps[...].reshape(9 * outs, 16)
    spread[0 : 9 * outs, :] = jnp.dot(flat, spreading, preferred_element_type=F32)


def tap_rows(spread, outs, c, o):
    at = [(a * 3 + c) * outs + o for a in range(3)]
    return [jnp.broadcast_to(spread[i : i + 1, :], (8, 128)) for i in at]


def shifted_bands(spread, band, shift):
    ahead = iota((8, 128), 1) % 8 - iota((8, 128), 0)
    for c in range(3):
        for pair in range(8):
            parts = []
            for o in (2 * pair, 2 * pair + 1):
                tap = tap_rows(spread, 16, c, o)
                groups = []
                for g in range(2):
                    part = jnp.zeros((8, 128), F32)
                    for a in range(3):
                        part = jnp.where(ahead == shift + a - 1 - 8 * g, tap[a], part)
                    groups.append(part)
                parts.append(jnp.concatenate(groups, axis=1))
            at = c * 128 + pair * 16
            band[at : at + 16, :] = jnp.concatenate(parts, axis=0).astype(BF16)


def bands(taps, spread, band):
    outs = taps.shape[2]
    spread_taps(taps, spread)
    ahead = iota((8, 128), 1) % 8 - iota((8, 128), 0)
    for c in range(3):
        for pair in range(8):
            parts = []
            for o in (2 * pair, 2 * pair + 1):
                if o >= outs:
                    parts.append(jnp.zeros((8, 384), F32))
                    continue
                tap = tap_rows(spread, outs, c, o)
                before = jnp.where(ahead == 7, tap[0], 0.0)
                centre = jnp.where(
                    ahead == -1,
                    tap[0],
                    jnp.where(ahead == 0, tap[1], jnp.where(ahead == 1, tap[2], 0.0)),
                )
                after = jnp.where(ahead == -7, tap[2], 0.0)
                parts.append(jnp.concatenate([before, centre, after], axis=1))
            at = c * 128 + pair * 16
            band[at : at + 16, :] = jnp.concatenate(parts, axis=0).astype(BF16)


def across(y, outs):
    parts = []
    for at in range(0, y.shape[1], 128):
        z = y[:, at : at + 128]
        parts.append(
            roll(z[0:outs], 1, 1) + z[outs : 2 * outs] + roll(z[2 * outs : 3 * outs], -1, 1)
        )
    return parts


def down(y, groups):
    z = [y[:, 128 * c : 128 * c + 128].reshape(groups, 32, 128) for c in range(3)]
    return roll(z[0], 1, 1) + z[1] + roll(z[2], -1, 1)


def kernel(
    lon_count,
    lat_count,
    state,
    land_mask,
    kernel_one,
    bias_one,
    kernel_two,
    bias_two,
    kernel_three,
    bias_three,
    out,
    own,
    mask,
    taps_one,
    taps_two,
    taps_three,
    b_one,
    b_two,
    b_three,
    south,
    north,
    edges,
    west_cols,
    east_cols,
    corner_sw,
    corner_se,
    corner_nw,
    corner_ne,
    fold_rows,
    fold_edges,
    spread,
    band_one,
    band_two,
    band_three,
    band_south,
    band_north,
    edge_groups,
    bias_full,
    hidden_a,
    hidden_b,
    in_sems,
    send_sems,
    recv_sems,
    answers,
):
    t, j = lax.axis_index("lon"), lax.axis_index("lat")
    top = lat_count - 1
    east, west = lax.rem(t + 1, lon_count), lax.rem(t + lon_count - 1, lon_count)
    mirror = lon_count - 1 - t
    mirror_up = lax.rem(mirror + 1, lon_count)
    mirror_down = lax.rem(mirror + lon_count - 1, lon_count)

    loads = [
        pltpu.make_async_copy(src, dst, in_sems.at[i])
        for i, (src, dst) in enumerate(
            [
                (state.at[:, 0:8, :], own.at[:, 8:16, :]),
                (state.at[:, 56:64, :], own.at[:, 64:72, :]),
                (state.at[:, 8:56, :], own.at[:, 16:64, :]),
                (land_mask, mask),
                (kernel_one, taps_one),
                (kernel_two, taps_two),
                (kernel_three, taps_three),
                (bias_one, b_one),
                (bias_two, b_two),
                (bias_three, b_three),
            ]
        )
    ]
    for load in loads:
        load.start()

    def rank(lon, lat):
        z, y, x, core = (lat // 4) * 6 + lon // 16, (lon % 16) // 2, lat % 4, lon % 2
        guess = jnp.where(z < 6, 128 + 150 * z, 940 + 30 * z) + 45 * x - 41 * core
        guess = guess + jnp.where(y < 4, 57 * y, 430 - 35 * y)
        guess = jnp.where(lon + lat == 0, 1050, guess)
        return guess * 1024 + lat * lon_count + lon

    mine = rank(t, j)
    first, last = pl.ds(0, 128), pl.ds(896, 128)

    def copy(src, dst, slot, sender, lon, lat):
        return pltpu.make_async_remote_copy(
            src_ref=src,
            dst_ref=dst,
            send_sem=send_sems.at[sender],
            recv_sem=recv_sems.at[slot],
            device_id={"lon": lon, "lat": lat},
            device_id_type=MESH,
        )

    class Route:
        def __init__(self, there, lon, lat, here, yonder, *copies, step=0, quiet=False):
            self.there, self.lon, self.lat, self.here, self.yonder = there, lon, lat, here, yonder
            theirs = rank(lon, lat)
            ahead = mine < theirs
            level = jnp.abs(theirs - mine) < 300 * 1024
            if here == yonder:
                both = level
            else:
                inside = (lon > 0) & (t > 0) & (lon < lon_count - 1) & (t < lon_count - 1)
                crossing = (j == seam) if step == -1 else (j == seam - 1) if step == 1 else False
                both = level & inside & crossing
            if step == 1:
                ahead = ahead | (j == seam)
            if step == -1:
                ahead = ahead & (j != seam + 1)
            if (here, yonder) == (5, 6):
                ahead = ahead | ((t == lon_count - 1) & (j == seam))
            if (here, yonder) == (6, 5):
                ahead = ahead & ~((t == lon_count - 2) & (j == seam - 1))
            loud = there & ~jnp.bool_(quiet)
            self.greets = loud & (both | ahead)
            self.counts = loud & (both | ~ahead)
            self.answers = loud & ~both & ~ahead
            self.awaits = loud & ~both & ahead
            wraps = (lon - t > 1) | (t - lon > 1)
            self.far = (theirs - mine > 250 * 1024) | (wraps & (here != yonder))
            if (here, yonder) == (5, 6):
                self.awaits = self.awaits & ~((t == lon_count - 1) & (j == seam))
            if (here, yonder) == (6, 5):
                self.answers = self.answers & ~((t == lon_count - 2) & (j == seam - 1))
            self.copies = [copy(*c, lon, lat) for c in copies]

        def signal(self, sem):
            pl.semaphore_signal(
                sem, inc=1, device_id={"lon": self.lon, "lat": self.lat}, device_id_type=MESH
            )

        def send(self):
            for c in self.copies:
                c.start()

    below, above, fold = j > 0, j < top, j == top
    seam = lat_count // 2 if lat_count > 3 and lon_count > 3 else 2 * lat_count
    end = lon_count - 1
    corner = seam < lat_count
    at_first = (t == 0) & (j == 0) & corner
    at_end, at_start = (t == end) & corner, (t == 0) & corner
    e_cols, w_cols = pl.ds(5, 3), pl.ds(8, 3)
    route_s = Route(
        below, t, j - 1, 2, 3, (state.at[:, 0:3, :], north.at[:, 0:3, :], HN, 2),
        step=-1, quiet=at_end & (j == seam),
    )
    route_n = Route(
        above, t, j + 1, 3, 2, (state.at[:, 61:64, :], south.at[:, 5:8, :], HS, 6),
        step=1, quiet=at_end & (j == seam - 1),
    )
    route_se = Route(
        below, east, j - 1, 4, 7, (edges.at[e_cols, first], corner_nw.at[5:8, :], NW, 4),
        step=-1, quiet=at_end & (j == 1),
    )
    route_sw = Route(
        below, west, j - 1, 5, 6, (edges.at[w_cols, first], corner_ne.at[0:3, :], NE, 5),
        step=-1, quiet=at_start & ((j == seam) | (j == seam + 1)),
    )
    route_ne = Route(
        above, east, j + 1, 6, 5, (edges.at[e_cols, last], corner_sw.at[5:8, :], SW, 8),
        step=1, quiet=at_end & ((j == seam - 1) | (j == seam)),
    )
    route_nw = Route(
        above, west, j + 1, 7, 4, (edges.at[w_cols, last], corner_se.at[0:3, :], SE, 9),
        step=1, quiet=at_first,
    )
    fold_routes = [
        Route(fold, mirror, j, 3, 3, (fold_rows.at[:, 0:3, :], north.at[:, 0:3, :], HN, 6)),
        Route(
            fold & (mirror_down != t), mirror_down, j, 6, 6,
            (fold_edges.at[8:11, :], corner_ne.at[0:3, :], NE, 9),
        ),
        Route(
            fold & (mirror_up != t), mirror_up, j, 7, 7,
            (fold_edges.at[5:8, :], corner_nw.at[5:8, :], NW, 8),
        ),
    ]
    route_e = Route(
        j >= 0, east, j, 0, 1, (edges.at[e_cols, :], west_cols.at[5:8, :], HW, 0),
        quiet=(j == seam) | (at_end & (j == 0)),
    )
    route_w = Route(
        j >= 0, west, j, 1, 0, (edges.at[w_cols, :], east_cols.at[0:3, :], HE, 1),
        quiet=(j == seam) | at_first,
    )
    rows_routes = [route_s, route_n]
    corner_routes = [route_se, route_sw, route_ne, route_nw] + fold_routes
    side_routes = [route_e, route_w]
    routes = rows_routes + corner_routes + side_routes

    barrier = pltpu.get_barrier_semaphore()
    greeted = jnp.int32(0)
    for route in routes:
        greeted = greeted + route.counts.astype(jnp.int32)

        @pl.when(route.greets)
        def _():
            route.signal(barrier)

    for host, guest in (((end - 1, 0), (0, 0)), ((end - 1, seam - 1), (0, seam))):
        greeted = greeted + ((t == host[0]) & (j == host[1]) & corner).astype(jnp.int32)

        @pl.when((t == guest[0]) & (j == guest[1]) & corner)
        def _():
            pl.semaphore_signal(
                barrier, inc=1, device_id={"lon": host[0], "lat": host[1]}, device_id_type=MESH
            )

    @pl.when(greeted > 0)
    def _():
        pl.semaphore_wait(barrier, greeted)

    for route in routes:

        @pl.when(route.answers)
        def _():
            route.signal(answers.at[route.yonder])

    for route in rows_routes:
        pl.when(route.counts)(route.send)

    own[:, 0:8, :] = jnp.zeros((16, 8, 128), F32)
    own[:, 72:80, :] = jnp.zeros((16, 8, 128), F32)
    zeros = jnp.zeros((128, 128), BF16)
    for ref in (hidden_a, hidden_b):
        ref[0:128, :] = zeros
        ref[1152:1280, :] = zeros

    loads[0].wait()
    loads[1].wait()

    def turn(g):
        turned = own[:, 8 * g + 8 : 8 * g + 16, :].reshape(128, 128).T
        edges[0:8, 128 * g : 128 * g + 128] = turned[120:128]
        edges[8:16, 128 * g : 128 * g + 128] = turned[0:8]
        if g in (0, 7):
            edge_groups[g // 7] = turned

    turn(0)
    turn(7)

    @pl.when(fold)
    def _():
        back = 127 - iota((8, 128), 1)
        up = 7 - iota((8, 128), 0)
        for ch in range(16):
            x = own[ch, 64:72, :]
            x = jnp.take_along_axis(x, back, axis=1)
            x = jnp.take_along_axis(x, up, axis=0)
            fold_rows[ch] = -x if ch < 8 else x
        lane = iota((8, 128), 1)
        rows_back = lane + 7 - 2 * (lane % 8)
        for at in (0, 8):
            x = edges[at : at + 8, 896:1024]
            x = jnp.take_along_axis(x, rows_back, axis=1)
            x = jnp.take_along_axis(x, up, axis=0)
            fold_edges[8 - at : 16 - at, :] = jnp.where(lane < 64, -x, x)

    for route in corner_routes:
        pl.when(route.counts)(route.send)

    loads[2].wait()
    for g in range(1, 7):
        turn(g)

    for route in side_routes:
        pl.when(route.counts)(route.send)

    @pl.when(fold & (mirror_up == t))
    def _():
        corner_nw[5:8, :] = fold_edges[5:8, :]

    @pl.when(fold & (mirror_down == t))
    def _():
        corner_ne[0:3, :] = fold_edges[8:11, :]

    for load in loads[3:]:
        load.wait()
    bands(taps_one, spread, band_one)
    shifted_bands(spread, band_south, 6)
    shifted_bands(spread, band_north, 2)
    bands(taps_two, spread, band_two)
    bands(taps_three, spread, band_three)
    lane_out = iota((1, 128), 1) // 8
    bias_rows = []
    for i, (ref, outs) in enumerate(((b_one, 16), (b_two, 16), (b_three, 8))):
        row = jnp.zeros((1, 128), F32)
        for o in range(outs):
            bias_full[i, 8 * o : 8 * o + 8, :] = jnp.full((8, 128), ref[o], F32)
            row = jnp.where(lane_out == o, ref[o], row)
        bias_rows.append(row)

    for route in routes:

        @pl.when(route.awaits & ~route.far)
        def _():
            pl.semaphore_wait(answers.at[route.here], 1)
            route.send()

    @pl.when(j == seam)
    def _():
        route_e.send()

        @pl.when(t > 0)
        def _():
            route_w.send()

        @pl.when(t == end)
        def _():
            route_ne.send()

    for g in range(8):
        x = own[:, 8 * g + 8 : 8 * g + 16, :].reshape(128, 128)
        hidden_a[128 * g + 128 : 128 * g + 256, :] = x.astype(BF16)

    band_last = jnp.concatenate(
        [band_three[128 * c : 128 * c + 64, :] for c in range(3)], axis=0
    )

    def windows(ref, g):
        return jnp.concatenate(
            [ref[128 * g : 128 * g + 384, :], ref[128 * g + 128 : 128 * g + 512, :]], axis=1
        )

    for src, band, i, dst in (
        (hidden_a, band_one, 0, hidden_b),
        (hidden_b, band_two, 1, hidden_a),
    ):
        for g in range(0, 8, 2):
            y = jnp.dot(band[...], windows(src, g), preferred_element_type=F32)
            for h, v in enumerate(across(y, 128)):
                at = 128 * (g + h) + 128
                dst[at : at + 128, :] = silu(v + bias_full[i]).astype(BF16)

    lane = iota((8, 128), 1)
    row = iota((8, 128), 0)
    for g in range(0, 8, 2):
        y = jnp.dot(band_last, windows(hidden_a, g), preferred_element_type=F32)
        for h, v in enumerate(across(y, 64)):
            inner = (lane >= 3) & (lane < 125)
            if g + h == 0:
                inner = inner & (row >= 3)
            if g + h == 7:
                inner = inner & (row < 5)
            forcing = jnp.where(inner[None], (v + bias_full[2, 0:64, :]).reshape(8, 8, 128), 0.0)
            at = 8 * (g + h)
            x = own[:, at + 8 : at + 16, :]
            qn = own[:, at + 9 : at + 17, :]
            qs = own[:, at + 7 : at + 15, :]
            qe = jnp.where(lane[None] < 127, roll(x, -1, 2), 0.0)
            qw = jnp.where(lane[None] > 0, roll(x, 1, 2), 0.0)
            u = jnp.concatenate([x[0:4]] * 4, axis=0)
            w = jnp.concatenate([x[4:8]] * 4, axis=0)
            tendency = -0.5 * (u * (qe - qw) + w * (qn - qs))
            tendency = tendency + 0.2 * (qe + qw + qn + qs - 4.0 * x)
            tendency = jnp.concatenate([tendency[0:8] + forcing, tendency[8:16]], axis=0)
            ocean = 0.1 * mask[at : at + 8, :].astype(F32)
            out[:, at : at + 8, :] = x + ocean[None] * tendency

    for route in [route_e, route_w, route_sw, route_se, route_nw, route_ne] + fold_routes + rows_routes:

        @pl.when(route.awaits & route.far)
        def _():
            pl.semaphore_wait(answers.at[route.here], 1)
            route.send()

        if route is route_w:

            @pl.when(at_start & (j == seam + 1))
            def _():
                route_sw.send()

    def arrive(dst, slot):
        copy(dst, dst, slot, 0, east, j).wait_recv()

    def arrive_west():
        arrive(west_cols.at[5:8, :], HW)

    def arrive_south():
        arrive(south.at[:, 5:8, :], HS)

    def arrive_north():
        arrive(north.at[:, 0:3, :], HN)

    def arrive_sw():
        arrive(corner_sw.at[5:8, :], SW)

    via_west = at_end & ((j == 0) | (j == seam - 1) | (j == seam))
    via_sw = at_end & (j == 1)
    via_south = at_start & (j == seam)
    via_north = at_first

    @pl.when(via_west)
    def _():
        arrive_west()

        @pl.when(j == 0)
        def _():
            route_e.send()

        @pl.when(j == seam - 1)
        def _():
            route_n.send()
            route_ne.send()

        @pl.when(j == seam)
        def _():
            route_s.send()
            route_sw.send()

    @pl.when(via_sw)
    def _():
        arrive_sw()
        route_se.send()

    @pl.when(via_south)
    def _():
        arrive_south()
        route_w.send()
        route_sw.send()

    @pl.when(via_north)
    def _():
        arrive_north()
        route_w.send()
        route_nw.send()

    def sideways():
        pl.when(~via_west)(arrive_west)
        arrive(east_cols.at[0:3, :], HE)

    def southern():
        @pl.when(below)
        def _():
            pl.when(~via_south)(arrive_south)
            pl.when(~via_sw)(arrive_sw)
            arrive(corner_se.at[0:3, :], SE)

    def northern():
        pl.when(~via_north)(arrive_north)

        @pl.when(above | (mirror_up != t))
        def _():
            arrive(corner_nw.at[5:8, :], NW)

        @pl.when(above | (mirror_down != t))
        def _():
            arrive(corner_ne.at[0:3, :], NE)

    place = iota((8, 128), 0)
    lane = iota((8, 128), 1)
    inner = (lane >= 3) & (lane < 125)

    def taps_on(x, band):
        return lax.dot_general(x, band, (((1,), (1,)), ((), ())), preferred_element_type=F32)

    def columns():
        none = jnp.zeros((32, 128), BF16)

        def layer(h, band, i):
            h = [none] + h + [none]
            lhs = jnp.concatenate(
                [jnp.concatenate(h[g : g + 3], axis=1) for g in range(8)], axis=0
            )
            return down(taps_on(lhs, band[...]), 8) + bias_rows[i][None]

        h = []
        for g in range(8):
            at = pl.ds(128 * g, 128)
            parts = [west_cols[:, at], edges[8:16, at], edges[0:8, at], east_cols[:, at]]
            h.append(jnp.concatenate(parts, axis=0).astype(BF16))
        for band, i in ((band_one, 0), (band_two, 1)):
            y = silu(layer(h, band, i)).astype(BF16)
            h = [y[g] for g in range(8)]
        f = layer(h, band_three, 2)

        def speed(x):
            x = jnp.where(lane < 32, x, 0.0)
            x = x + roll(x, 32, 1)
            return x + roll(x, 64, 1)

        parts = []
        for g in range(8):
            at = pl.ds(128 * g, 128)
            fe, fw = f[g, 16:24], f[g, 8:16]
            if g in (0, 7):
                kept = lane % 8 >= 3 if g == 0 else lane % 8 < 5
                fe, fw = jnp.where(kept, fe, 0.0), jnp.where(kept, fw, 0.0)
            e, w = speed(edges[0:8, at]), speed(edges[8:16, at])
            e = jnp.where(place == 7, (0.2 - 0.5 * e) * roll(east_cols[:, at], -1, 0), 0.0)
            w = jnp.where(place == 0, (0.2 + 0.5 * w) * roll(west_cols[:, at], 1, 0), 0.0)
            parts += [fe + e, fw + w]
        turned = jnp.concatenate(parts, axis=0).T
        for g in range(8):
            patch = roll(turned, 120 - 16 * g, 1).reshape(16, 8, 128)
            add(g, jnp.where(inner[None], 0.0, patch))

    def add(g, patch):
        at = 8 * g
        ocean = 0.1 * mask[at : at + 8, :].astype(F32)
        out[:, at : at + 8, :] = out[:, at : at + 8, :] + ocean[None] * patch

    def edge(side):
        if side == "south":
            g, at, shift, band = 0, pl.ds(0, 128), -2, band_south
            rows = jnp.where(((place >= 5) & below)[None], south[...], 0.0)
            ends = [jnp.where(below, x[...], 0.0) for x in (corner_sw, corner_se)]
            outer, next_to, step, sign = place < 3, place == 0, 1, 0.5
        else:
            g, at, shift, band = 7, pl.ds(896, 128), 2, band_north
            rows = jnp.where((place < 3)[None], north[...], 0.0)
            ends = [corner_nw[...], corner_ne[...]]
            outer, next_to, step, sign = place >= 5, place == 7, -1, -0.5
        beyond = jnp.concatenate([ends[0], rows.reshape(128, 128).T, ends[1]], axis=0)
        here = jnp.concatenate([west_cols[:, at], edge_groups[g // 7], east_cols[:, at]], axis=0)
        pair = [beyond, here] if side == "south" else [here, beyond]
        h = jnp.concatenate(pair, axis=1).astype(BF16)
        for taps, i in (
            (band[...], 0),
            (band_two[:, 128:256], 1),
            (band_three[:, 128:256], 2),
        ):
            y = taps_on(h, taps)
            y = roll(y[:, 0:128], 1, 0) + y[:, 128:256] + roll(y[:, 256:384], -1, 0) + bias_rows[i]
            h = silu(y).astype(BF16)
        forcing = roll(y[8:136].T[0:64].reshape(8, 8, 128), shift, 1)
        forcing = jnp.where(outer[None], forcing, 0.0)
        x = own[:, 8 * g + 8 : 8 * g + 16, :]
        v = jnp.concatenate([x[4:8]] * 4, axis=0)
        near = jnp.where(next_to[None], (0.2 + sign * v) * roll(rows, step, 1), 0.0)
        add(g, jnp.concatenate([near[0:8] + forcing, near[8:16]], axis=0))

    @pl.when(t == 0)
    def _():
        sideways()
        southern()
        northern()
        columns()
        edge("south")
        edge("north")

    @pl.when((t > 0) & (j == seam))
    def _():
        sideways()
        northern()
        columns()
        edge("north")
        southern()
        edge("south")

    @pl.when((t > 0) & (j != seam))
    def _():
        sideways()
        southern()
        columns()
        edge("south")
        northern()
        edge("north")

    for route in routes:

        @pl.when(route.there)
        def _():
            for c in route.copies:
                c.wait_send()


def solution(mesh):
    lon_count, lat_count = mesh.shape["lon"], mesh.shape["lat"]

    def step(*args):
        state, *rest = [pltpu.with_memory_space_constraint(x, pltpu.HBM) for x in args]
        return pl.pallas_call(
            functools.partial(kernel, lon_count, lat_count),
            out_shape=jax.ShapeDtypeStruct(state.shape, F32),
            in_specs=[pl.BlockSpec(memory_space=pltpu.HBM)] * 8,
            out_specs=pl.BlockSpec(memory_space=pltpu.VMEM),
            scratch_shapes=[
                pltpu.VMEM((16, 80, 128), F32),
                pltpu.VMEM((64, 128), jnp.int32),
                pltpu.VMEM((3, 3, 16, 16), BF16),
                pltpu.VMEM((3, 3, 16, 16), BF16),
                pltpu.VMEM((3, 3, 8, 16), BF16),
                pltpu.SMEM((16,), F32),
                pltpu.SMEM((16,), F32),
                pltpu.SMEM((8,), F32),
                pltpu.VMEM((16, 8, 128), F32),
                pltpu.VMEM((16, 8, 128), F32),
                pltpu.VMEM((16, 1024), F32),
                pltpu.VMEM((8, 1024), F32),
                pltpu.VMEM((8, 1024), F32),
                pltpu.VMEM((8, 128), F32),
                pltpu.VMEM((8, 128), F32),
                pltpu.VMEM((8, 128), F32),
                pltpu.VMEM((8, 128), F32),
                pltpu.VMEM((16, 8, 128), F32),
                pltpu.VMEM((16, 128), F32),
                pltpu.VMEM((144, 128), F32),
                pltpu.VMEM((384, 384), BF16),
                pltpu.VMEM((384, 384), BF16),
                pltpu.VMEM((384, 384), BF16),
                pltpu.VMEM((384, 256), BF16),
                pltpu.VMEM((384, 256), BF16),
                pltpu.VMEM((2, 128, 128), F32),
                pltpu.VMEM((3, 128, 128), F32),
                pltpu.VMEM((1280, 128), BF16),
                pltpu.VMEM((1280, 128), BF16),
                pltpu.SemaphoreType.DMA((10,)),
                pltpu.SemaphoreType.DMA((10,)),
                pltpu.SemaphoreType.DMA((10,)),
                pltpu.SemaphoreType.REGULAR((8,)),
            ],
            compiler_params=pltpu.CompilerParams(
                collective_id=0, has_side_effects=True, vmem_limit_bytes=32 * 1024 * 1024
            ),
        )(state, *rest)

    return jax.shard_map(
        step,
        mesh=mesh,
        in_specs=(P(None, "lat", "lon"), P("lat", "lon"), P(), P(), P(), P(), P(), P()),
        out_specs=P(None, "lat", "lon"),
        check_vma=False,
    )
```

```python
import functools

import jax
import jax.numpy as jnp
from jax import lax
from jax.experimental import pallas as pl
from jax.experimental.pallas import tpu as pltpu
from jax.sharding import PartitionSpec as P

MESH = pl.DeviceIdType.MESH
F32, BF16 = jnp.float32, jnp.bfloat16
HW, HE, HS, HN, SW, SE, NW, NE = range(8)


def iota(shape, dim):
    return lax.broadcasted_iota(jnp.int32, shape, dim)


def silu(v):
    half = 0.5 * v
    return half + half * jnp.tanh(half)


def roll(x, shift, axis):
    return pltpu.roll(x, shift % x.shape[axis], axis)


def spread_taps(taps, spread):
    outs = taps.shape[2]
    spreading = (iota((16, 128), 0) == iota((16, 128), 1) // 8).astype(BF16)
    flat = taps[...].reshape(9 * outs, 16)
    spread[0 : 9 * outs, :] = jnp.dot(flat, spreading, preferred_element_type=F32)


def tap_rows(spread, outs, c, o):
    at = [(a * 3 + c) * outs + o for a in range(3)]
    return [jnp.broadcast_to(spread[i : i + 1, :], (8, 128)) for i in at]


def shifted_bands(spread, band, shift):
    ahead = iota((8, 128), 1) % 8 - iota((8, 128), 0)
    for c in range(3):
        for pair in range(8):
            parts = []
            for o in (2 * pair, 2 * pair + 1):
                tap = tap_rows(spread, 16, c, o)
                groups = []
                for g in range(2):
                    part = jnp.zeros((8, 128), F32)
                    for a in range(3):
                        part = jnp.where(ahead == shift + a - 1 - 8 * g, tap[a], part)
                    groups.append(part)
                parts.append(jnp.concatenate(groups, axis=1))
            at = c * 128 + pair * 16
            band[at : at + 16, :] = jnp.concatenate(parts, axis=0).astype(BF16)


def bands(taps, spread, band):
    outs = taps.shape[2]
    spread_taps(taps, spread)
    ahead = iota((8, 128), 1) % 8 - iota((8, 128), 0)
    for c in range(3):
        for pair in range(8):
            parts = []
            for o in (2 * pair, 2 * pair + 1):
                if o >= outs:
                    parts.append(jnp.zeros((8, 384), F32))
                    continue
                tap = tap_rows(spread, outs, c, o)
                before = jnp.where(ahead == 7, tap[0], 0.0)
                centre = jnp.where(
                    ahead == -1,
                    tap[0],
                    jnp.where(ahead == 0, tap[1], jnp.where(ahead == 1, tap[2], 0.0)),
                )
                after = jnp.where(ahead == -7, tap[2], 0.0)
                parts.append(jnp.concatenate([before, centre, after], axis=1))
            at = c * 128 + pair * 16
            band[at : at + 16, :] = jnp.concatenate(parts, axis=0).astype(BF16)


def across(y, outs):
    parts = []
    for at in range(0, y.shape[1], 128):
        z = y[:, at : at + 128]
        parts.append(
            roll(z[0:outs], 1, 1) + z[outs : 2 * outs] + roll(z[2 * outs : 3 * outs], -1, 1)
        )
    return parts


def down(y, groups):
    z = [y[:, 128 * c : 128 * c + 128].reshape(groups, 32, 128) for c in range(3)]
    return roll(z[0], 1, 1) + z[1] + roll(z[2], -1, 1)


def kernel(
    lon_count,
    lat_count,
    state,
    land_mask,
    kernel_one,
    bias_one,
    kernel_two,
    bias_two,
    kernel_three,
    bias_three,
    out,
    own,
    mask,
    taps_one,
    taps_two,
    taps_three,
    b_one,
    b_two,
    b_three,
    south,
    north,
    edges,
    west_cols,
    east_cols,
    corner_sw,
    corner_se,
    corner_nw,
    corner_ne,
    fold_rows,
    fold_edges,
    spread,
    band_one,
    band_two,
    band_three,
    band_south,
    band_north,
    edge_groups,
    bias_full,
    hidden_a,
    hidden_b,
    in_sems,
    send_sems,
    recv_sems,
    answers,
):
    t, j = lax.axis_index("lon"), lax.axis_index("lat")
    top = lat_count - 1
    east, west = lax.rem(t + 1, lon_count), lax.rem(t + lon_count - 1, lon_count)
    mirror = lon_count - 1 - t
    mirror_up = lax.rem(mirror + 1, lon_count)
    mirror_down = lax.rem(mirror + lon_count - 1, lon_count)

    loads = [
        pltpu.make_async_copy(src, dst, in_sems.at[i])
        for i, (src, dst) in enumerate(
            [
                (state.at[:, 0:8, :], own.at[:, 8:16, :]),
                (state.at[:, 56:64, :], own.at[:, 64:72, :]),
                (state.at[:, 8:56, :], own.at[:, 16:64, :]),
                (land_mask, mask),
                (kernel_one, taps_one),
                (kernel_two, taps_two),
                (kernel_three, taps_three),
                (bias_one, b_one),
                (bias_two, b_two),
                (bias_three, b_three),
            ]
        )
    ]
    for load in loads:
        load.start()

    def rank(lon, lat):
        z, y, x, core = (lat >> 2) * 6 + (lon >> 4), (lon & 15) >> 1, lat & 3, lon & 1
        guess = jnp.where(z < 6, 128 + 150 * z, 940 + 30 * z) + 45 * x - 41 * core
        guess = guess + jnp.where(y < 4, 57 * y, 430 - 35 * y)
        guess = jnp.where(lon + lat == 0, 1050, guess)
        return guess * 1024 + lat * lon_count + lon

    mine = rank(t, j)
    first, last = pl.ds(0, 128), pl.ds(896, 128)

    def copy(src, dst, slot, sender, lon, lat):
        return pltpu.make_async_remote_copy(
            src_ref=src,
            dst_ref=dst,
            send_sem=send_sems.at[sender],
            recv_sem=recv_sems.at[slot],
            device_id={"lon": lon, "lat": lat},
            device_id_type=MESH,
        )

    class Route:
        def __init__(self, there, lon, lat, here, yonder, *copies, step=0, quiet=False):
            self.there, self.lon, self.lat, self.here, self.yonder = there, lon, lat, here, yonder
            theirs = rank(lon, lat)
            ahead = mine < theirs
            level = jnp.abs(theirs - mine) < 300 * 1024
            if here == yonder:
                both = level
            else:
                inside = (lon > 0) & (t > 0) & (lon < lon_count - 1) & (t < lon_count - 1)
                crossing = (j == seam) if step == -1 else (j == seam - 1) if step == 1 else False
                both = level & inside & crossing
            if step == 1:
                ahead = ahead | (j == seam)
            if step == -1:
                ahead = ahead & (j != seam + 1)
            if (here, yonder) == (5, 6):
                ahead = ahead | ((t == lon_count - 1) & (j == seam))
            if (here, yonder) == (6, 5):
                ahead = ahead & ~((t == lon_count - 2) & (j == seam - 1))
            loud = there & ~jnp.bool_(quiet)
            self.greets = loud & (both | ahead)
            self.counts = loud & (both | ~ahead)
            self.answers = loud & ~both & ~ahead
            self.awaits = loud & ~both & ahead
            wraps = (lon - t > 1) | (t - lon > 1)
            self.far = (theirs - mine > 250 * 1024) | (wraps & (here != yonder))
            if (here, yonder) == (1, 0):
                self.far = self.far | ((t == lon_count - 1) & (j == seam - 1))
            if (here, yonder) == (5, 6):
                self.awaits = self.awaits & ~((t == lon_count - 1) & (j == seam))
            if (here, yonder) == (6, 5):
                self.answers = self.answers & ~((t == lon_count - 2) & (j == seam - 1))
            self.copies = [copy(*c, lon, lat) for c in copies]

        def signal(self, sem):
            pl.semaphore_signal(
                sem, inc=1, device_id={"lon": self.lon, "lat": self.lat}, device_id_type=MESH
            )

        def send(self):
            for c in self.copies:
                c.start()

    below, above, fold = j > 0, j < top, j == top
    seam = lat_count // 2 if lat_count > 3 and lon_count > 3 else 2 * lat_count
    end = lon_count - 1
    corner = seam < lat_count
    at_first = (t == 0) & (j == 0) & corner
    at_end, at_start = (t == end) & corner, (t == 0) & corner
    e_cols, w_cols = pl.ds(5, 3), pl.ds(8, 3)
    route_s = Route(
        below, t, j - 1, 2, 3, (state.at[:, 0:3, :], north.at[:, 0:3, :], HN, 2),
        step=-1, quiet=at_end & (j == seam),
    )
    route_n = Route(
        above, t, j + 1, 3, 2, (state.at[:, 61:64, :], south.at[:, 5:8, :], HS, 6),
        step=1, quiet=at_end & (j == seam - 1),
    )
    route_se = Route(
        below, east, j - 1, 4, 7, (edges.at[e_cols, first], corner_nw.at[5:8, :], NW, 4),
        step=-1, quiet=at_end & (j == 1),
    )
    route_sw = Route(
        below, west, j - 1, 5, 6, (edges.at[w_cols, first], corner_ne.at[0:3, :], NE, 5),
        step=-1, quiet=at_start & (j == seam + 1),
    )
    route_ne = Route(
        above, east, j + 1, 6, 5, (edges.at[e_cols, last], corner_sw.at[5:8, :], SW, 8),
        step=1, quiet=at_end & (j == seam),
    )
    route_nw = Route(
        above, west, j + 1, 7, 4, (edges.at[w_cols, last], corner_se.at[0:3, :], SE, 9),
        step=1, quiet=at_first,
    )
    fold_routes = [
        Route(fold, mirror, j, 3, 3, (fold_rows.at[:, 0:3, :], north.at[:, 0:3, :], HN, 6)),
        Route(
            fold & (mirror_down != t), mirror_down, j, 6, 6,
            (fold_edges.at[8:11, :], corner_ne.at[0:3, :], NE, 9),
        ),
        Route(
            fold & (mirror_up != t), mirror_up, j, 7, 7,
            (fold_edges.at[5:8, :], corner_nw.at[5:8, :], NW, 8),
        ),
    ]
    route_e = Route(
        j >= 0, east, j, 0, 1, (edges.at[e_cols, :], west_cols.at[5:8, :], HW, 0),
        quiet=(j == seam) | (at_end & (j == 0)),
    )
    route_w = Route(
        j >= 0, west, j, 1, 0, (edges.at[w_cols, :], east_cols.at[0:3, :], HE, 1),
        quiet=(j == seam) | at_first,
    )
    rows_routes = [route_s, route_n]
    corner_routes = [route_se, route_sw, route_ne, route_nw] + fold_routes
    side_routes = [route_e, route_w]
    routes = rows_routes + corner_routes + side_routes

    barrier = pltpu.get_barrier_semaphore()
    greeted = jnp.int32(0)
    for route in routes:
        greeted = greeted + route.counts.astype(jnp.int32)

        @pl.when(route.greets)
        def _():
            route.signal(barrier)

    for host, guest in (((end - 1, 0), (0, 0)),):
        greeted = greeted + ((t == host[0]) & (j == host[1]) & corner).astype(jnp.int32)

        @pl.when((t == guest[0]) & (j == guest[1]) & corner)
        def _():
            pl.semaphore_signal(
                barrier, inc=1, device_id={"lon": host[0], "lat": host[1]}, device_id_type=MESH
            )

    @pl.when(greeted > 0)
    def _():
        pl.semaphore_wait(barrier, greeted)

    for route in routes:

        @pl.when(route.answers)
        def _():
            route.signal(answers.at[route.yonder])

    for route in rows_routes:
        pl.when(route.counts)(route.send)

    own[:, 0:8, :] = jnp.zeros((16, 8, 128), F32)
    own[:, 72:80, :] = jnp.zeros((16, 8, 128), F32)
    zeros = jnp.zeros((128, 128), BF16)
    for ref in (hidden_a, hidden_b):
        ref[0:128, :] = zeros
        ref[1152:1280, :] = zeros

    loads[0].wait()

    def turn(g):
        turned = own[:, 8 * g + 8 : 8 * g + 16, :].reshape(128, 128).T
        edges[0:8, 128 * g : 128 * g + 128] = turned[120:128]
        edges[8:16, 128 * g : 128 * g + 128] = turned[0:8]
        if g in (0, 7):
            edge_groups[g // 7] = turned

    turn(0)
    for route in corner_routes[0:2]:
        pl.when(route.counts)(route.send)

    loads[1].wait()
    turn(7)

    @pl.when(fold)
    def _():
        back = 127 - iota((8, 128), 1)
        up = 7 - iota((8, 128), 0)
        for ch in range(16):
            x = own[ch, 64:72, :]
            x = jnp.take_along_axis(x, back, axis=1)
            x = jnp.take_along_axis(x, up, axis=0)
            fold_rows[ch] = -x if ch < 8 else x
        lane = iota((8, 128), 1)
        rows_back = lane + 7 - 2 * (lane % 8)
        for at in (0, 8):
            x = edges[at : at + 8, 896:1024]
            x = jnp.take_along_axis(x, rows_back, axis=1)
            x = jnp.take_along_axis(x, up, axis=0)
            fold_edges[8 - at : 16 - at, :] = jnp.where(lane < 64, -x, x)

    for route in corner_routes[2:]:
        pl.when(route.counts)(route.send)

    loads[2].wait()
    for g in range(1, 7):
        turn(g)

    for route in side_routes:
        pl.when(route.counts)(route.send)

    @pl.when(fold & (mirror_up == t))
    def _():
        corner_nw[5:8, :] = fold_edges[5:8, :]

    @pl.when(fold & (mirror_down == t))
    def _():
        corner_ne[0:3, :] = fold_edges[8:11, :]

    for load in loads[3:]:
        load.wait()
    bands(taps_one, spread, band_one)
    shifted_bands(spread, band_south, 6)
    shifted_bands(spread, band_north, 2)
    bands(taps_two, spread, band_two)
    bands(taps_three, spread, band_three)
    lane_out = iota((1, 128), 1) // 8
    bias_rows = []
    for i, (ref, outs) in enumerate(((b_one, 16), (b_two, 16), (b_three, 8))):
        row = jnp.zeros((1, 128), F32)
        for o in range(outs):
            bias_full[i, 8 * o : 8 * o + 8, :] = jnp.full((8, 128), ref[o], F32)
            row = jnp.where(lane_out == o, ref[o], row)
        bias_rows.append(row)

    for route in routes:

        @pl.when(route.awaits & ~route.far)
        def _():
            pl.semaphore_wait(answers.at[route.here], 1)
            route.send()

    @pl.when(j == seam)
    def _():
        route_e.send()

        @pl.when(t > 0)
        def _():
            route_w.send()

        @pl.when(t == end)
        def _():
            route_ne.send()

    for g in range(8):
        x = own[:, 8 * g + 8 : 8 * g + 16, :].reshape(128, 128)
        hidden_a[128 * g + 128 : 128 * g + 256, :] = x.astype(BF16)

    band_last = jnp.concatenate(
        [band_three[128 * c : 128 * c + 64, :] for c in range(3)], axis=0
    )

    def windows(ref, g):
        return jnp.concatenate(
            [ref[128 * g : 128 * g + 384, :], ref[128 * g + 128 : 128 * g + 512, :]], axis=1
        )

    for src, band, i, dst in (
        (hidden_a, band_one, 0, hidden_b),
        (hidden_b, band_two, 1, hidden_a),
    ):
        for g in range(0, 8, 2):
            y = jnp.dot(band[...], windows(src, g), preferred_element_type=F32)
            for h, v in enumerate(across(y, 128)):
                at = 128 * (g + h) + 128
                dst[at : at + 128, :] = silu(v + bias_full[i]).astype(BF16)

    lane = iota((8, 128), 1)
    row = iota((8, 128), 0)
    for g in range(0, 8, 2):
        y = jnp.dot(band_last, windows(hidden_a, g), preferred_element_type=F32)
        for h, v in enumerate(across(y, 64)):
            inner = (lane >= 3) & (lane < 125)
            if g + h == 0:
                inner = inner & (row >= 3)
            if g + h == 7:
                inner = inner & (row < 5)
            forcing = jnp.where(inner[None], (v + bias_full[2, 0:64, :]).reshape(8, 8, 128), 0.0)
            at = 8 * (g + h)
            x = own[:, at + 8 : at + 16, :]
            qn = own[:, at + 9 : at + 17, :]
            qs = own[:, at + 7 : at + 15, :]
            qe = jnp.where(lane[None] < 127, roll(x, -1, 2), 0.0)
            qw = jnp.where(lane[None] > 0, roll(x, 1, 2), 0.0)
            u = jnp.concatenate([x[0:4]] * 4, axis=0)
            w = jnp.concatenate([x[4:8]] * 4, axis=0)
            tendency = -0.5 * (u * (qe - qw) + w * (qn - qs))
            tendency = tendency + 0.2 * (qe + qw + qn + qs - 4.0 * x)
            tendency = jnp.concatenate([tendency[0:8] + forcing, tendency[8:16]], axis=0)
            ocean = 0.1 * mask[at : at + 8, :].astype(F32)
            out[:, at : at + 8, :] = x + ocean[None] * tendency

    def arrive(dst, slot):
        copy(dst, dst, slot, 0, east, j).wait_recv()

    def arrive_west():
        arrive(west_cols.at[5:8, :], HW)

    def arrive_south():
        arrive(south.at[:, 5:8, :], HS)

    def arrive_north():
        arrive(north.at[:, 0:3, :], HN)

    def arrive_sw():
        arrive(corner_sw.at[5:8, :], SW)

    via_west = at_end & ((j == 0) | (j == seam - 1) | (j == seam))
    via_sw = at_end & (j == 1)
    via_south = at_start & (j == seam)
    via_north = at_first

    @pl.when(via_west)
    def _():
        arrive_west()

        @pl.when(j == 0)
        def _():
            route_e.send()

        @pl.when(j == seam - 1)
        def _():
            route_n.send()

        @pl.when(j == seam)
        def _():
            route_s.send()
            route_sw.send()

    @pl.when(via_sw)
    def _():
        arrive_sw()
        route_se.send()

    for route in [route_e, route_w, route_sw, route_se, route_nw, route_ne] + fold_routes + rows_routes:

        @pl.when(route.awaits & route.far)
        def _():
            pl.semaphore_wait(answers.at[route.here], 1)
            route.send()

        if route is route_w:

            @pl.when(at_start & (j == seam + 1))
            def _():
                route_sw.send()

    @pl.when(via_south)
    def _():
        arrive_south()
        route_w.send()

    @pl.when(via_north)
    def _():
        arrive_north()
        route_w.send()
        route_nw.send()

    place = iota((8, 128), 0)
    lane = iota((8, 128), 1)
    inner = (lane >= 3) & (lane < 125)

    def sideways():
        pl.when(~via_west)(arrive_west)
        arrive(east_cols.at[0:3, :], HE)

    def southern():
        @pl.when(below)
        def _():
            pl.when(~via_south)(arrive_south)
            pl.when(~via_sw)(arrive_sw)
            arrive(corner_se.at[0:3, :], SE)

    def northern():
        pl.when(~via_north)(arrive_north)

        @pl.when(above | (mirror_up != t))
        def _():
            arrive(corner_nw.at[5:8, :], NW)

        @pl.when(above | (mirror_down != t))
        def _():
            arrive(corner_ne.at[0:3, :], NE)


    def taps_on(x, band):
        return lax.dot_general(x, band, (((1,), (1,)), ((), ())), preferred_element_type=F32)

    def columns():
        none = jnp.zeros((32, 128), BF16)

        def layer(h, band, i):
            h = [none] + h + [none]
            lhs = jnp.concatenate(
                [jnp.concatenate(h[g : g + 3], axis=1) for g in range(8)], axis=0
            )
            return down(taps_on(lhs, band[...]), 8) + bias_rows[i][None]

        h = []
        for g in range(8):
            at = pl.ds(128 * g, 128)
            parts = [west_cols[:, at], edges[8:16, at], edges[0:8, at], east_cols[:, at]]
            h.append(jnp.concatenate(parts, axis=0).astype(BF16))
        for band, i in ((band_one, 0), (band_two, 1)):
            y = silu(layer(h, band, i)).astype(BF16)
            h = [y[g] for g in range(8)]
            yield
        f = layer(h, band_three, 2)
        yield

        def speed(x):
            x = jnp.where(lane < 32, x, 0.0)
            x = x + roll(x, 32, 1)
            return x + roll(x, 64, 1)

        parts = []
        for g in range(8):
            at = pl.ds(128 * g, 128)
            fe, fw = f[g, 16:24], f[g, 8:16]
            if g in (0, 7):
                kept = lane % 8 >= 3 if g == 0 else lane % 8 < 5
                fe, fw = jnp.where(kept, fe, 0.0), jnp.where(kept, fw, 0.0)
            e, w = speed(edges[0:8, at]), speed(edges[8:16, at])
            e = jnp.where(place == 7, (0.2 - 0.5 * e) * roll(east_cols[:, at], -1, 0), 0.0)
            w = jnp.where(place == 0, (0.2 + 0.5 * w) * roll(west_cols[:, at], 1, 0), 0.0)
            parts += [fe + e, fw + w]
        turned = jnp.concatenate(parts, axis=0).T
        for g in range(8):
            patch = roll(turned, 120 - 16 * g, 1).reshape(16, 8, 128)
            add(g, jnp.where(inner[None], 0.0, patch))

    def add(g, patch):
        at = 8 * g
        ocean = 0.1 * mask[at : at + 8, :].astype(F32)
        out[:, at : at + 8, :] = out[:, at : at + 8, :] + ocean[None] * patch

    def edge(side):
        if side == "south":
            g, at, shift, band = 0, pl.ds(0, 128), -2, band_south
            rows = jnp.where(((place >= 5) & below)[None], south[...], 0.0)
            ends = [jnp.where(below, x[...], 0.0) for x in (corner_sw, corner_se)]
            outer, next_to, step, sign = place < 3, place == 0, 1, 0.5
        else:
            g, at, shift, band = 7, pl.ds(896, 128), 2, band_north
            rows = jnp.where((place < 3)[None], north[...], 0.0)
            ends = [corner_nw[...], corner_ne[...]]
            outer, next_to, step, sign = place >= 5, place == 7, -1, -0.5
        beyond = jnp.concatenate([ends[0], rows.reshape(128, 128).T, ends[1]], axis=0)
        here = jnp.concatenate([west_cols[:, at], edge_groups[g // 7], east_cols[:, at]], axis=0)
        pair = [beyond, here] if side == "south" else [here, beyond]
        h = jnp.concatenate(pair, axis=1).astype(BF16)
        for taps, i in (
            (band[...], 0),
            (band_two[:, 128:256], 1),
            (band_three[:, 128:256], 2),
        ):
            y = taps_on(h, taps)
            y = roll(y[:, 0:128], 1, 0) + y[:, 128:256] + roll(y[:, 256:384], -1, 0) + bias_rows[i]
            h = silu(y).astype(BF16)
            yield
        forcing = roll(y[8:136].T[0:64].reshape(8, 8, 128), shift, 1)
        forcing = jnp.where(outer[None], forcing, 0.0)
        x = own[:, 8 * g + 8 : 8 * g + 16, :]
        v = jnp.concatenate([x[4:8]] * 4, axis=0)
        near = jnp.where(next_to[None], (0.2 + sign * v) * roll(rows, step, 1), 0.0)
        add(g, jnp.concatenate([near[0:8] + forcing, near[8:16]], axis=0))

    def together(*pieces):
        pieces = list(pieces)
        while pieces:
            pieces = [p for p in pieces if next(p, pieces) is not pieces]

    @pl.when(t == 0)
    def _():
        sideways()
        southern()
        northern()
        together(edge("south"), edge("north"), columns())

    @pl.when((t > 0) & (j == seam))
    def _():
        sideways()
        northern()
        together(edge("north"), columns())
        southern()
        together(edge("south"))

    @pl.when((t > 0) & (j != seam))
    def _():
        sideways()
        southern()
        together(edge("south"), columns())
        northern()
        together(edge("north"))

    for route in routes:

        @pl.when(route.there)
        def _():
            for c in route.copies:
                c.wait_send()


def solution(mesh):
    lon_count, lat_count = mesh.shape["lon"], mesh.shape["lat"]

    def step(*args):
        state, *rest = [pltpu.with_memory_space_constraint(x, pltpu.HBM) for x in args]
        return pl.pallas_call(
            functools.partial(kernel, lon_count, lat_count),
            out_shape=jax.ShapeDtypeStruct(state.shape, F32),
            in_specs=[pl.BlockSpec(memory_space=pltpu.HBM)] * 8,
            out_specs=pl.BlockSpec(memory_space=pltpu.VMEM),
            scratch_shapes=[
                pltpu.VMEM((16, 80, 128), F32),
                pltpu.VMEM((64, 128), jnp.int32),
                pltpu.VMEM((3, 3, 16, 16), BF16),
                pltpu.VMEM((3, 3, 16, 16), BF16),
                pltpu.VMEM((3, 3, 8, 16), BF16),
                pltpu.SMEM((16,), F32),
                pltpu.SMEM((16,), F32),
                pltpu.SMEM((8,), F32),
                pltpu.VMEM((16, 8, 128), F32),
                pltpu.VMEM((16, 8, 128), F32),
                pltpu.VMEM((16, 1024), F32),
                pltpu.VMEM((8, 1024), F32),
                pltpu.VMEM((8, 1024), F32),
                pltpu.VMEM((8, 128), F32),
                pltpu.VMEM((8, 128), F32),
                pltpu.VMEM((8, 128), F32),
                pltpu.VMEM((8, 128), F32),
                pltpu.VMEM((16, 8, 128), F32),
                pltpu.VMEM((16, 128), F32),
                pltpu.VMEM((144, 128), F32),
                pltpu.VMEM((384, 384), BF16),
                pltpu.VMEM((384, 384), BF16),
                pltpu.VMEM((384, 384), BF16),
                pltpu.VMEM((384, 256), BF16),
                pltpu.VMEM((384, 256), BF16),
                pltpu.VMEM((2, 128, 128), F32),
                pltpu.VMEM((3, 128, 128), F32),
                pltpu.VMEM((1280, 128), BF16),
                pltpu.VMEM((1280, 128), BF16),
                pltpu.SemaphoreType.DMA((10,)),
                pltpu.SemaphoreType.DMA((10,)),
                pltpu.SemaphoreType.DMA((10,)),
                pltpu.SemaphoreType.REGULAR((8,)),
            ],
            compiler_params=pltpu.CompilerParams(
                collective_id=0, has_side_effects=True, vmem_limit_bytes=32 * 1024 * 1024
            ),
        )(state, *rest)

    return jax.shard_map(
        step,
        mesh=mesh,
        in_specs=(P(None, "lat", "lon"), P("lat", "lon"), P(), P(), P(), P(), P(), P()),
        out_specs=P(None, "lat", "lon"),
        check_vma=False,
    )
```

```python
import functools

import jax
import jax.numpy as jnp
from jax import lax
from jax.experimental import pallas as pl
from jax.experimental.pallas import tpu as pltpu
from jax.sharding import PartitionSpec as P

MESH = pl.DeviceIdType.MESH
F32, BF16 = jnp.float32, jnp.bfloat16
HW, HE, HS, HN, SW, SE, NW, NE = range(8)


def iota(shape, dim):
    return lax.broadcasted_iota(jnp.int32, shape, dim)


def silu(v):
    half = 0.5 * v
    return half + half * jnp.tanh(half)


def roll(x, shift, axis):
    return pltpu.roll(x, shift % x.shape[axis], axis)


def spread_taps(taps, spread):
    outs = taps.shape[2]
    spreading = (iota((16, 128), 0) == iota((16, 128), 1) // 8).astype(BF16)
    flat = taps[...].reshape(9 * outs, 16)
    spread[0 : 9 * outs, :] = jnp.dot(flat, spreading, preferred_element_type=F32)


def tap_rows(spread, outs, c, o):
    at = [(a * 3 + c) * outs + o for a in range(3)]
    return [jnp.broadcast_to(spread[i : i + 1, :], (8, 128)) for i in at]


def shifted_bands(spread, band, shift):
    ahead = iota((8, 128), 1) % 8 - iota((8, 128), 0)
    for c in range(3):
        for pair in range(8):
            parts = []
            for o in (2 * pair, 2 * pair + 1):
                tap = tap_rows(spread, 16, c, o)
                groups = []
                for g in range(2):
                    part = jnp.zeros((8, 128), F32)
                    for a in range(3):
                        part = jnp.where(ahead == shift + a - 1 - 8 * g, tap[a], part)
                    groups.append(part)
                parts.append(jnp.concatenate(groups, axis=1))
            at = c * 128 + pair * 16
            band[at : at + 16, :] = jnp.concatenate(parts, axis=0).astype(BF16)


def bands(taps, spread, band):
    outs = taps.shape[2]
    spread_taps(taps, spread)
    ahead = iota((8, 128), 1) % 8 - iota((8, 128), 0)
    for c in range(3):
        for pair in range(8):
            parts = []
            for o in (2 * pair, 2 * pair + 1):
                if o >= outs:
                    parts.append(jnp.zeros((8, 384), F32))
                    continue
                tap = tap_rows(spread, outs, c, o)
                before = jnp.where(ahead == 7, tap[0], 0.0)
                centre = jnp.where(
                    ahead == -1,
                    tap[0],
                    jnp.where(ahead == 0, tap[1], jnp.where(ahead == 1, tap[2], 0.0)),
                )
                after = jnp.where(ahead == -7, tap[2], 0.0)
                parts.append(jnp.concatenate([before, centre, after], axis=1))
            at = c * 128 + pair * 16
            band[at : at + 16, :] = jnp.concatenate(parts, axis=0).astype(BF16)


def across(y, outs):
    parts = []
    for at in range(0, y.shape[1], 128):
        z = y[:, at : at + 128]
        parts.append(
            roll(z[0:outs], 1, 1) + z[outs : 2 * outs] + roll(z[2 * outs : 3 * outs], -1, 1)
        )
    return parts


def down(y, groups):
    z = [y[:, 128 * c : 128 * c + 128].reshape(groups, -1, 128) for c in range(3)]
    return roll(z[0], 1, 1) + z[1] + roll(z[2], -1, 1)


def kernel(
    lon_count,
    lat_count,
    state,
    land_mask,
    kernel_one,
    bias_one,
    kernel_two,
    bias_two,
    kernel_three,
    bias_three,
    out,
    own,
    mask,
    taps_one,
    taps_two,
    taps_three,
    b_one,
    b_two,
    b_three,
    south,
    north,
    edges,
    west_cols,
    east_cols,
    corner_sw,
    corner_se,
    corner_nw,
    corner_ne,
    fold_rows,
    fold_edges,
    spread,
    band_one,
    band_two,
    band_three,
    band_south,
    band_north,
    edge_groups,
    bias_full,
    hidden_a,
    hidden_b,
    in_sems,
    send_sems,
    recv_sems,
    answers,
):
    t, j = lax.axis_index("lon"), lax.axis_index("lat")
    top = lat_count - 1
    east, west = lax.rem(t + 1, lon_count), lax.rem(t + lon_count - 1, lon_count)
    mirror = lon_count - 1 - t
    mirror_up = lax.rem(mirror + 1, lon_count)
    mirror_down = lax.rem(mirror + lon_count - 1, lon_count)

    loads = [
        pltpu.make_async_copy(src, dst, in_sems.at[i])
        for i, (src, dst) in enumerate(
            [
                (state.at[:, 0:8, :], own.at[:, 8:16, :]),
                (state.at[:, 56:64, :], own.at[:, 64:72, :]),
                (state.at[:, 8:56, :], own.at[:, 16:64, :]),
                (land_mask, mask),
                (kernel_one, taps_one),
                (kernel_two, taps_two),
                (kernel_three, taps_three),
                (bias_one, b_one),
                (bias_two, b_two),
                (bias_three, b_three),
            ]
        )
    ]
    for load in loads:
        load.start()

    def rank(lon, lat):
        z, y, x, core = (lat >> 2) * 6 + (lon >> 4), (lon & 15) >> 1, lat & 3, lon & 1
        guess = jnp.where(z < 6, 128 + 150 * z, 940 + 30 * z) + 45 * x - 41 * core
        guess = guess + jnp.where(y < 4, 57 * y, 430 - 35 * y)
        guess = jnp.where(lon + lat == 0, 1050, guess)
        return guess * 1024 + lat * lon_count + lon

    mine = rank(t, j)
    first, last = pl.ds(0, 128), pl.ds(896, 128)

    def copy(src, dst, slot, sender, lon, lat):
        return pltpu.make_async_remote_copy(
            src_ref=src,
            dst_ref=dst,
            send_sem=send_sems.at[sender],
            recv_sem=recv_sems.at[slot],
            device_id={"lon": lon, "lat": lat},
            device_id_type=MESH,
        )

    class Route:
        def __init__(self, there, lon, lat, here, yonder, *copies, step=0, quiet=False):
            self.there, self.lon, self.lat, self.here, self.yonder = there, lon, lat, here, yonder
            theirs = rank(lon, lat)
            ahead = mine < theirs
            level = jnp.abs(theirs - mine) < 300 * 1024
            if here == yonder:
                both = level
            else:
                inside = (lon > 0) & (t > 0) & (lon < lon_count - 1) & (t < lon_count - 1)
                crossing = (j == seam) if step == -1 else (j == seam - 1) if step == 1 else False
                both = level & inside & crossing
            if step == 1:
                ahead = ahead | (j == seam)
            if step == -1:
                ahead = ahead & (j != seam + 1)
            if (here, yonder) == (5, 6):
                ahead = ahead | ((t == lon_count - 1) & (j == seam))
            if (here, yonder) == (6, 5):
                ahead = ahead & ~((t == lon_count - 2) & (j == seam - 1))
            loud = there & ~jnp.bool_(quiet)
            self.greets = loud & (both | ahead)
            self.counts = loud & (both | ~ahead)
            self.answers = loud & ~both & ~ahead
            self.awaits = loud & ~both & ahead
            wraps = (lon - t > 1) | (t - lon > 1)
            self.far = (theirs - mine > 250 * 1024) | (wraps & (here != yonder))
            if (here, yonder) == (1, 0):
                self.far = self.far | ((t == lon_count - 1) & (j == seam - 1))
            if (here, yonder) == (5, 6):
                self.awaits = self.awaits & ~((t == lon_count - 1) & (j == seam))
            if (here, yonder) == (6, 5):
                self.answers = self.answers & ~((t == lon_count - 2) & (j == seam - 1))
            self.copies = [copy(*c, lon, lat) for c in copies]

        def signal(self, sem):
            pl.semaphore_signal(
                sem, inc=1, device_id={"lon": self.lon, "lat": self.lat}, device_id_type=MESH
            )

        def send(self):
            for c in self.copies:
                c.start()

    below, above, fold = j > 0, j < top, j == top
    seam = lat_count // 2 if lat_count > 3 and lon_count > 3 else 2 * lat_count
    end = lon_count - 1
    corner = seam < lat_count
    at_first = (t == 0) & (j == 0) & corner
    at_end, at_start = (t == end) & corner, (t == 0) & corner
    e_cols, w_cols = pl.ds(5, 3), pl.ds(8, 3)
    route_s = Route(
        below, t, j - 1, 2, 3, (state.at[:, 0:3, :], north.at[:, 0:3, :], HN, 2),
        step=-1, quiet=at_end & (j == seam),
    )
    route_n = Route(
        above, t, j + 1, 3, 2, (state.at[:, 61:64, :], south.at[:, 5:8, :], HS, 6),
        step=1, quiet=at_end & (j == seam - 1),
    )
    route_se = Route(
        below, east, j - 1, 4, 7, (edges.at[e_cols, first], corner_nw.at[5:8, :], NW, 4),
        step=-1, quiet=at_end & (j == 1),
    )
    route_sw = Route(
        below, west, j - 1, 5, 6, (edges.at[w_cols, first], corner_ne.at[0:3, :], NE, 5),
        step=-1, quiet=at_start & (j == seam + 1),
    )
    route_ne = Route(
        above, east, j + 1, 6, 5, (edges.at[e_cols, last], corner_sw.at[5:8, :], SW, 8),
        step=1, quiet=at_end & (j == seam),
    )
    route_nw = Route(
        above, west, j + 1, 7, 4, (edges.at[w_cols, last], corner_se.at[0:3, :], SE, 9),
        step=1, quiet=at_first,
    )
    fold_routes = [
        Route(fold, mirror, j, 3, 3, (fold_rows.at[:, 0:3, :], north.at[:, 0:3, :], HN, 6)),
        Route(
            fold & (mirror_down != t), mirror_down, j, 6, 6,
            (fold_edges.at[8:11, :], corner_ne.at[0:3, :], NE, 9),
        ),
        Route(
            fold & (mirror_up != t), mirror_up, j, 7, 7,
            (fold_edges.at[5:8, :], corner_nw.at[5:8, :], NW, 8),
        ),
    ]
    route_e = Route(
        j >= 0, east, j, 0, 1, (edges.at[e_cols, :], west_cols.at[5:8, :], HW, 0),
        quiet=(j == seam) | (at_end & (j == 0)),
    )
    route_w = Route(
        j >= 0, west, j, 1, 0, (edges.at[w_cols, :], east_cols.at[0:3, :], HE, 1),
        quiet=(j == seam) | at_first,
    )
    rows_routes = [route_s, route_n]
    corner_routes = [route_se, route_sw, route_ne, route_nw] + fold_routes
    side_routes = [route_e, route_w]
    routes = rows_routes + corner_routes + side_routes

    barrier = pltpu.get_barrier_semaphore()
    greeted = jnp.int32(0)
    for route in routes:
        greeted = greeted + route.counts.astype(jnp.int32)

        @pl.when(route.greets)
        def _():
            route.signal(barrier)

    for host, guest in (((end - 1, 0), (0, 0)),):
        greeted = greeted + ((t == host[0]) & (j == host[1]) & corner).astype(jnp.int32)

        @pl.when((t == guest[0]) & (j == guest[1]) & corner)
        def _():
            pl.semaphore_signal(
                barrier, inc=1, device_id={"lon": host[0], "lat": host[1]}, device_id_type=MESH
            )

    @pl.when(greeted > 0)
    def _():
        pl.semaphore_wait(barrier, greeted)

    for route in routes:

        @pl.when(route.answers)
        def _():
            route.signal(answers.at[route.yonder])

    for route in rows_routes:
        pl.when(route.counts)(route.send)

    own[:, 0:8, :] = jnp.zeros((16, 8, 128), F32)
    own[:, 72:80, :] = jnp.zeros((16, 8, 128), F32)
    zeros = jnp.zeros((128, 128), BF16)
    for ref in (hidden_a, hidden_b):
        ref[0:128, :] = zeros
        ref[1152:1280, :] = zeros

    loads[0].wait()

    def turn(g):
        turned = own[:, 8 * g + 8 : 8 * g + 16, :].reshape(128, 128).T
        edges[0:8, 128 * g : 128 * g + 128] = turned[120:128]
        edges[8:16, 128 * g : 128 * g + 128] = turned[0:8]
        if g in (0, 7):
            edge_groups[g // 7] = turned

    turn(0)
    for route in corner_routes[0:2]:
        pl.when(route.counts)(route.send)

    loads[1].wait()
    turn(7)

    @pl.when(fold)
    def _():
        back = 127 - iota((8, 128), 1)
        up = 7 - iota((8, 128), 0)
        for ch in range(16):
            x = own[ch, 64:72, :]
            x = jnp.take_along_axis(x, back, axis=1)
            x = jnp.take_along_axis(x, up, axis=0)
            fold_rows[ch] = -x if ch < 8 else x
        lane = iota((8, 128), 1)
        rows_back = lane + 7 - 2 * (lane % 8)
        for at in (0, 8):
            x = edges[at : at + 8, 896:1024]
            x = jnp.take_along_axis(x, rows_back, axis=1)
            x = jnp.take_along_axis(x, up, axis=0)
            fold_edges[8 - at : 16 - at, :] = jnp.where(lane < 64, -x, x)

    for route in corner_routes[2:]:
        pl.when(route.counts)(route.send)

    loads[2].wait()
    for g in range(1, 7):
        turn(g)

    for route in side_routes:
        pl.when(route.counts)(route.send)

    @pl.when(fold & (mirror_up == t))
    def _():
        corner_nw[5:8, :] = fold_edges[5:8, :]

    @pl.when(fold & (mirror_down == t))
    def _():
        corner_ne[0:3, :] = fold_edges[8:11, :]

    for load in loads[3:]:
        load.wait()
    bands(taps_one, spread, band_one)
    shifted_bands(spread, band_south, 6)
    shifted_bands(spread, band_north, 2)
    bands(taps_two, spread, band_two)
    bands(taps_three, spread, band_three)
    lane_out = iota((1, 128), 1) // 8
    bias_rows = []
    for i, (ref, outs) in enumerate(((b_one, 16), (b_two, 16), (b_three, 8))):
        row = jnp.zeros((1, 128), F32)
        for o in range(outs):
            bias_full[i, 8 * o : 8 * o + 8, :] = jnp.full((8, 128), ref[o], F32)
            row = jnp.where(lane_out == o, ref[o], row)
        bias_rows.append(row)

    for route in routes:

        @pl.when(route.awaits & ~route.far)
        def _():
            pl.semaphore_wait(answers.at[route.here], 1)
            route.send()

    @pl.when(j == seam)
    def _():
        route_e.send()

        @pl.when(t > 0)
        def _():
            route_w.send()

        @pl.when(t == end)
        def _():
            route_ne.send()

    for g in range(8):
        x = own[:, 8 * g + 8 : 8 * g + 16, :].reshape(128, 128)
        hidden_a[128 * g + 128 : 128 * g + 256, :] = x.astype(BF16)

    band_last = jnp.concatenate(
        [band_three[128 * c : 128 * c + 64, :] for c in range(3)], axis=0
    )

    def windows(ref, g):
        return jnp.concatenate(
            [ref[128 * g : 128 * g + 384, :], ref[128 * g + 128 : 128 * g + 512, :]], axis=1
        )

    for src, band, i, dst in (
        (hidden_a, band_one, 0, hidden_b),
        (hidden_b, band_two, 1, hidden_a),
    ):
        for g in range(0, 8, 2):
            y = jnp.dot(band[...], windows(src, g), preferred_element_type=F32)
            for h, v in enumerate(across(y, 128)):
                at = 128 * (g + h) + 128
                dst[at : at + 128, :] = silu(v + bias_full[i]).astype(BF16)

    lane = iota((8, 128), 1)
    row = iota((8, 128), 0)
    for g in range(0, 8, 2):
        y = jnp.dot(band_last, windows(hidden_a, g), preferred_element_type=F32)
        for h, v in enumerate(across(y, 64)):
            inner = (lane >= 3) & (lane < 125)
            if g + h == 0:
                inner = inner & (row >= 3)
            if g + h == 7:
                inner = inner & (row < 5)
            forcing = jnp.where(inner[None], (v + bias_full[2, 0:64, :]).reshape(8, 8, 128), 0.0)
            at = 8 * (g + h)
            x = own[:, at + 8 : at + 16, :]
            qn = own[:, at + 9 : at + 17, :]
            qs = own[:, at + 7 : at + 15, :]
            qe = jnp.where(lane[None] < 127, roll(x, -1, 2), 0.0)
            qw = jnp.where(lane[None] > 0, roll(x, 1, 2), 0.0)
            u = jnp.concatenate([x[0:4]] * 4, axis=0)
            w = jnp.concatenate([x[4:8]] * 4, axis=0)
            tendency = -0.5 * (u * (qe - qw) + w * (qn - qs))
            tendency = tendency + 0.2 * (qe + qw + qn + qs - 4.0 * x)
            tendency = jnp.concatenate([tendency[0:8] + forcing, tendency[8:16]], axis=0)
            ocean = 0.1 * mask[at : at + 8, :].astype(F32)
            out[:, at : at + 8, :] = x + ocean[None] * tendency

    def arrive(dst, slot):
        copy(dst, dst, slot, 0, east, j).wait_recv()

    def arrive_west():
        arrive(west_cols.at[5:8, :], HW)

    def arrive_south():
        arrive(south.at[:, 5:8, :], HS)

    def arrive_north():
        arrive(north.at[:, 0:3, :], HN)

    def arrive_sw():
        arrive(corner_sw.at[5:8, :], SW)

    via_west = at_end & ((j == 0) | (j == seam - 1) | (j == seam))
    via_sw = at_end & (j == 1)
    via_north = at_first

    @pl.when(via_west)
    def _():
        arrive_west()

        @pl.when(j == 0)
        def _():
            route_e.send()

        @pl.when(j == seam - 1)
        def _():
            route_n.send()

        @pl.when(j == seam)
        def _():
            route_s.send()
            route_sw.send()

    @pl.when(via_sw)
    def _():
        arrive_sw()
        route_se.send()

    for route in [route_e, route_w, route_sw, route_se, route_nw, route_ne] + fold_routes + rows_routes:

        @pl.when(route.awaits & route.far)
        def _():
            pl.semaphore_wait(answers.at[route.here], 1)
            route.send()

        if route is route_w:

            @pl.when(at_start & (j == seam + 1))
            def _():
                route_sw.send()

        if route is route_nw:

            @pl.when(at_start & (j == seam))
            def _():
                route_w.send()

    @pl.when(via_north)
    def _():
        arrive_north()
        route_w.send()
        route_nw.send()

    place = iota((8, 128), 0)
    lane = iota((8, 128), 1)
    inner = (lane >= 3) & (lane < 125)

    def from_se():
        pl.when(below)(lambda: arrive(corner_se.at[0:3, :], SE))

    def from_south():
        pl.when(below)(arrive_south)

    def from_sw():
        pl.when(below & ~via_sw)(arrive_sw)

    def from_ne():
        pl.when(above | (mirror_down != t))(lambda: arrive(corner_ne.at[0:3, :], NE))

    def from_north():
        pl.when(~via_north)(arrive_north)

    def from_nw():
        pl.when(above | (mirror_up != t))(lambda: arrive(corner_nw.at[5:8, :], NW))

    def from_west():
        pl.when(~via_west)(arrive_west)

    def from_east():
        arrive(east_cols.at[0:3, :], HE)


    def taps_on(x, band):
        return lax.dot_general(x, band, (((1,), (1,)), ((), ())), preferred_element_type=F32)

    def columns(kept_lanes, west=True):
        none = jnp.zeros((32, 128), BF16)

        def layer(h, band, i):
            h = [none] + h + [none]
            lhs = jnp.concatenate(
                [jnp.concatenate(h[g : g + 3], axis=1) for g in range(8)], axis=0
            )
            return down(taps_on(lhs, band[...]), 8) + bias_rows[i][None]

        h = []
        for g in range(8):
            at = pl.ds(128 * g, 128)
            beside = west_cols[:, at] if west else jnp.zeros((8, 128), F32)
            parts = [beside, edges[8:16, at], edges[0:8, at], east_cols[:, at]]
            h.append(jnp.concatenate(parts, axis=0).astype(BF16))
        for band, i in ((band_one, 0), (band_two, 1)):
            y = silu(layer(h, band, i)).astype(BF16)
            h = [y[g] for g in range(8)]
            yield
        f = layer(h, band_three, 2)
        yield

        parts = []
        for g in range(8):
            at = pl.ds(128 * g, 128)
            fe, fw = f[g, 16:24], f[g, 8:16]
            if g in (0, 7):
                kept = lane % 8 >= 3 if g == 0 else lane % 8 < 5
                fe, fw = jnp.where(kept, fe, 0.0), jnp.where(kept, fw, 0.0)
            e, w = speed(edges[0:8, at]), speed(edges[8:16, at])
            e = jnp.where(place == 7, (0.2 - 0.5 * e) * roll(east_cols[:, at], -1, 0), 0.0)
            if west:
                w = jnp.where(place == 0, (0.2 + 0.5 * w) * roll(west_cols[:, at], 1, 0), 0.0)
                fw = fw + w
            parts += [fe + e, fw]
        turned = jnp.concatenate(parts, axis=0).T
        for g in range(8):
            patch = roll(turned, 120 - 16 * g, 1).reshape(16, 8, 128)
            add(g, jnp.where(kept_lanes[None], patch, 0.0))

    def speed(x):
        x = jnp.where(lane < 32, x, 0.0)
        x = x + roll(x, 32, 1)
        return x + roll(x, 64, 1)

    def western():
        none = jnp.zeros((16, 128), BF16)
        south_rows, north_rows = rows_at("south"), rows_at("north")
        h = [jnp.concatenate([jnp.where(below, corner_sw[...], 0.0), south_rows.reshape(128, 128).T[0:8]], axis=0)]
        for g in range(8):
            at = pl.ds(128 * g, 128)
            h.append(jnp.concatenate([west_cols[:, at], edges[8:16, at]], axis=0))
        h.append(jnp.concatenate([corner_nw[...], north_rows.reshape(128, 128).T[0:8]], axis=0))
        h = [x.astype(BF16) for x in h]
        for band, i, groups in ((band_one, 0, range(10)), (band_two, 1, range(10)), (band_three, 2, range(1, 9))):
            h = [none] + h + [none]
            lhs = [jnp.concatenate(h[g : g + 3], axis=1) for g in groups]
            y = down(taps_on(jnp.concatenate(lhs, axis=0), band[...]), len(lhs)) + bias_rows[i][None]
            z = silu(y).astype(BF16)
            h = [z[g] for g in range(len(lhs))]
        parts = []
        for g in range(8):
            at = pl.ds(128 * g, 128)
            w = (0.2 + 0.5 * speed(edges[8:16, at])) * roll(west_cols[:, at], 1, 0)
            parts.append(y[g, 8:16] + jnp.where(place == 0, w, 0.0))
        turned = jnp.concatenate(parts + [jnp.zeros((64, 128), F32)], axis=0).T
        for g in range(8):
            patch = roll(turned, -8 * g, 1).reshape(16, 8, 128)
            add(g, jnp.where((lane < 3)[None], patch, 0.0))

    def rows_at(side):
        if side == "south":
            return jnp.where(((place >= 5) & below)[None], south[...], 0.0)
        return jnp.where((place < 3)[None], north[...], 0.0)

    def add(g, patch):
        at = 8 * g
        ocean = 0.1 * mask[at : at + 8, :].astype(F32)
        out[:, at : at + 8, :] = out[:, at : at + 8, :] + ocean[None] * patch

    def edge(side, kept_lanes, west=True, corner=True):
        if side == "south":
            g, at, shift, band = 0, pl.ds(0, 128), -2, band_south
            rows = rows_at(side)
            ends = [corner_sw, corner_se]
            outer, next_to, step, sign = place < 3, place == 0, 1, 0.5
        else:
            g, at, shift, band = 7, pl.ds(896, 128), 2, band_north
            rows = rows_at(side)
            ends = [corner_nw, corner_ne]
            outer, next_to, step, sign = place >= 5, place == 7, -1, -0.5
        blank = jnp.zeros((8, 128), F32)
        ends = [x[...] if come else blank for x, come in zip(ends, (west, corner))]
        if side == "south":
            ends = [jnp.where(below, x, 0.0) for x in ends]
        beyond = jnp.concatenate([ends[0], rows.reshape(128, 128).T, ends[1]], axis=0)
        beside = west_cols[:, at] if west else blank
        here = jnp.concatenate([beside, edge_groups[g // 7], east_cols[:, at]], axis=0)
        pair = [beyond, here] if side == "south" else [here, beyond]
        h = jnp.concatenate(pair, axis=1).astype(BF16)
        for y in edge_layers(h, band):
            yield
        forcing = roll(y[8:136].T[0:64].reshape(8, 8, 128), shift, 1)
        forcing = jnp.where((outer & kept_lanes)[None], forcing, 0.0)
        x = own[:, 8 * g + 8 : 8 * g + 16, :]
        v = jnp.concatenate([x[4:8]] * 4, axis=0)
        near = jnp.where(next_to[None], (0.2 + sign * v) * roll(rows, step, 1), 0.0)
        add(g, jnp.concatenate([near[0:8] + forcing, near[8:16]], axis=0))

    def edge_layers(h, band):
        for taps, i in (
            (band[...], 0),
            (band_two[:, 128:256], 1),
            (band_three[:, 128:256], 2),
        ):
            y = taps_on(h, taps)
            y = roll(y[:, 0:128], 1, 0) + y[:, 128:256] + roll(y[:, 256:384], -1, 0) + bias_rows[i]
            h = silu(y).astype(BF16)
            yield y

    def north_east():
        beyond = rows_at("north").reshape(128, 128).T[104:128]
        beyond = jnp.concatenate([beyond, corner_ne[...]], axis=0)
        here = jnp.concatenate([edge_groups[1, 104:128, :], east_cols[:, 896:1024]], axis=0)
        for y in edge_layers(jnp.concatenate([here, beyond], axis=1).astype(BF16), band_north):
            pass
        turned = jnp.concatenate([jnp.zeros((104, 128), F32), y[0:24]], axis=0).T
        forcing = roll(turned[0:64].reshape(8, 8, 128), 2, 1)
        forcing = jnp.where(((place >= 5) & (lane >= 125))[None], forcing, 0.0)
        ocean = 0.1 * mask[56:64, :].astype(F32)
        out[0:8, 56:64, :] = out[0:8, 56:64, :] + ocean[None] * forcing

    def together(*pieces):
        pieces = list(pieces)
        while pieces:
            pieces = [p for p in pieces if next(p, pieces) is not pieces]

    everywhere = lane >= 0
    outside = (lane < 3) | (lane >= 125)

    @pl.when(t == 0)
    def _():
        for wait in (from_east, from_south, from_se, from_north, from_ne):
            wait()
        together(
            edge("south", lane >= 3, west=False),
            edge("north", lane >= 3, west=False),
            columns(lane >= 125, west=False),
        )
        for wait in (from_west, from_sw, from_nw):
            wait()
        western()

    @pl.when((t > 0) & (j == seam))
    def _():
        for wait in (from_west, from_east, from_north, from_nw, from_ne):
            wait()
        together(edge("north", everywhere), columns(outside))
        for wait in (from_south, from_sw, from_se):
            wait()
        together(edge("south", everywhere))

    @pl.when((t > 0) & (j != seam))
    def _():
        for wait in (from_west, from_east, from_south, from_sw, from_se):
            wait()
        together(edge("south", everywhere), columns(outside))
        from_north()
        from_nw()
        together(edge("north", lane < 125, corner=False))
        from_ne()
        north_east()

    for route in routes:

        @pl.when(route.there)
        def _():
            for c in route.copies:
                c.wait_send()


def solution(mesh):
    lon_count, lat_count = mesh.shape["lon"], mesh.shape["lat"]

    def step(*args):
        state, *rest = [pltpu.with_memory_space_constraint(x, pltpu.HBM) for x in args]
        return pl.pallas_call(
            functools.partial(kernel, lon_count, lat_count),
            out_shape=jax.ShapeDtypeStruct(state.shape, F32),
            in_specs=[pl.BlockSpec(memory_space=pltpu.HBM)] * 8,
            out_specs=pl.BlockSpec(memory_space=pltpu.VMEM),
            scratch_shapes=[
                pltpu.VMEM((16, 80, 128), F32),
                pltpu.VMEM((64, 128), jnp.int32),
                pltpu.VMEM((3, 3, 16, 16), BF16),
                pltpu.VMEM((3, 3, 16, 16), BF16),
                pltpu.VMEM((3, 3, 8, 16), BF16),
                pltpu.SMEM((16,), F32),
                pltpu.SMEM((16,), F32),
                pltpu.SMEM((8,), F32),
                pltpu.VMEM((16, 8, 128), F32),
                pltpu.VMEM((16, 8, 128), F32),
                pltpu.VMEM((16, 1024), F32),
                pltpu.VMEM((8, 1024), F32),
                pltpu.VMEM((8, 1024), F32),
                pltpu.VMEM((8, 128), F32),
                pltpu.VMEM((8, 128), F32),
                pltpu.VMEM((8, 128), F32),
                pltpu.VMEM((8, 128), F32),
                pltpu.VMEM((16, 8, 128), F32),
                pltpu.VMEM((16, 128), F32),
                pltpu.VMEM((144, 128), F32),
                pltpu.VMEM((384, 384), BF16),
                pltpu.VMEM((384, 384), BF16),
                pltpu.VMEM((384, 384), BF16),
                pltpu.VMEM((384, 256), BF16),
                pltpu.VMEM((384, 256), BF16),
                pltpu.VMEM((2, 128, 128), F32),
                pltpu.VMEM((3, 128, 128), F32),
                pltpu.VMEM((1280, 128), BF16),
                pltpu.VMEM((1280, 128), BF16),
                pltpu.SemaphoreType.DMA((10,)),
                pltpu.SemaphoreType.DMA((10,)),
                pltpu.SemaphoreType.DMA((10,)),
                pltpu.SemaphoreType.REGULAR((8,)),
            ],
            compiler_params=pltpu.CompilerParams(
                collective_id=0, has_side_effects=True, vmem_limit_bytes=32 * 1024 * 1024
            ),
        )(state, *rest)

    return jax.shard_map(
        step,
        mesh=mesh,
        in_specs=(P(None, "lat", "lon"), P("lat", "lon"), P(), P(), P(), P(), P(), P()),
        out_specs=P(None, "lat", "lon"),
        check_vma=False,
    )
```

```python
import functools

import jax
import jax.numpy as jnp
from jax import lax
from jax.experimental import pallas as pl
from jax.experimental.pallas import tpu as pltpu
from jax.sharding import PartitionSpec as P

MESH = pl.DeviceIdType.MESH
F32, BF16 = jnp.float32, jnp.bfloat16
HW, HE, HS, HN, SW, SE, NW, NE = range(8)


def iota(shape, dim):
    return lax.broadcasted_iota(jnp.int32, shape, dim)


def silu(v):
    half = 0.5 * v
    return half + half * jnp.tanh(half)


def roll(x, shift, axis):
    return pltpu.roll(x, shift % x.shape[axis], axis)


def spread_taps(taps, spread):
    outs = taps.shape[2]
    spreading = (iota((16, 128), 0) == iota((16, 128), 1) // 8).astype(BF16)
    flat = taps[...].reshape(9 * outs, 16)
    spread[0 : 9 * outs, :] = jnp.dot(flat, spreading, preferred_element_type=F32)


def tap_rows(spread, outs, c, o):
    at = [(a * 3 + c) * outs + o for a in range(3)]
    return [jnp.broadcast_to(spread[i : i + 1, :], (8, 128)) for i in at]


def shifted_bands(spread, band, shift):
    ahead = iota((8, 128), 1) % 8 - iota((8, 128), 0)
    for c in range(3):
        for pair in range(8):
            parts = []
            for o in (2 * pair, 2 * pair + 1):
                tap = tap_rows(spread, 16, c, o)
                groups = []
                for g in range(2):
                    part = jnp.zeros((8, 128), F32)
                    for a in range(3):
                        part = jnp.where(ahead == shift + a - 1 - 8 * g, tap[a], part)
                    groups.append(part)
                parts.append(jnp.concatenate(groups, axis=1))
            at = c * 128 + pair * 16
            band[at : at + 16, :] = jnp.concatenate(parts, axis=0).astype(BF16)


def bands(taps, spread, band):
    outs = taps.shape[2]
    spread_taps(taps, spread)
    ahead = iota((8, 128), 1) % 8 - iota((8, 128), 0)
    for c in range(3):
        for pair in range(8):
            parts = []
            for o in (2 * pair, 2 * pair + 1):
                if o >= outs:
                    parts.append(jnp.zeros((8, 384), F32))
                    continue
                tap = tap_rows(spread, outs, c, o)
                before = jnp.where(ahead == 7, tap[0], 0.0)
                centre = jnp.where(
                    ahead == -1,
                    tap[0],
                    jnp.where(ahead == 0, tap[1], jnp.where(ahead == 1, tap[2], 0.0)),
                )
                after = jnp.where(ahead == -7, tap[2], 0.0)
                parts.append(jnp.concatenate([before, centre, after], axis=1))
            at = c * 128 + pair * 16
            band[at : at + 16, :] = jnp.concatenate(parts, axis=0).astype(BF16)


def across(y, outs):
    parts = []
    for at in range(0, y.shape[1], 128):
        z = y[:, at : at + 128]
        parts.append(
            roll(z[0:outs], 1, 1) + z[outs : 2 * outs] + roll(z[2 * outs : 3 * outs], -1, 1)
        )
    return parts


def down(y, groups):
    z = [y[:, 128 * c : 128 * c + 128].reshape(groups, -1, 128) for c in range(3)]
    return roll(z[0], 1, 1) + z[1] + roll(z[2], -1, 1)


def kernel(
    lon_count,
    lat_count,
    state,
    land_mask,
    kernel_one,
    bias_one,
    kernel_two,
    bias_two,
    kernel_three,
    bias_three,
    out,
    own,
    mask,
    taps_one,
    taps_two,
    taps_three,
    b_one,
    b_two,
    b_three,
    south,
    north,
    edges,
    west_cols,
    east_cols,
    corner_sw,
    corner_se,
    corner_nw,
    corner_ne,
    fold_rows,
    fold_edges,
    spread,
    band_one,
    band_two,
    band_three,
    band_south,
    band_north,
    edge_groups,
    bias_full,
    hidden_a,
    hidden_b,
    in_sems,
    send_sems,
    recv_sems,
    answers,
):
    t, j = lax.axis_index("lon"), lax.axis_index("lat")
    top = lat_count - 1
    east, west = lax.rem(t + 1, lon_count), lax.rem(t + lon_count - 1, lon_count)
    mirror = lon_count - 1 - t
    mirror_up = lax.rem(mirror + 1, lon_count)
    mirror_down = lax.rem(mirror + lon_count - 1, lon_count)

    loads = [
        pltpu.make_async_copy(src, dst, in_sems.at[i])
        for i, (src, dst) in enumerate(
            [
                (state.at[:, 0:8, :], own.at[:, 8:16, :]),
                (state.at[:, 56:64, :], own.at[:, 64:72, :]),
                (state.at[:, 8:56, :], own.at[:, 16:64, :]),
                (land_mask, mask),
                (kernel_one, taps_one),
                (kernel_two, taps_two),
                (kernel_three, taps_three),
                (bias_one, b_one),
                (bias_two, b_two),
                (bias_three, b_three),
            ]
        )
    ]
    row_seam = lat_count // 2 if lat_count > 3 and lon_count > 3 else 2 * lat_count
    loads[0].start()

    def load_rest():
        for load in loads[1:]:
            load.start()

    pl.when(j != row_seam)(load_rest)

    def rank(lon, lat):
        z, y, x, core = (lat >> 2) * 6 + (lon >> 4), (lon & 15) >> 1, lat & 3, lon & 1
        guess = jnp.where(z < 6, 128 + 150 * z, 940 + 30 * z) + 45 * x - 41 * core
        guess = guess + jnp.where(y < 4, 57 * y, 430 - 35 * y)
        guess = jnp.where(lon + lat == 0, 1050, guess)
        return guess * 1024 + lat * lon_count + lon

    mine = rank(t, j)
    first, last = pl.ds(0, 128), pl.ds(896, 128)

    def copy(src, dst, slot, sender, lon, lat):
        return pltpu.make_async_remote_copy(
            src_ref=src,
            dst_ref=dst,
            send_sem=send_sems.at[sender],
            recv_sem=recv_sems.at[slot],
            device_id={"lon": lon, "lat": lat},
            device_id_type=MESH,
        )

    class Route:
        def __init__(self, there, lon, lat, here, yonder, *copies, step=0, quiet=False):
            self.there, self.lon, self.lat, self.here, self.yonder = there, lon, lat, here, yonder
            theirs = rank(lon, lat)
            ahead = mine < theirs
            level = jnp.abs(theirs - mine) < 300 * 1024
            if here == yonder:
                both = level
            else:
                inside = (lon > 0) & (t > 0) & (lon < lon_count - 1) & (t < lon_count - 1)
                crossing = (j == seam) if step == -1 else (j == seam - 1) if step == 1 else False
                both = level & inside & crossing
            if (here, yonder) == (6, 5):
                spared = (j == seam - 1) & ((t & 15) == 7) & (2 * t < lon_count)
                both, ahead = both & ~spared, ahead | spared
            if (here, yonder) == (5, 6):
                spared = (j == seam) & ((t & 15) == 8) & (2 * t < lon_count)
                both, ahead = both & ~spared, ahead & ~spared
            if step == 1:
                ahead = ahead | (j == seam)
            if step == -1:
                ahead = ahead & (j != seam + 1)
            if (here, yonder) == (5, 6):
                ahead = ahead | ((t == lon_count - 1) & (j == seam))
            if (here, yonder) == (6, 5):
                ahead = ahead & ~((t == lon_count - 2) & (j == seam - 1))
            loud = there & ~jnp.bool_(quiet)
            self.greets = loud & (both | ahead)
            self.counts = loud & (both | ~ahead)
            self.answers = loud & ~both & ~ahead
            self.awaits = loud & ~both & ahead
            wraps = (lon - t > 1) | (t - lon > 1)
            self.far = (theirs - mine > 250 * 1024) | (wraps & (here != yonder))
            if (here, yonder) == (1, 0):
                self.far = self.far | ((t == lon_count - 1) & (j == seam - 1))
            if (here, yonder) == (6, 5):
                self.awaits, self.there = self.awaits & ~spared, there & ~spared
            if (here, yonder) == (5, 6):
                self.answers = self.answers & ~spared
            if (here, yonder) == (5, 6):
                self.awaits = self.awaits & ~((t == lon_count - 1) & (j == seam))
            if (here, yonder) == (6, 5):
                self.answers = self.answers & ~((t == lon_count - 2) & (j == seam - 1))
            self.copies = [copy(*c, lon, lat) for c in copies]

        def signal(self, sem):
            pl.semaphore_signal(
                sem, inc=1, device_id={"lon": self.lon, "lat": self.lat}, device_id_type=MESH
            )

        def send(self):
            for c in self.copies:
                c.start()

    below, above, fold = j > 0, j < top, j == top
    seam = lat_count // 2 if lat_count > 3 and lon_count > 3 else 2 * lat_count
    end = lon_count - 1
    corner = seam < lat_count
    at_first = (t == 0) & (j == 0) & corner
    at_end, at_start = (t == end) & corner, (t == 0) & corner
    e_cols, w_cols = pl.ds(5, 3), pl.ds(8, 3)
    route_s = Route(
        below, t, j - 1, 2, 3, (state.at[:, 0:3, :], north.at[:, 0:3, :], HN, 2),
        step=-1, quiet=at_end & (j == seam),
    )
    route_n = Route(
        above, t, j + 1, 3, 2, (state.at[:, 61:64, :], south.at[:, 5:8, :], HS, 6),
        step=1, quiet=at_end & (j == seam - 1),
    )
    route_se = Route(
        below, east, j - 1, 4, 7, (edges.at[e_cols, first], corner_nw.at[5:8, :], NW, 4),
        step=-1, quiet=at_end & (j == 1),
    )
    route_sw = Route(
        below, west, j - 1, 5, 6, (edges.at[w_cols, first], corner_ne.at[0:3, :], NE, 5),
        step=-1, quiet=at_start & (j == seam + 1),
    )
    route_ne = Route(
        above, east, j + 1, 6, 5, (edges.at[e_cols, last], corner_sw.at[5:8, :], SW, 8),
        step=1, quiet=at_end & (j == seam),
    )
    route_nw = Route(
        above, west, j + 1, 7, 4, (edges.at[w_cols, last], corner_se.at[0:3, :], SE, 9),
        step=1, quiet=at_first,
    )
    fold_routes = [
        Route(fold, mirror, j, 3, 3, (fold_rows.at[:, 0:3, :], north.at[:, 0:3, :], HN, 6)),
        Route(
            fold & (mirror_down != t), mirror_down, j, 6, 6,
            (fold_edges.at[8:11, :], corner_ne.at[0:3, :], NE, 9),
        ),
        Route(
            fold & (mirror_up != t), mirror_up, j, 7, 7,
            (fold_edges.at[5:8, :], corner_nw.at[5:8, :], NW, 8),
        ),
    ]
    route_e = Route(
        j >= 0, east, j, 0, 1, (edges.at[e_cols, :], west_cols.at[5:8, :], HW, 0),
        quiet=(j == seam) | (at_end & (j == 0)),
    )
    route_w = Route(
        j >= 0, west, j, 1, 0, (edges.at[w_cols, :], east_cols.at[0:3, :], HE, 1),
        quiet=(j == seam) | at_first,
    )
    stands_in = (j == seam - 1) & ((t & 15) == 8) & (2 * t < lon_count)
    for_neighbour = copy(
        west_cols.at[5:8, last], corner_sw.at[5:8, :], SW, 10, t, j + 1
    )
    rows_routes = [route_s, route_n]
    corner_routes = [route_sw, route_se, route_ne, route_nw] + fold_routes
    side_routes = [route_e, route_w]
    routes = rows_routes + corner_routes + side_routes

    barrier = pltpu.get_barrier_semaphore()
    greeted = jnp.int32(0)
    for route in routes:
        greeted = greeted + route.counts.astype(jnp.int32)

        @pl.when(route.greets)
        def _():
            route.signal(barrier)

    for host, guest in (((end - 1, 0), (0, 0)),):
        greeted = greeted + ((t == host[0]) & (j == host[1]) & corner).astype(jnp.int32)

        @pl.when((t == guest[0]) & (j == guest[1]) & corner)
        def _():
            pl.semaphore_signal(
                barrier, inc=1, device_id={"lon": host[0], "lat": host[1]}, device_id_type=MESH
            )

    @pl.when(greeted > 0)
    def _():
        pl.semaphore_wait(barrier, greeted)

    for route in routes:

        @pl.when(route.answers)
        def _():
            route.signal(answers.at[route.yonder])

    for route in rows_routes:
        pl.when(route.counts)(route.send)

    pl.when(j == row_seam)(load_rest)

    own[:, 0:8, :] = jnp.zeros((16, 8, 128), F32)
    own[:, 72:80, :] = jnp.zeros((16, 8, 128), F32)
    zeros = jnp.zeros((128, 128), BF16)
    for ref in (hidden_a, hidden_b):
        ref[0:128, :] = zeros
        ref[1152:1280, :] = zeros

    loads[0].wait()

    def turn(g):
        turned = own[:, 8 * g + 8 : 8 * g + 16, :].reshape(128, 128).T
        edges[0:8, 128 * g : 128 * g + 128] = turned[120:128]
        edges[8:16, 128 * g : 128 * g + 128] = turned[0:8]
        if g in (0, 7):
            edge_groups[g // 7] = turned

    turn(0)
    for route in corner_routes[0:2]:
        pl.when(route.counts)(route.send)

    loads[1].wait()
    turn(7)

    @pl.when(fold)
    def _():
        back = 127 - iota((8, 128), 1)
        up = 7 - iota((8, 128), 0)
        for ch in range(16):
            x = own[ch, 64:72, :]
            x = jnp.take_along_axis(x, back, axis=1)
            x = jnp.take_along_axis(x, up, axis=0)
            fold_rows[ch] = -x if ch < 8 else x
        lane = iota((8, 128), 1)
        rows_back = lane + 7 - 2 * (lane % 8)
        for at in (0, 8):
            x = edges[at : at + 8, 896:1024]
            x = jnp.take_along_axis(x, rows_back, axis=1)
            x = jnp.take_along_axis(x, up, axis=0)
            fold_edges[8 - at : 16 - at, :] = jnp.where(lane < 64, -x, x)

    for route in corner_routes[2:]:
        pl.when(route.counts)(route.send)

    loads[2].wait()
    for g in range(1, 7):
        turn(g)

    for route in side_routes:
        pl.when(route.counts)(route.send)

    @pl.when(fold & (mirror_up == t))
    def _():
        corner_nw[5:8, :] = fold_edges[5:8, :]

    @pl.when(fold & (mirror_down == t))
    def _():
        corner_ne[0:3, :] = fold_edges[8:11, :]

    for load in loads[3:]:
        load.wait()
    bands(taps_one, spread, band_one)
    shifted_bands(spread, band_south, 6)
    shifted_bands(spread, band_north, 2)
    bands(taps_two, spread, band_two)
    bands(taps_three, spread, band_three)
    lane_out = iota((1, 128), 1) // 8
    bias_rows = []
    for i, (ref, outs) in enumerate(((b_one, 16), (b_two, 16), (b_three, 8))):
        row = jnp.zeros((1, 128), F32)
        for o in range(outs):
            bias_full[i, 8 * o : 8 * o + 8, :] = jnp.full((8, 128), ref[o], F32)
            row = jnp.where(lane_out == o, ref[o], row)
        bias_rows.append(row)

    for route in routes:

        @pl.when(route.awaits & ~route.far)
        def _():
            pl.semaphore_wait(answers.at[route.here], 1)
            route.send()

    @pl.when(j == seam)
    def _():
        route_e.send()

        @pl.when(t > 0)
        def _():
            route_w.send()

        @pl.when(t == end)
        def _():
            route_ne.send()

    for g in range(8):
        x = own[:, 8 * g + 8 : 8 * g + 16, :].reshape(128, 128)
        hidden_a[128 * g + 128 : 128 * g + 256, :] = x.astype(BF16)

    band_last = jnp.concatenate(
        [band_three[128 * c : 128 * c + 64, :] for c in range(3)], axis=0
    )

    def windows(ref, g):
        return jnp.concatenate(
            [ref[128 * g : 128 * g + 384, :], ref[128 * g + 128 : 128 * g + 512, :]], axis=1
        )

    for src, band, i, dst in (
        (hidden_a, band_one, 0, hidden_b),
        (hidden_b, band_two, 1, hidden_a),
    ):
        for g in range(0, 8, 2):
            y = jnp.dot(band[...], windows(src, g), preferred_element_type=F32)
            for h, v in enumerate(across(y, 128)):
                at = 128 * (g + h) + 128
                dst[at : at + 128, :] = silu(v + bias_full[i]).astype(BF16)

    lane = iota((8, 128), 1)
    row = iota((8, 128), 0)
    for g in range(0, 8, 2):
        y = jnp.dot(band_last, windows(hidden_a, g), preferred_element_type=F32)
        for h, v in enumerate(across(y, 64)):
            inner = (lane >= 3) & (lane < 125)
            if g + h == 0:
                inner = inner & (row >= 3)
            if g + h == 7:
                inner = inner & (row < 5)
            forcing = jnp.where(inner[None], (v + bias_full[2, 0:64, :]).reshape(8, 8, 128), 0.0)
            at = 8 * (g + h)
            x = own[:, at + 8 : at + 16, :]
            qn = own[:, at + 9 : at + 17, :]
            qs = own[:, at + 7 : at + 15, :]
            qe = jnp.where(lane[None] < 127, roll(x, -1, 2), 0.0)
            qw = jnp.where(lane[None] > 0, roll(x, 1, 2), 0.0)
            u = jnp.concatenate([x[0:4]] * 4, axis=0)
            w = jnp.concatenate([x[4:8]] * 4, axis=0)
            tendency = -0.5 * (u * (qe - qw) + w * (qn - qs))
            tendency = tendency + 0.2 * (qe + qw + qn + qs - 4.0 * x)
            tendency = jnp.concatenate([tendency[0:8] + forcing, tendency[8:16]], axis=0)
            ocean = 0.1 * mask[at : at + 8, :].astype(F32)
            out[:, at : at + 8, :] = x + ocean[None] * tendency

    def arrive(dst, slot):
        copy(dst, dst, slot, 0, east, j).wait_recv()

    def arrive_west():
        arrive(west_cols.at[5:8, :], HW)

    def arrive_south():
        arrive(south.at[:, 5:8, :], HS)

    def arrive_north():
        arrive(north.at[:, 0:3, :], HN)

    def arrive_sw():
        arrive(corner_sw.at[5:8, :], SW)

    via_west = at_end & ((j == 0) | (j == seam - 1) | (j == seam))
    via_sw = at_end & (j == 1)
    via_north = at_first

    @pl.when(via_west)
    def _():
        arrive_west()

        @pl.when(j == 0)
        def _():
            route_e.send()

        @pl.when(j == seam - 1)
        def _():
            route_n.send()

        @pl.when(j == seam)
        def _():
            route_s.send()
            route_sw.send()

    @pl.when(via_sw)
    def _():
        arrive_sw()
        route_se.send()

    for route in [route_e, route_w, route_sw, route_se, route_nw, route_ne] + fold_routes + rows_routes:

        @pl.when(route.awaits & route.far)
        def _():
            pl.semaphore_wait(answers.at[route.here], 1)
            route.send()

        if route is route_w:

            @pl.when(at_start & (j == seam + 1))
            def _():
                route_sw.send()

        if route is route_nw:

            @pl.when(at_start & (j == seam))
            def _():
                route_w.send()

    @pl.when(stands_in)
    def _():
        arrive_west()
        for_neighbour.start()

    @pl.when(via_north)
    def _():
        arrive_north()
        route_w.send()
        route_nw.send()

    place = iota((8, 128), 0)
    lane = iota((8, 128), 1)
    inner = (lane >= 3) & (lane < 125)

    def from_se():
        pl.when(below)(lambda: arrive(corner_se.at[0:3, :], SE))

    def from_south():
        pl.when(below)(arrive_south)

    def from_sw():
        pl.when(below & ~via_sw)(arrive_sw)

    def from_ne():
        pl.when(above | (mirror_down != t))(lambda: arrive(corner_ne.at[0:3, :], NE))

    def from_north():
        pl.when(~via_north)(arrive_north)

    def from_nw():
        pl.when(above | (mirror_up != t))(lambda: arrive(corner_nw.at[5:8, :], NW))

    def from_west():
        pl.when(~via_west & ~stands_in)(arrive_west)

    def from_east():
        arrive(east_cols.at[0:3, :], HE)


    def taps_on(x, band):
        return lax.dot_general(x, band, (((1,), (1,)), ((), ())), preferred_element_type=F32)

    def columns(kept_lanes, west=True):
        none = jnp.zeros((32, 128), BF16)

        def layer(h, band, i):
            h = [none] + h + [none]
            lhs = jnp.concatenate(
                [jnp.concatenate(h[g : g + 3], axis=1) for g in range(8)], axis=0
            )
            return down(taps_on(lhs, band[...]), 8) + bias_rows[i][None]

        h = []
        for g in range(8):
            at = pl.ds(128 * g, 128)
            beside = west_cols[:, at] if west else jnp.zeros((8, 128), F32)
            parts = [beside, edges[8:16, at], edges[0:8, at], east_cols[:, at]]
            h.append(jnp.concatenate(parts, axis=0).astype(BF16))
        for band, i in ((band_one, 0), (band_two, 1)):
            y = silu(layer(h, band, i)).astype(BF16)
            h = [y[g] for g in range(8)]
            yield
        f = layer(h, band_three, 2)
        yield

        parts = []
        for g in range(8):
            at = pl.ds(128 * g, 128)
            fe, fw = f[g, 16:24], f[g, 8:16]
            if g in (0, 7):
                kept = lane % 8 >= 3 if g == 0 else lane % 8 < 5
                fe, fw = jnp.where(kept, fe, 0.0), jnp.where(kept, fw, 0.0)
            e, w = speed(edges[0:8, at]), speed(edges[8:16, at])
            e = jnp.where(place == 7, (0.2 - 0.5 * e) * roll(east_cols[:, at], -1, 0), 0.0)
            if west:
                w = jnp.where(place == 0, (0.2 + 0.5 * w) * roll(west_cols[:, at], 1, 0), 0.0)
                fw = fw + w
            parts += [fe + e, fw]
        turned = jnp.concatenate(parts, axis=0).T
        for g in range(8):
            patch = roll(turned, 120 - 16 * g, 1).reshape(16, 8, 128)
            add(g, jnp.where(kept_lanes[None], patch, 0.0))

    def speed(x):
        x = jnp.where(lane < 32, x, 0.0)
        x = x + roll(x, 32, 1)
        return x + roll(x, 64, 1)

    def western():
        none = jnp.zeros((16, 128), BF16)
        south_rows, north_rows = rows_at("south"), rows_at("north")
        h = [jnp.concatenate([jnp.where(below, corner_sw[...], 0.0), south_rows.reshape(128, 128).T[0:8]], axis=0)]
        for g in range(8):
            at = pl.ds(128 * g, 128)
            h.append(jnp.concatenate([west_cols[:, at], edges[8:16, at]], axis=0))
        h.append(jnp.concatenate([corner_nw[...], north_rows.reshape(128, 128).T[0:8]], axis=0))
        h = [x.astype(BF16) for x in h]
        for band, i, groups in ((band_one, 0, range(10)), (band_two, 1, range(10)), (band_three, 2, range(1, 9))):
            h = [none] + h + [none]
            lhs = [jnp.concatenate(h[g : g + 3], axis=1) for g in groups]
            y = down(taps_on(jnp.concatenate(lhs, axis=0), band[...]), len(lhs)) + bias_rows[i][None]
            z = silu(y).astype(BF16)
            h = [z[g] for g in range(len(lhs))]
        parts = []
        for g in range(8):
            at = pl.ds(128 * g, 128)
            w = (0.2 + 0.5 * speed(edges[8:16, at])) * roll(west_cols[:, at], 1, 0)
            parts.append(y[g, 8:16] + jnp.where(place == 0, w, 0.0))
        turned = jnp.concatenate(parts + [jnp.zeros((64, 128), F32)], axis=0).T
        for g in range(8):
            patch = roll(turned, -8 * g, 1).reshape(16, 8, 128)
            add(g, jnp.where((lane < 3)[None], patch, 0.0))

    def rows_at(side):
        if side == "south":
            return jnp.where(((place >= 5) & below)[None], south[...], 0.0)
        return jnp.where((place < 3)[None], north[...], 0.0)

    def add(g, patch):
        at = 8 * g
        ocean = 0.1 * mask[at : at + 8, :].astype(F32)
        out[:, at : at + 8, :] = out[:, at : at + 8, :] + ocean[None] * patch

    def edge(side, kept_lanes, west=True, corner=True):
        if side == "south":
            g, at, shift, band = 0, pl.ds(0, 128), -2, band_south
            rows = rows_at(side)
            ends = [corner_sw, corner_se]
            outer, next_to, step, sign = place < 3, place == 0, 1, 0.5
        else:
            g, at, shift, band = 7, pl.ds(896, 128), 2, band_north
            rows = rows_at(side)
            ends = [corner_nw, corner_ne]
            outer, next_to, step, sign = place >= 5, place == 7, -1, -0.5
        blank = jnp.zeros((8, 128), F32)
        ends = [x[...] if come else blank for x, come in zip(ends, (west, corner))]
        if side == "south":
            ends = [jnp.where(below, x, 0.0) for x in ends]
        beyond = jnp.concatenate([ends[0], rows.reshape(128, 128).T, ends[1]], axis=0)
        beside = west_cols[:, at] if west else blank
        here = jnp.concatenate([beside, edge_groups[g // 7], east_cols[:, at]], axis=0)
        pair = [beyond, here] if side == "south" else [here, beyond]
        h = jnp.concatenate(pair, axis=1).astype(BF16)
        for y in edge_layers(h, band):
            yield
        forcing = roll(y[8:136].T[0:64].reshape(8, 8, 128), shift, 1)
        forcing = jnp.where((outer & kept_lanes)[None], forcing, 0.0)
        x = own[:, 8 * g + 8 : 8 * g + 16, :]
        v = jnp.concatenate([x[4:8]] * 4, axis=0)
        near = jnp.where(next_to[None], (0.2 + sign * v) * roll(rows, step, 1), 0.0)
        add(g, jnp.concatenate([near[0:8] + forcing, near[8:16]], axis=0))

    def edge_layers(h, band):
        for taps, i in (
            (band[...], 0),
            (band_two[:, 128:256], 1),
            (band_three[:, 128:256], 2),
        ):
            y = taps_on(h, taps)
            y = roll(y[:, 0:128], 1, 0) + y[:, 128:256] + roll(y[:, 256:384], -1, 0) + bias_rows[i]
            h = silu(y).astype(BF16)
            yield y

    def north_east():
        beyond = rows_at("north").reshape(128, 128).T[104:128]
        beyond = jnp.concatenate([beyond, corner_ne[...]], axis=0)
        here = jnp.concatenate([edge_groups[1, 104:128, :], east_cols[:, 896:1024]], axis=0)
        for y in edge_layers(jnp.concatenate([here, beyond], axis=1).astype(BF16), band_north):
            pass
        turned = jnp.concatenate([jnp.zeros((104, 128), F32), y[0:24]], axis=0).T
        forcing = roll(turned[0:64].reshape(8, 8, 128), 2, 1)
        forcing = jnp.where(((place >= 5) & (lane >= 125))[None], forcing, 0.0)
        ocean = 0.1 * mask[56:64, :].astype(F32)
        out[0:8, 56:64, :] = out[0:8, 56:64, :] + ocean[None] * forcing

    def together(*pieces):
        pieces = list(pieces)
        while pieces:
            pieces = [p for p in pieces if next(p, pieces) is not pieces]

    everywhere = lane >= 0
    outside = (lane < 3) | (lane >= 125)

    @pl.when(t == 0)
    def _():
        for wait in (from_east, from_south, from_se, from_north, from_ne):
            wait()
        together(
            edge("south", lane >= 3, west=False),
            edge("north", lane >= 3, west=False),
            columns(lane >= 125, west=False),
        )
        for wait in (from_west, from_sw, from_nw):
            wait()
        western()

    @pl.when((t > 0) & (j == seam))
    def _():
        for wait in (from_west, from_east, from_north, from_nw, from_ne):
            wait()
        together(edge("north", everywhere), columns(outside))
        for wait in (from_south, from_sw, from_se):
            wait()
        together(edge("south", everywhere))

    @pl.when((t > 0) & (j != seam))
    def _():
        for wait in (from_west, from_east, from_south, from_sw, from_se):
            wait()
        together(edge("south", everywhere), columns(outside))
        from_north()
        from_nw()
        together(edge("north", lane < 125, corner=False))
        from_ne()
        north_east()

    for route in routes:

        @pl.when(route.there)
        def _():
            for c in route.copies:
                c.wait_send()

    pl.when(stands_in)(lambda: for_neighbour.wait_send())


def solution(mesh):
    lon_count, lat_count = mesh.shape["lon"], mesh.shape["lat"]

    def step(*args):
        state, *rest = [pltpu.with_memory_space_constraint(x, pltpu.HBM) for x in args]
        return pl.pallas_call(
            functools.partial(kernel, lon_count, lat_count),
            out_shape=jax.ShapeDtypeStruct(state.shape, F32),
            in_specs=[pl.BlockSpec(memory_space=pltpu.HBM)] * 8,
            out_specs=pl.BlockSpec(memory_space=pltpu.VMEM),
            scratch_shapes=[
                pltpu.VMEM((16, 80, 128), F32),
                pltpu.VMEM((64, 128), jnp.int32),
                pltpu.VMEM((3, 3, 16, 16), BF16),
                pltpu.VMEM((3, 3, 16, 16), BF16),
                pltpu.VMEM((3, 3, 8, 16), BF16),
                pltpu.SMEM((16,), F32),
                pltpu.SMEM((16,), F32),
                pltpu.SMEM((8,), F32),
                pltpu.VMEM((16, 8, 128), F32),
                pltpu.VMEM((16, 8, 128), F32),
                pltpu.VMEM((16, 1024), F32),
                pltpu.VMEM((8, 1024), F32),
                pltpu.VMEM((8, 1024), F32),
                pltpu.VMEM((8, 128), F32),
                pltpu.VMEM((8, 128), F32),
                pltpu.VMEM((8, 128), F32),
                pltpu.VMEM((8, 128), F32),
                pltpu.VMEM((16, 8, 128), F32),
                pltpu.VMEM((16, 128), F32),
                pltpu.VMEM((144, 128), F32),
                pltpu.VMEM((384, 384), BF16),
                pltpu.VMEM((384, 384), BF16),
                pltpu.VMEM((384, 384), BF16),
                pltpu.VMEM((384, 256), BF16),
                pltpu.VMEM((384, 256), BF16),
                pltpu.VMEM((2, 128, 128), F32),
                pltpu.VMEM((3, 128, 128), F32),
                pltpu.VMEM((1280, 128), BF16),
                pltpu.VMEM((1280, 128), BF16),
                pltpu.SemaphoreType.DMA((10,)),
                pltpu.SemaphoreType.DMA((11,)),
                pltpu.SemaphoreType.DMA((10,)),
                pltpu.SemaphoreType.REGULAR((8,)),
            ],
            compiler_params=pltpu.CompilerParams(
                collective_id=0, has_side_effects=True, vmem_limit_bytes=32 * 1024 * 1024
            ),
        )(state, *rest)

    return jax.shard_map(
        step,
        mesh=mesh,
        in_specs=(P(None, "lat", "lon"), P("lat", "lon"), P(), P(), P(), P(), P(), P()),
        out_specs=P(None, "lat", "lon"),
        check_vma=False,
    )
```
